256 devices in a mesh: cluster: 8 (over z), tm: 32 (over x, y, core).
Axes of the slice: x: 4, y: 4, z: 8, core: 2. Of those that a mesh axis runs over, the one named last changes fastest.
Arguments:
- obs: float32 [24, 2048, 128], P('cluster', 'tm'), parts along dimension 0, may hold values from -6 to 6
- present: int32 [24, 2048], P('cluster', 'tm'), parts along dimension 0, may hold values 0 or 1
- sensors: int32 [8], P('cluster'), parts along dimension 0, may hold values from 32 to 128
- log_prec: float32 [1024], P('cluster'), parts along dimension 0, may hold values from -1 to 1
- dynamics: float32 [1024, 128], P('cluster'), parts along dimension 0, may hold values from -1 to 1
- prior_var: float32 [1024], P('cluster'), parts along dimension 0, may hold values from 0 to 0.06, as said below
- obs_map: float32 [1024, 128], P('cluster'), parts along dimension 0, may hold values from -0.5 to 0.5
- init_state: float32 [24, 128], P('cluster'), parts along dimension 0, may hold values from -6 to 6
Outputs:
- smoothed: float32 [24, 2048, 128], P('cluster', 'tm'), parts along dimension 0
- new_log_prec: float32 [1024], P('cluster'), parts along dimension 0
- mean_loglik: float32 [8], P('cluster'), parts along dimension 0
The draws below stay inside these ranges and needn't reach their ends.
There are 8 independent parts, one for each index of `cluster`. The reference program is written for one: setup_inputs(seed, part) draws one part's arguments, and reference() takes and returns one part's arrays. A program takes and returns all parts, laid end to end along the dimension named above; each array names one. Nothing has to cross between parts.
Inputs may be any that keep to these rules, and one draw needn't show every extreme that they name: `prior_var`: positive variances.
All inputs are finite; a program needn't handle non-finite values. No bound on the sum of `present` on one device may be relied on, other than what follows from the above.
Results may differ from the reference program's by a relative error of at most 0.0003.
Values sent between devices are 32-bit elements; how exact they have to be, the bound alone decides.
No kernel may reach another device: no remote copies, remote signals or barrier semaphores. Data moves between devices by JAX's collectives and lax.ppermute only.
A program may use at most 128 MiB of HBM per device.

```python
import math
import jax
import jax.numpy as jnp
from jax import lax

S = 128
P_SIZE = 128
SEQS = 3
STEPS = 2048


def structure(key):
    folded = jax.random.fold_in(key, 31)
    subkeys = jax.random.split(folded, 4)
    share = 0.5
    slow_mask = jax.random.uniform(subkeys[0], (S,)) < share
    slow_rate = jnp.exp(jnp.log(0.3) / STEPS)
    memory_steps = jax.random.uniform(subkeys[1], (S,), minval=30.0, maxval=50.0)
    decay_rates = jnp.where(slow_mask, slow_rate, jnp.exp(-1.0 / memory_steps))
    same_group = (slow_mask[:, None] == slow_mask[None, :]).astype(jnp.float32)
    mixing_noise = jax.random.normal(subkeys[2], (S, S)) * (0.35 / math.sqrt(S))
    initial = (jnp.eye(S, dtype=jnp.float32) + mixing_noise * same_group) / 1.8

    def refine(repeat, matrix):
        cubic = jnp.dot(jnp.dot(matrix, matrix.T, precision=lax.Precision.HIGHEST), matrix, precision=lax.Precision.HIGHEST)
        return 1.5 * matrix - 0.5 * cubic
    rotation = lax.fori_loop(0, 40, refine, initial)
    transition = decay_rates[:, None] * rotation
    variances = jnp.where(slow_mask, 0.3 / STEPS, 0.05) * jax.random.uniform(subkeys[3], (S,), minval=0.9, maxval=1.1)
    return (transition.astype(jnp.float32), variances.astype(jnp.float32))


def draw_dynamics(key, part):
    return structure(key)[0]


def draw_prior_var(key, part):
    return structure(key)[1]


def set_ends(entries, key, smallest, high):
    dims = entries.shape
    place = [jax.random.randint(jax.random.fold_in(key, axis), (), 0, dims[axis]) for axis in range(len(dims))]
    entries = entries.at[tuple(place)].set(smallest)
    longest = dims.index(max(dims))
    place[longest] = (place[longest] + 1) % dims[longest]
    return entries.at[tuple(place)].set(high)


def steps_of(own_key, dims, shards, least, high):
    def one(position, shards_of):
        steps = jax.random.uniform(jax.random.fold_in(jax.random.fold_in(own_key, 6), position), (shards_of,), jnp.float32, least / len(shards), high / len(shards))
        return jnp.repeat(jnp.exp(steps), dims[position] // shards_of).reshape((-1,) + (1,) * (len(dims) - position - 1))

    level = one(*shards[0])
    for cut in shards[1:]:
        level = level * one(*cut)
    return level


def normal_values(rng, shape, spread, bound, cuts=(), held_as=jnp.bfloat16):
    entries = jax.random.normal(rng, shape, jnp.float32) * spread
    if len(cuts) > 0:
        entries = steps_of(rng, shape, cuts, -0.22, 0.18) * entries
    return jnp.clip(entries, min=-bound, max=bound).astype(held_as)


def setup_inputs(seed: int = 0, part: int = 0) -> dict:
    splits = jax.random.split(jax.random.key(seed), 9)
    own_keys = jax.random.split(jax.random.fold_in(splits[8], part), 9)
    obs = normal_values(own_keys[0], (SEQS, STEPS, P_SIZE), 1.0, 6.0, ((1, 32),), jnp.float32)
    present = set_ends((jax.random.randint(own_keys[1], (SEQS, STEPS), 0, 5) < 4).astype(jnp.int32), jax.random.fold_in(own_keys[1], 1), 0, 1)
    sensors = jax.random.randint(own_keys[2], (1,), P_SIZE // 4, P_SIZE + 1).astype(jnp.int32)
    log_prec = jnp.clip(jax.random.uniform(own_keys[3], (P_SIZE,), jnp.float32, -1.0, 1.0), -1.0, 1.0)
    dynamics = draw_dynamics(jax.random.fold_in(jax.random.fold_in(splits[8], part), 71), part)
    prior_var = draw_prior_var(jax.random.fold_in(jax.random.fold_in(splits[8], part), 71), part)
    obs_map = normal_values(own_keys[6], (P_SIZE, S), S ** -0.5, 0.5, (), jnp.float32)
    init_state = normal_values(own_keys[7], (SEQS, S), 1.0, 6.0, (), jnp.float32)
    return dict(obs=obs, present=present, sensors=sensors, log_prec=log_prec, dynamics=dynamics, prior_var=prior_var, obs_map=obs_map, init_state=init_state)


def reference(obs, present, sensors, log_prec, dynamics, prior_var, obs_map, init_state):
    highest = lax.Precision.HIGHEST
    channel_on = (jnp.arange(P_SIZE) < sensors[0]).astype(jnp.float32)
    sensor_precision = jnp.exp(log_prec)
    gain_matrix = prior_var[:, None] * (obs_map.T * (sensor_precision * channel_on)[None, :])
    outputs = []
    gradient = jnp.zeros((P_SIZE,), jnp.float32)
    loglik = jnp.zeros((), jnp.float32)
    for sequence in range(SEQS):
        def forward(carried, inputs):
            reading, flag = inputs
            predicted = jnp.dot(dynamics, carried, precision=highest)
            innovation = channel_on * (reading - jnp.dot(obs_map, predicted, precision=highest))
            updated = predicted + flag.astype(jnp.float32) * jnp.dot(gain_matrix, innovation, precision=highest)
            return updated, (updated, innovation)

        last_state, (filtered, innovations) = lax.scan(forward, init_state[sequence], (obs[sequence], present[sequence]))

        def backward(later, current):
            moved = later - jnp.dot(dynamics, current, precision=highest)
            smooth = current + jnp.dot(dynamics.T, moved, precision=highest)
            return smooth, smooth

        boundary = jnp.dot(dynamics, last_state, precision=highest)
        ignored, smooth_states = lax.scan(backward, boundary, filtered, reverse=True)
        outputs.append(smooth_states)
        observed = present[sequence].astype(jnp.float32)[:, None]
        weighted = sensor_precision * innovations * innovations
        gradient = gradient + 0.5 * jnp.sum(observed * channel_on * (1.0 - weighted), axis=0)
        loglik = loglik + 0.5 * jnp.sum(observed * channel_on * (log_prec - weighted))
    count_all = SEQS * STEPS
    smoothed = jnp.stack(outputs)
    new_log_prec = log_prec + gradient / count_all
    mean_loglik = (loglik / (count_all * P_SIZE)).reshape(1)
    return smoothed, new_log_prec, mean_loglik
```

```python
import jax
import jax.numpy as jnp
from jax import lax
from jax.experimental import pallas as pl
from jax.experimental.pallas import tpu as pltpu
from jax.sharding import Mesh
from jax.sharding import PartitionSpec as P

F32, BF16 = jnp.float32, jnp.bfloat16
TM = ("tm_0", "tm_1", "tm_2")
N = 128
SEQ, STEPS, SUB = 3, 64, 4
LEAVES = STEPS // SUB
ROWS = SEQ * LEAVES
AUG = N + 8
BLOCKS = 32
VMEM_LIMIT = 40 * 1024 * 1024


def dot(a, b):
    return lax.dot(a, b, preferred_element_type=F32)


def lanes(*parts):
    return jnp.concatenate(parts, axis=1)


def stacked(*parts):
    return jnp.concatenate(parts, axis=0)


def split2(a):
    hi = a.astype(BF16)
    return hi, (a - hi.astype(F32)).astype(BF16)


def split3(a):
    hi = a.astype(BF16)
    rest = a - hi.astype(F32)
    mid = rest.astype(BF16)
    return hi, mid, (rest - mid.astype(F32)).astype(BF16)


def pair(a):
    return lanes(*split2(a))


def whole(x):
    n = x.shape[1] // 2
    return x[:, :n].astype(F32) + x[:, n:].astype(F32)


def mul_pair(x, y):
    d = dot(x, stacked(y, y))
    n = y.shape[1] // 2
    return d[:, :n] + d[:, n:]


def mul_exact(a, b):
    a0, a1, a2 = split3(a)
    b0, b1, b2 = split3(b)
    n = b.shape[1]
    y = lanes(b0, b1)
    d = dot(lanes(a0, a1), stacked(y, y))
    return d[:, :n] + (d[:, n:] + dot(lanes(a0, a2), stacked(b2, b0)))


def apply_row(row, matrix):
    column = jnp.transpose(jnp.broadcast_to(row, (N, N)))
    return jnp.sum(column * matrix, axis=0, keepdims=True)


def step_major(ref, i):
    return stacked(*(ref[b, pl.ds(i, LEAVES, stride=SUB), :] for b in range(SEQ)))


def model(sensors_ref, lp_ref, dyn_ref, pv_ref, map_ref):
    on = (lax.broadcasted_iota(jnp.int32, (1, N), 1) < sensors_ref[0]).astype(F32)
    weight = jnp.exp(lp_ref[...]) * on
    dyn_t = jnp.transpose(dyn_ref[...])
    out_t = mul_exact(dyn_t, jnp.transpose(map_ref[...]))
    filt_t = dyn_t - mul_exact(out_t * weight, map_ref[...]) * pv_ref[...]
    return on, weight, dyn_t, out_t, filt_t


def drives(obs_ref, pres_ref, weight, pv, obs_map, mask_scr, u_scr):
    flags = pres_ref[...].astype(F32)
    flags = jnp.transpose(stacked(flags, jnp.zeros((8 - SEQ, STEPS), F32)))
    y = pair(obs_map)
    for b in range(SEQ):
        mask = jnp.broadcast_to(flags[:, b : b + 1], (STEPS, N))
        mask_scr[b] = mask
        u_scr[b] = mul_pair(pair(obs_ref[b] * weight), y) * pv * mask


def tree(pres_smem, dyn_t, filt_t, mask_scr, u_scr, table, nodes1, nodes2, nodes3, offs):
    two = mul_exact(stacked(dyn_t, filt_t), lanes(dyn_t, filt_t))
    twos = [two[i * N : (i + 1) * N, j * N : (j + 1) * N] for i in (0, 1) for j in (0, 1)]
    wide = lanes(*twos)
    for i in range(4):
        four = mul_exact(twos[i], wide)
        for j in range(4):
            table[4 * i + j] = pair(four[:, j * N : (j + 1) * N])
    y = pair(lanes(dyn_t, filt_t))
    z = step_major(u_scr, 0)
    for i in range(1, SUB):
        d = mul_pair(pair(z), y)
        z = jnp.where(step_major(mask_scr, i) > 0.5, d[:, N:], d[:, :N]) + step_major(u_scr, i)
    offs[0:ROWS, :] = z

    def leaf(k):
        b, j = k // LEAVES, k % LEAVES
        at = 0
        for i in range(SUB):
            at = at * 2 + pres_smem[b, SUB * j + i]
        return table[at]

    def join(left, left_off, right, right_off):
        off = pair(jnp.broadcast_to(left_off, (16, N)))
        got = mul_pair(stacked(left, off), right)
        return got[:N], got[N : N + 1] + right_off

    base, count = 0, ROWS
    roots = []
    get = leaf
    for store in (nodes1, nodes2, nodes3, None):
        for k in range(count // 2):
            matrix, off = join(
                get(2 * k),
                offs[base + 2 * k : base + 2 * k + 1, :],
                get(2 * k + 1),
                offs[base + 2 * k + 1 : base + 2 * k + 2, :],
            )
            if store is None:
                roots.append((matrix, off))
            else:
                store[k] = pair(matrix)
                offs[base + count + k : base + count + k + 1, :] = off
        base, count = base + count, count // 2
        if store is not None:
            get = lambda k, store=store: store[k]
    return roots, leaf


TREE_SCRATCH = [
    pltpu.VMEM((SEQ, STEPS, N), F32),
    pltpu.VMEM((SEQ, STEPS, N), F32),
    pltpu.VMEM((16, N, 2 * N), BF16),
    pltpu.VMEM((24, N, 2 * N), BF16),
    pltpu.VMEM((12, N, 2 * N), BF16),
    pltpu.VMEM((6, N, 2 * N), BF16),
    pltpu.VMEM((96, N), F32),
]


def k_block(
    pres_smem, sensors_ref, obs_ref, pres_ref, lp_ref, dyn_ref, pv_ref, map_ref, msg_ref,
    mask_scr, u_scr, table, nodes1, nodes2, nodes3, offs,
):
    on, weight, dyn_t, out_t, filt_t = model(sensors_ref, lp_ref, dyn_ref, pv_ref, map_ref)
    drives(obs_ref, pres_ref, weight, pv_ref[...], map_ref[...], mask_scr, u_scr)
    roots, leaf = tree(
        pres_smem, dyn_t, filt_t, mask_scr, u_scr, table, nodes1, nodes2, nodes3, offs
    )
    for b in range(SEQ):
        msg_ref[b, 0:N, :] = roots[b][0]
        msg_ref[b, N:AUG, :] = jnp.broadcast_to(roots[b][1], (8, N))


def k_tables(
    pres_smem, sensors_ref, obs_ref, pres_ref, lp_ref, dyn_ref, pv_ref, map_ref,
    pre_ref, preoff_ref, step_ref, u_ref, mask_ref, far_ref, near_ref, cross_ref, resid_ref,
    mask_scr, u_scr, table, nodes1, nodes2, nodes3, offs,
):
    on, weight, dyn_t, out_t, filt_t = model(sensors_ref, lp_ref, dyn_ref, pv_ref, map_ref)
    drives(obs_ref, pres_ref, weight, pv_ref[...], map_ref[...], mask_scr, u_scr)
    roots, leaf = tree(
        pres_smem, dyn_t, filt_t, mask_scr, u_scr, table, nodes1, nodes2, nodes3, offs
    )
    for i in range(SUB):
        u_ref[i] = step_major(u_scr, i)
        mask_ref[i] = step_major(mask_scr, i)
    step_ref[...] = pair(lanes(dyn_t, filt_t, out_t))
    starts = {1: ROWS + 24 + 12, 2: ROWS + 24, 4: ROWS, 8: 0}
    stores = {1: nodes3, 2: nodes2, 4: nodes1}
    preoff_ref[...] = jnp.zeros_like(preoff_ref)
    for b in range(SEQ):
        pre_ref[b * LEAVES] = jnp.zeros((N, N), F32)
        for parents in (1, 2, 4, 8):
            span = LEAVES // parents
            for k in range(parents):
                at = b * LEAVES + k * span
                left = b * 2 * parents + 2 * k
                off = offs[starts[parents] + left : starts[parents] + left + 1, :]
                got = leaf(left) if parents == 8 else stores[parents][left]
                if k == 0:
                    matrix = whole(got)
                else:
                    before = stacked(
                        pair(pre_ref[at]),
                        pair(jnp.broadcast_to(preoff_ref[at : at + 1, :], (16, N))),
                    )
                    both = mul_pair(before, got)
                    matrix, off = both[:N], both[N : N + 1] + off
                to = at + span // 2
                pre_ref[to] = matrix
                preoff_ref[to : to + 1, :] = off
    dyn = dyn_ref[...]
    eye = (
        lax.broadcasted_iota(jnp.int32, (N, N), 0) == lax.broadcasted_iota(jnp.int32, (N, N), 1)
    ).astype(F32)
    resid_ref[...] = pair(eye - mul_exact(dyn_t, dyn))
    d2 = mul_exact(dyn, dyn)
    d34 = mul_exact(d2, lanes(dyn, d2))
    d4 = d34[:, N:]
    for i, a in enumerate((dyn, d2, d34[:, :N], d4)):
        near_ref[i] = pair(a)
    far_ref[0] = eye
    far_ref[1] = d4
    for have in (1, 2, 4, 8):
        last = far_ref[have]
        for k in range(1, have + 1):
            got = mul_exact(last, far_ref[k])
            if have + k < LEAVES:
                far_ref[have + k] = got
    for i, k in enumerate((2, 4, 8)):
        near_ref[4 + i] = pair(far_ref[k])
    block = got
    cross_ref[0] = pair(eye)
    powers = [None, block]
    for k in range(2, 9):
        powers.append(mul_exact(powers[k // 2], powers[k - k // 2]))
    for k in range(1, 8):
        cross_ref[k] = pair(powers[k])
    w16 = mul_exact(powers[8], powers[8])
    cross_ref[8] = pair(powers[8])
    cross_ref[9] = pair(w16)
    cross_ref[10] = pair(mul_exact(w16, powers[8]))


def aug_pair(a):
    return pair(stacked(a, a[N:AUG]))


def compose(a, b):
    got = mul_pair(aug_pair(a), pair(b[:N]))
    return stacked(got[:N], got[N:AUG] + b[N:AUG])


def pick(flag, a, b):
    return jnp.where(flag, a, b)


def k_core(own_ref, other_ref, out_ref):
    first = lax.axis_index("tm_2") == 0
    for b in range(SEQ):
        own, other = own_ref[b], other_ref[b]
        out_ref[b] = compose(pick(first, own, other), pick(first, other, own))


def ordered(axis, refs, scr):
    me = lax.axis_index(axis)
    for d, ref in enumerate(refs):
        scr[lax.rem(me + 4 - d, 4)] = ref[...]


def k_total(own_ref, r1_ref, r2_ref, r3_ref, out_ref, scr):
    ordered("tm_1", (own_ref, r1_ref, r2_ref, r3_ref), scr)
    for b in range(SEQ):
        out_ref[b] = compose(compose(scr[0, b], scr[1, b]), compose(scr[2, b], scr[3, b]))


def k_entry(own_ref, r1_ref, r2_ref, r3_ref, mate_ref, out_ref, scr):
    ordered("tm_1", (own_ref, r1_ref, r2_ref, r3_ref), scr)
    me, second = lax.axis_index("tm_1"), lax.axis_index("tm_2") == 1
    eye = (
        lax.broadcasted_iota(jnp.int32, (AUG, N), 0) == lax.broadcasted_iota(jnp.int32, (AUG, N), 1)
    ).astype(F32)
    for b in range(SEQ):
        so_far = eye
        for k in range(3):
            so_far = pick(k < me, compose(so_far, scr[k, b]), so_far)
        out_ref[b] = pick(second, compose(so_far, mate_ref[b]), so_far)


def k_filter(
    sensors_ref, own_ref, r1_ref, r2_ref, r3_ref, entry_ref, init_ref, obs_ref, lp_ref,
    dyn_ref, pre_ref, preoff_ref, step_ref, u_ref, mask_ref, far_ref, near_ref, resid_ref,
    send_ref, local_ref, suffix_ref, final_ref, scr,
):
    ordered("tm_0", (own_ref, r1_ref, r2_ref, r3_ref), scr)
    group = lax.axis_index("tm_0")
    last = (group == 3) & (lax.axis_index("tm_1") == 3) & (lax.axis_index("tm_2") == 1)
    starts = []
    for b in range(SEQ):
        row = init_ref[b : b + 1, :]
        for k in range(3):
            row = pick(k < group, apply_row(row, scr[k, b, 0:N, :]) + scr[k, b, N : N + 1, :], row)
        row = apply_row(row, entry_ref[b, 0:N, :]) + entry_ref[b, N : N + 1, :]
        starts.append(row)
    rows = []
    for b in range(SEQ):
        column = jnp.transpose(jnp.broadcast_to(starts[b], (N, N)))
        rows.append(starts[b])
        for j in range(1, LEAVES):
            k = b * LEAVES + j
            rows.append(
                jnp.sum(column * pre_ref[k], axis=0, keepdims=True) + preoff_ref[k : k + 1, :]
            )
    state = stacked(*rows)
    on = (lax.broadcasted_iota(jnp.int32, (1, N), 1) < sensors_ref[0]).astype(F32)
    weight = jnp.exp(lp_ref[...]) * on
    step = step_ref[...]
    resid = resid_ref[...]
    square = jnp.zeros((ROWS, N), F32)
    seen = jnp.zeros((ROWS, N), F32)
    residuals = []
    for i in range(SUB):
        d = mul_pair(pair(state), step)
        mask = mask_ref[i]
        error = step_major(obs_ref, i) - d[:, 2 * N :]
        square = square + mask * (error * error)
        seen = seen + mask
        state = pick(mask > 0.5, d[:, N : 2 * N], d[:, :N]) + u_ref[i]
        residuals.append(mul_pair(pair(state), resid))
    square = jnp.sum(square, axis=0, keepdims=True) * weight
    seen = jnp.sum(seen, axis=0, keepdims=True)
    ends = stacked(*(state[(b + 1) * LEAVES - 1 : (b + 1) * LEAVES, :] for b in range(SEQ)))
    ends = stacked(ends, jnp.zeros((8 - SEQ, N), F32))
    final = mul_pair(pair(ends), pair(jnp.transpose(dyn_ref[...])))
    final_ref[...] = final
    y = near_ref[0]
    run = residuals[SUB - 1]
    local_ref[SUB - 1] = run
    for i in reversed(range(SUB - 1)):
        run = mul_pair(pair(run), y) + residuals[i]
        local_ref[i] = run
    place = lax.broadcasted_iota(jnp.int32, (ROWS, N), 0) % LEAVES
    for k, reach in zip((3, 4, 5, 6), (1, 2, 4, 8)):
        moved = mul_pair(pair(run), near_ref[k])
        moved = pltpu.roll(moved, ROWS - reach, 0)
        run = run + pick(place < LEAVES - reach, moved, 0.0)
    suffix_ref[...] = run
    offsets = stacked(*(run[b * LEAVES : b * LEAVES + 1, :] for b in range(SEQ)))
    offsets = stacked(offsets, jnp.zeros((8 - SEQ, N), F32))
    half = mul_pair(pair(final), near_ref[6])
    through = mul_pair(pair(half), near_ref[6])
    offsets = offsets + pick(last, through, 0.0)
    packed = stacked(offsets[:SEQ], square, seen, jnp.zeros((8 - SEQ - 2, N), F32))
    send_ref[...] = jnp.broadcast_to(packed[None], (BLOCKS, 8, N))


def k_smooth(
    sensors_ref, got_ref, local_ref, suffix_ref, final_ref, lp_ref, far_ref, near_ref, cross_ref,
    out_ref, prec_ref, lik_ref,
):
    me = (lax.axis_index("tm_0") * 4 + lax.axis_index("tm_1")) * 2 + lax.axis_index("tm_2")
    on = (lax.broadcasted_iota(jnp.int32, (1, N), 1) < sensors_ref[0]).astype(F32)
    acc = jnp.zeros((4 * 8, N), F32)
    for h in range(8):
        parts = []
        for g in range(4):
            at = me + 1 + 8 * g + h
            parts.append(pick(at < BLOCKS, got_ref[jnp.minimum(at, BLOCKS - 1)], 0.0))
        acc = acc + mul_pair(pair(stacked(*parts)), cross_ref[h])
    leaving = acc[0:8]
    for g in range(1, 4):
        leaving = leaving + mul_pair(pair(acc[8 * g : 8 * g + 8]), cross_ref[7 + g])
    leaving = pick(me == BLOCKS - 1, final_ref[...], leaving)
    rows = []
    for b in range(SEQ):
        column = jnp.transpose(jnp.broadcast_to(leaving[b : b + 1, :], (N, N)))
        for j in range(LEAVES - 1):
            k = b * LEAVES + j
            rows.append(
                jnp.sum(column * far_ref[LEAVES - 1 - j], axis=0, keepdims=True)
                + suffix_ref[k + 1 : k + 2, :]
            )
        rows.append(leaving[b : b + 1, :])
    x = pair(stacked(*rows))
    for i in range(SUB):
        got = mul_pair(x, near_ref[SUB - 1 - i]) + local_ref[i]
        for b in range(SEQ):
            out_ref[b, pl.ds(i, LEAVES, stride=SUB), :] = got[b * LEAVES : (b + 1) * LEAVES]
    sums = jnp.sum(got_ref[...], axis=0)
    square, seen = sums[SEQ : SEQ + 1], sums[SEQ + 1 : SEQ + 2]
    total = float(SEQ * STEPS * BLOCKS)
    lp = lp_ref[...]
    prec_ref[...] = lp + (0.5 / total) * on * (seen - square)
    lik = jnp.sum(on * (seen * lp - square), axis=1, keepdims=True) * (0.5 / (total * N))
    lik_ref[...] = jnp.broadcast_to(lik, (1, N))


VM = pl.BlockSpec(memory_space=pltpu.VMEM)
SM = pl.BlockSpec(memory_space=pltpu.SMEM)


def call(kernel, name, specs, shapes, scratch=(), flops=0, moved=0):
    return pl.pallas_call(
        kernel,
        out_shape=shapes,
        in_specs=specs,
        out_specs=jax.tree.map(lambda _: VM, shapes),
        scratch_shapes=list(scratch),
        compiler_params=pltpu.CompilerParams(vmem_limit_bytes=VMEM_LIMIT),
        cost_estimate=pl.CostEstimate(flops=flops, bytes_accessed=moved, transcendentals=0),
        name=name,
    )


def out(shape, dtype=F32):
    return jax.ShapeDtypeStruct(shape, dtype)


def shifted(a, axis, by):
    count = lax.axis_size(axis)
    return lax.ppermute(a, axis, [(i, (i + by) % count) for i in range(count)])


def local(obs, present, sensors, log_prec, dynamics, prior_var, obs_map, init_state):
    lp, pv = log_prec.reshape(1, N), prior_var.reshape(1, N)
    msg = out((SEQ, AUG, N))
    args = (present, sensors, obs, present, lp, dynamics, pv, obs_map)
    specs = [SM, SM] + [VM] * 6
    four = pltpu.VMEM((4, SEQ, AUG, N), F32)
    block = call(k_block, "k_block", specs, msg, TREE_SCRATCH, 10**9, 10**6)(*args)
    mate = shifted(block, "tm_2", 1)
    pre, preoff, step, u, mask, far, near, cross, resid = call(
        k_tables,
        "k_tables",
        specs,
        (
            out((ROWS, N, N)),
            out((ROWS, N)),
            out((N, 6 * N), BF16),
            out((SUB, ROWS, N)),
            out((SUB, ROWS, N)),
            out((LEAVES, N, N)),
            out((7, N, 2 * N), BF16),
            out((11, N, 2 * N), BF16),
            out((N, 2 * N), BF16),
        ),
        TREE_SCRATCH,
        6 * 10**9,
        10**7,
    )(*args)
    chip = call(k_core, "k_core", [VM] * 2, msg, (), 10**7, 10**6)(block, mate)
    ys = [shifted(chip, "tm_1", d) for d in (1, 2, 3)]
    column = call(k_total, "k_total", [VM] * 4, msg, [four], 10**7, 10**6)(chip, *ys)
    xs = [shifted(column, "tm_0", d) for d in (1, 2, 3)]
    entry = call(k_entry, "k_entry", [VM] * 5, msg, [four], 10**8, 10**6)(chip, *ys, mate)
    send, near_sums, suffix, final = call(
        k_filter,
        "k_filter",
        [SM] + [VM] * 17,
        (out((BLOCKS, 8, N)), out((SUB, ROWS, N)), out((ROWS, N)), out((8, N))),
        [four],
        10**7,
        10**6,
    )(
        sensors, column, *xs, entry, init_state, obs, lp, dynamics, pre, preoff, step, u, mask,
        far, near, resid,
    )
    got = lax.all_to_all(send, TM, 0, 0, tiled=True)
    smoothed, prec, lik = call(
        k_smooth,
        "k_smooth",
        [SM] + [VM] * 8,
        (out((SEQ, STEPS, N)), out((1, N)), out((1, N))),
        (),
        10**7,
        10**6,
    )(sensors, got, near_sums, suffix, final, lp, far, near, cross)
    return smoothed, prec.reshape(N), lik[0, :1]


def solution(mesh):
    split = Mesh(
        mesh.devices.reshape(mesh.shape["cluster"], 4, 4, 2), ("cluster", "tm_0", "tm_1", "tm_2")
    )
    return jax.shard_map(
        local,
        mesh=split,
        in_specs=(
            P("cluster", TM, None),
            P("cluster", TM),
            P("cluster"),
            P("cluster"),
            P("cluster", None),
            P("cluster"),
            P("cluster", None),
            P("cluster", None),
        ),
        out_specs=(P("cluster", TM, None), P("cluster"), P("cluster")),
        check_vma=False,
    )
```

```python
import jax
import jax.numpy as jnp
from jax import lax
from jax.experimental import pallas as pl
from jax.experimental.pallas import tpu as pltpu
from jax.sharding import Mesh
from jax.sharding import PartitionSpec as P

F32, BF16 = jnp.float32, jnp.bfloat16
TM = ("tm_0", "tm_1", "tm_2")
N = 128
SEQ, STEPS, SUB = 3, 64, 4
LEAVES = STEPS // SUB
ROWS = SEQ * LEAVES
HALF = N // 2
BLOCKS = 32
VMEM_LIMIT = 40 * 1024 * 1024


def dot(a, b):
    return lax.dot(a, b, preferred_element_type=F32)


def lanes(*parts):
    return jnp.concatenate(parts, axis=1)


def stacked(*parts):
    return jnp.concatenate(parts, axis=0)


def split2(a):
    hi = a.astype(BF16)
    return hi, (a - hi.astype(F32)).astype(BF16)


def split3(a):
    hi = a.astype(BF16)
    rest = a - hi.astype(F32)
    mid = rest.astype(BF16)
    return hi, mid, (rest - mid.astype(F32)).astype(BF16)


def pair(a):
    return lanes(*split2(a))


def whole(x):
    n = x.shape[1] // 2
    return x[:, :n].astype(F32) + x[:, n:].astype(F32)


def mul_pair(x, y):
    d = dot(x, stacked(y, y))
    n = y.shape[1] // 2
    return d[:, :n] + d[:, n:]


def mul_exact(a, b):
    a0, a1, a2 = split3(a)
    b0, b1, b2 = split3(b)
    n = b.shape[1]
    y = lanes(b0, b1)
    d = dot(lanes(a0, a1), stacked(y, y))
    return d[:, :n] + (d[:, n:] + dot(lanes(a0, a2), stacked(b2, b0)))


def apply_row(row, matrix):
    column = jnp.transpose(jnp.broadcast_to(row, (N, N)))
    return jnp.sum(column * matrix, axis=0, keepdims=True)


def step_major(ref, i):
    return stacked(*(ref[b, pl.ds(i, LEAVES, stride=SUB), :] for b in range(SEQ)))


def pick(flag, a, b):
    return jnp.where(flag, a, b)


def on_row(sensors_ref):
    return (lax.broadcasted_iota(jnp.int32, (1, N), 1) < sensors_ref[0]).astype(F32)


def identity(rows=N):
    shape = (rows, N)
    return (
        lax.broadcasted_iota(jnp.int32, shape, 0) == lax.broadcasted_iota(jnp.int32, shape, 1)
    ).astype(F32)


def leaf_number(flags, b, j):
    at = 0
    for i in range(SUB):
        at = at * 2 + flags[b, SUB * j + i]
    return at


def joined(left, left_off, right, right_off):
    off = pair(jnp.broadcast_to(left_off, (16, N)))
    got = mul_pair(stacked(left, off), right)
    return got[:N], got[N : N + 1] + right_off


LEVELS = ((0, 24), (24, 12), (36, 6))
OFFS = (0, 48, 72, 84)
PART = HALF + 8


def k_first(dyn_ref, dynt_ref, near_ref, d4_ref, resid_ref):
    dyn = dyn_ref[...]
    dyn_t = jnp.transpose(dyn)
    dynt_ref[...] = dyn_t
    resid_ref[...] = pair(identity() - mul_exact(dyn_t, dyn))
    d2 = mul_exact(dyn, dyn)
    d34 = mul_exact(d2, lanes(dyn, d2))
    d4_ref[...] = d34[:, N:]
    for i, a in enumerate((dyn, d2, d34[:, :N], d34[:, N:])):
        near_ref[i] = pair(a)


def k_block(
    flags, sensors_ref, obs_raw, pres_ref, lp_ref, dynt_ref, pv_ref, map_ref,
    root_ref, table, nodes, offs, step_ref, u_ref, mask_ref, obs_ref, rows_ref, mask_scr, u_scr,
):
    on = on_row(sensors_ref)
    weight = jnp.exp(lp_ref[...]) * on
    pv, obs_map = pv_ref[...], map_ref[...]
    dyn_t = dynt_ref[...]
    out_t = mul_exact(dyn_t, jnp.transpose(obs_map))
    filt_t = dyn_t - mul_exact(out_t * weight, obs_map) * pv
    rows_ref[...] = stacked(on, weight, lp_ref[...], jnp.zeros((5, N), F32))
    step_ref[...] = pair(lanes(dyn_t, filt_t, out_t))
    seen = pres_ref[...].astype(F32)
    seen = jnp.transpose(stacked(seen, jnp.zeros((8 - SEQ, STEPS), F32)))
    y = pair(obs_map)
    for b in range(SEQ):
        mask = jnp.broadcast_to(seen[:, b : b + 1], (STEPS, N))
        mask_scr[b] = mask
        u_scr[b] = mul_pair(pair(obs_raw[b] * weight), y) * pv * mask
    for i in range(SUB):
        u_ref[i] = step_major(u_scr, i)
        mask_ref[i] = step_major(mask_scr, i)
        obs_ref[i] = step_major(obs_raw, i)
    two = mul_exact(stacked(dyn_t, filt_t), lanes(dyn_t, filt_t))
    twos = [two[i * N : (i + 1) * N, j * N : (j + 1) * N] for i in (0, 1) for j in (0, 1)]
    wide = lanes(*twos)
    for i in range(4):
        four = mul_exact(twos[i], wide)
        for j in range(4):
            table[4 * i + j] = pair(four[:, j * N : (j + 1) * N])
    y = pair(lanes(dyn_t, filt_t))
    z = u_ref[0]
    for i in range(1, SUB):
        d = mul_pair(pair(z), y)
        z = pick(mask_ref[i] > 0.5, d[:, N:], d[:, :N]) + u_ref[i]
    offs[0:ROWS, :] = z

    def leaf(k):
        return table[leaf_number(flags, k // LEAVES, k % LEAVES)]

    get = leaf
    for level in range(4):
        count = ROWS >> (level + 1)
        for k in range(count):
            at = OFFS[level] + 2 * k
            matrix, off = joined(
                get(2 * k), offs[at : at + 1, :], get(2 * k + 1), offs[at + 1 : at + 2, :]
            )
            if level == 3:
                root_ref[k, 0:N, :] = matrix
                root_ref[k, N : N + 8, :] = jnp.broadcast_to(off, (8, N))
            else:
                nodes[LEVELS[level][0] + k] = pair(matrix)
                to = OFFS[level + 1] + k
                offs[to : to + 1, :] = off
        if level < 3:
            get = lambda k, level=level: nodes[LEVELS[level][0] + k]


def put_halves(refs, b, matrix, off):
    off = jnp.broadcast_to(off, (8, N))
    for c, ref in enumerate(refs):
        ref[b, 0:HALF, :] = matrix[c * HALF : (c + 1) * HALF]
        ref[b, HALF:PART, :] = off


def from_halves(low_ref, high_ref, b):
    return stacked(low_ref[b, 0:HALF, :], high_ref[b, 0:HALF, :]), low_ref[b, HALF : HALF + 1, :]


def in_order(mine_ref, mate_ref, b):
    first = lax.axis_index("tm_2") == 0
    mine, mate = mine_ref[b, 0:HALF, :], mate_ref[b, 0:HALF, :]
    matrix = stacked(pick(first, mine, mate), pick(first, mate, mine))
    return matrix, mine_ref[b, HALF : HALF + 1, :]


def then(p, q):
    return joined(pair(p[0]), p[1], pair(q[0]), q[1])


def then_half(p, q, ref, b):
    left = pick(lax.axis_index("tm_2") == 0, p[0][:HALF], p[0][HALF:])
    got = mul_pair(
        stacked(pair(left), pair(jnp.broadcast_to(p[1], (16, N)))), pair(q[0])
    )
    ref[b, 0:HALF, :] = got[:HALF]
    ref[b, HALF:PART, :] = got[HALF:PART] + q[1]


def k_core(own_ref, mate_ref, mine_ref, low_ref, high_ref):
    first = lax.axis_index("tm_2") == 0
    for b in range(SEQ):
        own, mate = own_ref[b], mate_ref[b]
        p, q = pick(first, own, mate), pick(first, mate, own)
        matrix, off = then((p[:N], p[N : N + 1]), (q[:N], q[N : N + 1]))
        put_halves((low_ref, high_ref), b, matrix, off)
        mine_ref[b, 0:HALF, :] = pick(first, matrix[:HALF], matrix[HALF:])
        mine_ref[b, HALF:PART, :] = jnp.broadcast_to(off, (8, N))


def k_total(low_ref, high_ref, r1, r2, r3, m1, m2, m3, out_ref, full_ref, maps, offs):
    me = lax.axis_index("tm_1")
    for b in range(SEQ):
        for d, (r, m) in enumerate(((r1, m1), (r2, m2), (r3, m3))):
            matrix, off = in_order(r, m, b)
            slot = lax.rem(me + 3 - d, 4)
            maps[slot, b] = matrix
            offs[slot, b] = jnp.broadcast_to(off, (8, N))
            full_ref[d, b, 0:N, :] = matrix
            full_ref[d, b, N : N + 8, :] = jnp.broadcast_to(off, (8, N))
        matrix, off = from_halves(low_ref, high_ref, b)
        maps[me, b] = matrix
        offs[me, b] = jnp.broadcast_to(off, (8, N))
    for b in range(SEQ):
        p = [(maps[k, b], offs[k, b, 0:1, :]) for k in range(4)]
        then_half(then(p[0], p[1]), then(p[2], p[3]), out_ref, b)


def k_prefix(chip_ref, flags, table, nodes, offs, pre_ref, preoff_ref):
    preoff_ref[...] = jnp.zeros_like(preoff_ref)
    for b in range(SEQ):
        pre_ref[b * LEAVES] = jnp.zeros((N, N), F32)
        for level in (3, 2, 1, 0):
            parents = 8 >> level
            span = LEAVES // parents
            for k in range(parents):
                at = b * LEAVES + k * span
                left = b * 2 * parents + 2 * k
                off = offs[OFFS[level] + left : OFFS[level] + left + 1, :]
                if level == 0:
                    got = table[leaf_number(flags, left // LEAVES, left % LEAVES)]
                else:
                    got = nodes[LEVELS[level - 1][0] + left]
                if k == 0:
                    matrix = whole(got)
                else:
                    matrix, off = joined(
                        pair(pre_ref[at]), preoff_ref[at : at + 1, :], got, off
                    )
                to = at + span // 2
                pre_ref[to] = matrix
                preoff_ref[to : to + 1, :] = off


def k_powers(after_ref, d4_ref, far_ref, reach_ref, cross_ref):
    eye = identity()
    far_ref[0] = eye
    far_ref[1] = d4_ref[...]
    for have in (1, 2, 4, 8):
        last = far_ref[have]
        for k in range(1, have + 1):
            got = mul_exact(last, far_ref[k])
            if have + k < LEAVES:
                far_ref[have + k] = got
    for i, k in enumerate((1, 2, 4, 8)):
        reach_ref[i] = pair(far_ref[k])
    cross_ref[0] = pair(eye)
    powers = [None, got]
    for k in range(2, 9):
        powers.append(mul_exact(powers[k // 2], powers[k - k // 2]))
    for k in range(1, 8):
        cross_ref[k] = pair(powers[k])
    w16 = mul_exact(powers[8], powers[8])
    cross_ref[8] = pair(powers[8])
    cross_ref[9] = pair(w16)
    cross_ref[10] = pair(mul_exact(w16, powers[8]))


def k_entry(after_ref, full_ref, mate_ref, entry_ref, entryoff_ref):
    me, second = lax.axis_index("tm_1"), lax.axis_index("tm_2") == 1
    entryoff_ref[...] = jnp.zeros_like(entryoff_ref)
    for b in range(SEQ):
        so_far = (identity(), jnp.zeros((1, N), F32))
        for source, flag in (
            (full_ref.at[2], me >= 3), (full_ref.at[1], me >= 2), (full_ref.at[0], me >= 1),
            (mate_ref, second),
        ):
            got = then(so_far, (source[b, 0:N, :], source[b, N : N + 1, :]))
            so_far = (pick(flag, got[0], so_far[0]), pick(flag, got[1], so_far[1]))
        entry_ref[b] = so_far[0]
        entryoff_ref[b : b + 1, :] = so_far[1]


def k_filter(
    r1, r2, r3, m1, m2, m3, entry_ref, entryoff_ref, init_ref, obs_ref,
    rows_ref, dynt_ref, pre_ref, preoff_ref, step_ref, u_ref, mask_ref, near_ref, reach_ref,
    resid_ref, send_ref, local_ref, suffix_ref, final_ref,
):
    group = lax.axis_index("tm_0")
    last = (group == 3) & (lax.axis_index("tm_1") == 3) & (lax.axis_index("tm_2") == 1)
    starts = []
    for b in range(SEQ):
        row = init_ref[b : b + 1, :]
        for d, r, m in ((3, r3, m3), (2, r2, m2), (1, r1, m1)):
            matrix, off = in_order(r, m, b)
            row = pick(group >= d, apply_row(row, matrix) + off, row)
        starts.append(apply_row(row, entry_ref[b]) + entryoff_ref[b : b + 1, :])
    rows = []
    for b in range(SEQ):
        column = jnp.transpose(jnp.broadcast_to(starts[b], (N, N)))
        rows.append(starts[b])
        for j in range(1, LEAVES):
            k = b * LEAVES + j
            rows.append(
                jnp.sum(column * pre_ref[k], axis=0, keepdims=True) + preoff_ref[k : k + 1, :]
            )
    state = stacked(*rows)
    weight = rows_ref[1:2, :]
    step = step_ref[...]
    resid = resid_ref[...]
    square = jnp.zeros((ROWS, N), F32)
    seen = jnp.zeros((ROWS, N), F32)
    residuals = []
    for i in range(SUB):
        d = mul_pair(pair(state), step)
        mask = mask_ref[i]
        error = obs_ref[i] - d[:, 2 * N :]
        square = square + mask * (error * error)
        seen = seen + mask
        state = pick(mask > 0.5, d[:, N : 2 * N], d[:, :N]) + u_ref[i]
        residuals.append(mul_pair(pair(state), resid))
    square = jnp.sum(square, axis=0, keepdims=True) * weight
    seen = jnp.sum(seen, axis=0, keepdims=True)
    ends = stacked(*(state[(b + 1) * LEAVES - 1 : (b + 1) * LEAVES, :] for b in range(SEQ)))
    ends = stacked(ends, jnp.zeros((8 - SEQ, N), F32))
    final = mul_pair(pair(ends), pair(dynt_ref[...]))
    final_ref[...] = final
    y = near_ref[0]
    run = residuals[SUB - 1]
    local_ref[SUB - 1] = run
    for i in reversed(range(SUB - 1)):
        run = mul_pair(pair(run), y) + residuals[i]
        local_ref[i] = run
    place = lax.broadcasted_iota(jnp.int32, (ROWS, N), 0) % LEAVES
    for k, reach in enumerate((1, 2, 4, 8)):
        moved = mul_pair(pair(run), reach_ref[k])
        moved = pltpu.roll(moved, ROWS - reach, 0)
        run = run + pick(place < LEAVES - reach, moved, 0.0)
    suffix_ref[...] = run
    offsets = stacked(*(run[b * LEAVES : b * LEAVES + 1, :] for b in range(SEQ)))
    offsets = stacked(offsets, jnp.zeros((8 - SEQ, N), F32))
    half = mul_pair(pair(final), reach_ref[3])
    through = mul_pair(pair(half), reach_ref[3])
    offsets = offsets + pick(last, through, 0.0)
    packed = stacked(offsets[:SEQ], square, seen, jnp.zeros((8 - SEQ - 2, N), F32))
    send_ref[...] = jnp.broadcast_to(packed[None], (BLOCKS, 8, N))


def k_smooth(
    got_ref, local_ref, suffix_ref, final_ref, rows_ref, far_ref, near_ref, cross_ref,
    out_ref, prec_ref, lik_ref,
):
    me = (lax.axis_index("tm_0") * 4 + lax.axis_index("tm_1")) * 2 + lax.axis_index("tm_2")
    on, lp = rows_ref[0:1, :], rows_ref[2:3, :]
    acc = jnp.zeros((4 * 8, N), F32)
    for h in range(8):
        parts = []
        for g in range(4):
            at = me + 1 + 8 * g + h
            parts.append(pick(at < BLOCKS, got_ref[jnp.minimum(at, BLOCKS - 1)], 0.0))
        acc = acc + mul_pair(pair(stacked(*parts)), cross_ref[h])
    leaving = acc[0:8]
    for g in range(1, 4):
        leaving = leaving + mul_pair(pair(acc[8 * g : 8 * g + 8]), cross_ref[7 + g])
    leaving = pick(me == BLOCKS - 1, final_ref[...], leaving)
    rows = []
    for b in range(SEQ):
        column = jnp.transpose(jnp.broadcast_to(leaving[b : b + 1, :], (N, N)))
        for j in range(LEAVES - 1):
            k = b * LEAVES + j
            rows.append(
                jnp.sum(column * far_ref[LEAVES - 1 - j], axis=0, keepdims=True)
                + suffix_ref[k + 1 : k + 2, :]
            )
        rows.append(leaving[b : b + 1, :])
    x = pair(stacked(*rows))
    for i in range(SUB):
        got = mul_pair(x, near_ref[SUB - 1 - i]) + local_ref[i]
        for b in range(SEQ):
            out_ref[b, pl.ds(i, LEAVES, stride=SUB), :] = got[b * LEAVES : (b + 1) * LEAVES]
    sums = jnp.sum(got_ref[...], axis=0)
    square, seen = sums[SEQ : SEQ + 1], sums[SEQ + 1 : SEQ + 2]
    total = float(SEQ * STEPS * BLOCKS)
    prec_ref[...] = lp + (0.5 / total) * on * (seen - square)
    lik = jnp.sum(on * (seen * lp - square), axis=1, keepdims=True) * (0.5 / (total * N))
    lik_ref[...] = jnp.broadcast_to(lik, (1, N))


VM = pl.BlockSpec(memory_space=pltpu.VMEM)
SM = pl.BlockSpec(memory_space=pltpu.SMEM)


def call(kernel, name, specs, shapes, scratch=(), flops=0, moved=0):
    return pl.pallas_call(
        kernel,
        out_shape=shapes,
        in_specs=specs,
        out_specs=jax.tree.map(lambda _: VM, shapes),
        scratch_shapes=list(scratch),
        compiler_params=pltpu.CompilerParams(vmem_limit_bytes=VMEM_LIMIT),
        cost_estimate=pl.CostEstimate(flops=flops, bytes_accessed=moved, transcendentals=0),
        name=name,
    )


def out(shape, dtype=F32):
    return jax.ShapeDtypeStruct(shape, dtype)


def shifted(a, axis, by):
    count = lax.axis_size(axis)
    return lax.ppermute(a, axis, [(i, (i + by) % count) for i in range(count)])


def exchanged(mine, axis, work):
    got = [shifted(mine, axis, d) for d in (1, 2, 3)]
    done = work(mine)
    tied, done = lax.optimization_barrier((got, done))
    return got, [shifted(a, "tm_2", 1) for a in tied], done


def local(obs, present, sensors, log_prec, dynamics, prior_var, obs_map, init_state):
    lp, pv = log_prec.reshape(1, N), prior_var.reshape(1, N)
    part = out((SEQ, PART, N))
    square = out((N, N))
    dyn_t, near, d4, resid = call(
        k_first,
        "k_first",
        [VM],
        (square, out((4, N, 2 * N), BF16), square, out((N, 2 * N), BF16)),
        (),
        4 * 10**9,
        10**7,
    )(dynamics)
    root, table, nodes, offs, step, u, mask, obs_s, rows = call(
        k_block,
        "k_block",
        [SM] * 2 + [VM] * 6,
        (
            out((SEQ, N + 8, N)),
            out((16, N, 2 * N), BF16),
            out((42, N, 2 * N), BF16),
            out((96, N)),
            out((N, 6 * N), BF16),
            out((SUB, ROWS, N)),
            out((SUB, ROWS, N)),
            out((SUB, ROWS, N)),
            out((8, N)),
        ),
        [pltpu.VMEM((SEQ, STEPS, N), F32), pltpu.VMEM((SEQ, STEPS, N), F32)],
        10**9,
        10**6,
    )(present, sensors, obs, present, lp, dyn_t, pv, obs_map)
    mate = shifted(root, "tm_2", 1)
    chip, low, high = call(k_core, "k_core", [VM] * 2, (part, part, part), (), 10**7, 10**6)(
        root, mate
    )
    prefix = call(
        k_prefix,
        "k_prefix",
        [VM, SM] + [VM] * 3,
        (out((ROWS, N, N)), out((ROWS, N))),
        (),
        3 * 10**9,
        10**7,
    )
    got, mates, (pre, preoff) = exchanged(
        chip, "tm_1", lambda a: prefix(a, present, table, nodes, offs)
    )
    group, full = call(
        k_total,
        "k_total",
        [VM] * 8,
        (part, out((3, SEQ, N + 8, N))),
        [pltpu.VMEM((4, SEQ, N, N), F32), pltpu.VMEM((4, SEQ, 8, N), F32)],
        10**8,
        10**6,
    )(low, high, *got, *mates)
    powers = call(
        k_powers,
        "k_powers",
        [VM] * 2,
        (out((LEAVES, N, N)), out((4, N, 2 * N), BF16), out((11, N, 2 * N), BF16)),
        (),
        3 * 10**9,
        10**7,
    )
    entries = call(
        k_entry, "k_entry", [VM] * 3, (out((SEQ, N, N)), out((8, N))), (), 10**9, 10**7
    )
    got, mates, ((far, reach, cross), (entry, entryoff)) = exchanged(
        group, "tm_0", lambda a: (powers(a, d4), entries(a, full, mate))
    )
    send, near_sums, suffix, final = call(
        k_filter,
        "k_filter",
        [VM] * 20,
        (out((BLOCKS, 8, N)), out((SUB, ROWS, N)), out((ROWS, N)), out((8, N))),
        (),
        10**7,
        10**6,
    )(
        *got, *mates, entry, entryoff, init_state, obs_s, rows, dyn_t, pre, preoff, step, u,
        mask, near, reach, resid,
    )
    got = lax.all_to_all(send, TM, 0, 0, tiled=True)
    smoothed, prec, lik = call(
        k_smooth,
        "k_smooth",
        [VM] * 8,
        (out((SEQ, STEPS, N)), out((1, N)), out((1, N))),
        (),
        10**7,
        10**6,
    )(got, near_sums, suffix, final, rows, far, near, cross)
    return smoothed, prec.reshape(N), lik[0, :1]


def solution(mesh):
    split = Mesh(
        mesh.devices.reshape(mesh.shape["cluster"], 4, 4, 2), ("cluster", "tm_0", "tm_1", "tm_2")
    )
    return jax.shard_map(
        local,
        mesh=split,
        in_specs=(
            P("cluster", TM, None),
            P("cluster", TM),
            P("cluster"),
            P("cluster"),
            P("cluster", None),
            P("cluster"),
            P("cluster", None),
            P("cluster", None),
        ),
        out_specs=(P("cluster", TM, None), P("cluster"), P("cluster")),
        check_vma=False,
    )
```

```python
import jax
import jax.numpy as jnp
from jax import lax
from jax.experimental import pallas as pl
from jax.experimental.pallas import tpu as pltpu
from jax.sharding import Mesh
from jax.sharding import PartitionSpec as P

F32, BF16 = jnp.float32, jnp.bfloat16
TM = ("tm_0", "tm_1", "tm_2")
N = 128
SEQ, STEPS, SUB = 3, 64, 4
LEAVES = STEPS // SUB
ROWS = SEQ * LEAVES
HALF = N // 2
BLOCKS = 32
VMEM_LIMIT = 40 * 1024 * 1024


def dot(a, b):
    return lax.dot(a, b, preferred_element_type=F32)


def lanes(*parts):
    return jnp.concatenate(parts, axis=1)


def stacked(*parts):
    return jnp.concatenate(parts, axis=0)


def split2(a):
    hi = a.astype(BF16)
    return hi, (a - hi.astype(F32)).astype(BF16)


def split3(a):
    hi = a.astype(BF16)
    rest = a - hi.astype(F32)
    mid = rest.astype(BF16)
    return hi, mid, (rest - mid.astype(F32)).astype(BF16)


def pair(a):
    return lanes(*split2(a))


def whole(x):
    n = x.shape[1] // 2
    return x[:, :n].astype(F32) + x[:, n:].astype(F32)


def mul_pair(x, y):
    d = dot(x, stacked(y, y))
    n = y.shape[1] // 2
    return d[:, :n] + d[:, n:]


def mul_exact(a, b):
    a0, a1, a2 = split3(a)
    b0, b1, b2 = split3(b)
    n = b.shape[1]
    y = lanes(b0, b1)
    d = dot(lanes(a0, a1), stacked(y, y))
    return d[:, :n] + (d[:, n:] + dot(lanes(a0, a2), stacked(b2, b0)))


def apply_row(row, matrix):
    column = jnp.transpose(jnp.broadcast_to(row, (N, N)))
    return jnp.sum(column * matrix, axis=0, keepdims=True)


def step_major(ref, i):
    return stacked(*(ref[b, pl.ds(i, LEAVES, stride=SUB), :] for b in range(SEQ)))


def pick(flag, a, b):
    return jnp.where(flag, a, b)


def on_row(sensors_ref):
    return (lax.broadcasted_iota(jnp.int32, (1, N), 1) < sensors_ref[0]).astype(F32)


def identity(rows=N):
    shape = (rows, N)
    return (
        lax.broadcasted_iota(jnp.int32, shape, 0) == lax.broadcasted_iota(jnp.int32, shape, 1)
    ).astype(F32)


def leaf_number(flags, b, j):
    at = 0
    for i in range(SUB):
        at = at * 2 + flags[b, SUB * j + i]
    return at


def joined(left, left_off, right, right_off):
    off = pair(jnp.broadcast_to(left_off, (16, N)))
    got = mul_pair(stacked(left, off), right)
    return got[:N], got[N : N + 1] + right_off


REACH = (1, 2, 3, 4, 8, 12)
LEVELS = ((0, 24), (24, 12), (36, 6))
OFFS = (0, 48, 72, 84)
PART = SEQ * HALF + 8


def k_first(eye_ref):
    eye_ref[...] = identity()


def k_block(
    flags, sensors_ref, eye_ref, obs_raw, pres_ref, lp_ref, dyn_ref, pv_ref, map_ref,
    root_ref, dynt_ref, table, nodes, offs, step_ref, u_ref, mask_ref, obs_ref, rows_ref, mask_scr, u_scr,
):
    on = on_row(sensors_ref)
    weight = jnp.exp(lp_ref[...]) * on
    pv, obs_map = pv_ref[...], map_ref[...]
    dyn_t = jnp.transpose(dyn_ref[...])
    dynt_ref[...] = dyn_t
    y = pair(obs_map)
    out_t = mul_pair(pair(dyn_t), pair(jnp.transpose(obs_map)))
    filt_t = dyn_t - mul_pair(pair(out_t * weight), y) * pv
    rows_ref[...] = stacked(on, weight, lp_ref[...], jnp.zeros((5, N), F32))
    step_ref[...] = pair(lanes(dyn_t, filt_t, out_t))
    seen = pres_ref[...].astype(F32)
    seen = jnp.transpose(stacked(seen, jnp.zeros((8 - SEQ, STEPS), F32)))
    for b in range(SEQ):
        mask = jnp.broadcast_to(seen[:, b : b + 1], (STEPS, N))
        mask_scr[b] = mask
        u_scr[b] = mul_pair(pair(obs_raw[b] * weight), y) * pv * mask
    for i in range(SUB):
        u_ref[i] = step_major(u_scr, i)
        mask_ref[i] = step_major(mask_scr, i)
        obs_ref[i] = step_major(obs_raw, i)
    two = mul_exact(stacked(dyn_t, filt_t), lanes(dyn_t, filt_t))
    twos = [two[i * N : (i + 1) * N, j * N : (j + 1) * N] for i in (0, 1) for j in (0, 1)]
    wide = lanes(*twos)
    for i in range(4):
        four = mul_exact(twos[i], wide)
        for j in range(4):
            table[4 * i + j] = pair(four[:, j * N : (j + 1) * N])
    y = pair(lanes(dyn_t, filt_t))
    z = u_ref[0]
    for i in range(1, SUB):
        d = mul_pair(pair(z), y)
        z = pick(mask_ref[i] > 0.5, d[:, N:], d[:, :N]) + u_ref[i]
    offs[0:ROWS, :] = z

    def leaf(k):
        return table[leaf_number(flags, k // LEAVES, k % LEAVES)]

    get = leaf
    for level in range(4):
        count = ROWS >> (level + 1)
        for k in range(count):
            at = OFFS[level] + 2 * k
            matrix, off = joined(
                get(2 * k), offs[at : at + 1, :], get(2 * k + 1), offs[at + 1 : at + 2, :]
            )
            if level == 3:
                root_ref[k, 0:N, :] = matrix
                root_ref[k, N : N + 8, :] = jnp.broadcast_to(off, (8, N))
            else:
                nodes[LEVELS[level][0] + k] = pair(matrix)
                to = OFFS[level + 1] + k
                offs[to : to + 1, :] = off
        if level < 3:
            get = lambda k, level=level: nodes[LEVELS[level][0] + k]


def put_offsets(ref, offs):
    ref[SEQ * HALF : PART, :] = stacked(*offs, jnp.zeros((8 - SEQ, N), F32))


def half_of(ref, b):
    return ref[b * HALF : (b + 1) * HALF, :]


def offset_of(ref, b):
    return ref[SEQ * HALF + b : SEQ * HALF + b + 1, :]


def from_halves(low_ref, high_ref, b):
    return stacked(half_of(low_ref, b), half_of(high_ref, b)), offset_of(low_ref, b)


def in_order(mine_ref, mate_ref, b):
    first = lax.axis_index("tm_2") == 0
    mine, mate = half_of(mine_ref, b), half_of(mate_ref, b)
    matrix = stacked(pick(first, mine, mate), pick(first, mate, mine))
    return matrix, offset_of(mine_ref, b)


def then(p, q):
    return joined(pair(p[0]), p[1], pair(q[0]), q[1])


def then_half(p, q, ref, b):
    left = pick(lax.axis_index("tm_2") == 0, p[0][:HALF], p[0][HALF:])
    got = mul_pair(stacked(pair(left), pair(jnp.broadcast_to(p[1], (16, N)))), pair(q[0]))
    ref[b * HALF : (b + 1) * HALF, :] = got[:HALF]
    return got[HALF : HALF + 1] + q[1]


def k_core(own_ref, mate_ref, mine_ref, low_ref, high_ref):
    first = lax.axis_index("tm_2") == 0
    offs = []
    for b in range(SEQ):
        own, mate = own_ref[b], mate_ref[b]
        p, q = pick(first, own, mate), pick(first, mate, own)
        matrix, off = then((p[:N], p[N : N + 1]), (q[:N], q[N : N + 1]))
        low, high = matrix[:HALF], matrix[HALF:]
        for ref, half in ((low_ref, low), (high_ref, high), (mine_ref, pick(first, low, high))):
            ref[b * HALF : (b + 1) * HALF, :] = half
        offs.append(off)
    for ref in (low_ref, high_ref, mine_ref):
        put_offsets(ref, offs)


def k_total(low_ref, high_ref, r1, r2, r3, m1, m2, m3, out_ref, full_ref, maps, offs):
    me = lax.axis_index("tm_1")
    for b in range(SEQ):
        for d, (r, m) in enumerate(((r1, m1), (r2, m2), (r3, m3))):
            matrix, off = in_order(r, m, b)
            slot = lax.rem(me + 3 - d, 4)
            maps[slot, b] = matrix
            offs[slot, b] = jnp.broadcast_to(off, (8, N))
            full_ref[d, b, 0:N, :] = matrix
            full_ref[d, b, N : N + 8, :] = jnp.broadcast_to(off, (8, N))
        matrix, off = from_halves(low_ref, high_ref, b)
        maps[me, b] = matrix
        offs[me, b] = jnp.broadcast_to(off, (8, N))
    ends = []
    for b in range(SEQ):
        p = [(maps[k, b], offs[k, b, 0:1, :]) for k in range(4)]
        ends.append(then_half(then(p[0], p[1]), then(p[2], p[3]), out_ref, b))
    put_offsets(out_ref, ends)


def k_prefix(chip_ref, flags, table, nodes, offs, pre_ref, preoff_ref):
    preoff_ref[...] = jnp.zeros_like(preoff_ref)
    for b in range(SEQ):
        pre_ref[b * LEAVES] = jnp.zeros((N, N), F32)
        for level in (3, 2, 1, 0):
            parents = 8 >> level
            span = LEAVES // parents
            for k in range(parents):
                at = b * LEAVES + k * span
                left = b * 2 * parents + 2 * k
                off = offs[OFFS[level] + left : OFFS[level] + left + 1, :]
                if level == 0:
                    got = table[leaf_number(flags, left // LEAVES, left % LEAVES)]
                else:
                    got = nodes[LEVELS[level - 1][0] + left]
                if k == 0:
                    matrix = whole(got)
                else:
                    matrix, off = joined(
                        pair(pre_ref[at]), preoff_ref[at : at + 1, :], got, off
                    )
                to = at + span // 2
                pre_ref[to] = matrix
                preoff_ref[to : to + 1, :] = off


def k_powers(
    after_ref, eye_ref, dyn_ref, dynt_ref, near_ref, far_ref, reach_ref, cross_ref, resid_ref
):
    eye, dyn = eye_ref[...], dyn_ref[...]
    d2 = mul_exact(dyn, dyn)
    d34 = mul_exact(d2, lanes(dyn, d2))
    d3, d4 = d34[:, :N], d34[:, N:]
    for i, a in enumerate((dyn, d2, d3, d4)):
        near_ref[i] = pair(a)
    resid = eye - mul_exact(dynt_ref[...], dyn)
    resid_ref[0] = pair(resid)
    more = mul_exact(resid, lanes(dyn, d2, d3))
    for i in range(3):
        resid_ref[i + 1] = pair(more[:, i * N : (i + 1) * N])
    far_ref[0] = eye
    far_ref[1] = d4
    for have in (1, 2, 4, 8):
        last = far_ref[have]
        for k in range(1, have + 1):
            got = mul_exact(last, far_ref[k])
            if have + k < LEAVES:
                far_ref[have + k] = got
    for i, k in enumerate(REACH):
        reach_ref[i] = pair(far_ref[k])
    cross_ref[0] = pair(eye)
    powers = [None, got]
    for k in range(2, 9):
        powers.append(mul_exact(powers[k // 2], powers[k - k // 2]))
    for k in range(1, 8):
        cross_ref[k] = pair(powers[k])
    w16 = mul_exact(powers[8], powers[8])
    cross_ref[8] = pair(powers[8])
    cross_ref[9] = pair(w16)
    cross_ref[10] = pair(mul_exact(w16, powers[8]))


def k_entry(after_ref, full_ref, mate_ref, entry_ref, entryoff_ref):
    me, second = lax.axis_index("tm_1"), lax.axis_index("tm_2") == 1
    entryoff_ref[...] = jnp.zeros_like(entryoff_ref)
    for b in range(SEQ):
        so_far = (identity(), jnp.zeros((1, N), F32))
        for source, flag in (
            (full_ref.at[2], me >= 3), (full_ref.at[1], me >= 2), (full_ref.at[0], me >= 1),
            (mate_ref, second),
        ):
            got = then(so_far, (source[b, 0:N, :], source[b, N : N + 1, :]))
            so_far = (pick(flag, got[0], so_far[0]), pick(flag, got[1], so_far[1]))
        entry_ref[b] = so_far[0]
        entryoff_ref[b : b + 1, :] = so_far[1]


def k_filter(
    r1, r2, r3, m1, m2, m3, entry_ref, entryoff_ref, init_ref, obs_ref,
    rows_ref, dynt_ref, pre_ref, preoff_ref, step_ref, u_ref, mask_ref, reach_ref,
    resid_ref, cross_ref, send_ref, local_ref, suffix_ref, final_ref,
):
    group = lax.axis_index("tm_0")
    last = (group == 3) & (lax.axis_index("tm_1") == 3) & (lax.axis_index("tm_2") == 1)
    starts = []
    for b in range(SEQ):
        row = init_ref[b : b + 1, :]
        for d, r, m in ((3, r3, m3), (2, r2, m2), (1, r1, m1)):
            matrix, off = in_order(r, m, b)
            row = pick(group >= d, apply_row(row, matrix) + off, row)
        starts.append(apply_row(row, entry_ref[b]) + entryoff_ref[b : b + 1, :])
    rows = []
    for b in range(SEQ):
        column = jnp.transpose(jnp.broadcast_to(starts[b], (N, N)))
        rows.append(starts[b])
        for j in range(1, LEAVES):
            k = b * LEAVES + j
            rows.append(
                jnp.sum(column * pre_ref[k], axis=0, keepdims=True) + preoff_ref[k : k + 1, :]
            )
    state = stacked(*rows)
    weight = rows_ref[1:2, :]
    step = step_ref[...]
    square = jnp.zeros((ROWS, N), F32)
    seen = jnp.zeros((ROWS, N), F32)
    sums = [None] * SUB
    for i in range(SUB):
        d = mul_pair(pair(state), step)
        mask = mask_ref[i]
        error = obs_ref[i] - d[:, 2 * N :]
        square = square + mask * (error * error)
        seen = seen + mask
        state = pick(mask > 0.5, d[:, N : 2 * N], d[:, :N]) + u_ref[i]
        x = pair(state)
        for k in range(i + 1):
            add = mul_pair(x, resid_ref[i - k])
            sums[k] = add if k == i else sums[k] + add
    square = jnp.sum(square, axis=0, keepdims=True) * weight
    seen = jnp.sum(seen, axis=0, keepdims=True)
    ends = stacked(*(state[(b + 1) * LEAVES - 1 : (b + 1) * LEAVES, :] for b in range(SEQ)))
    ends = stacked(ends, jnp.zeros((8 - SEQ, N), F32))
    final = mul_pair(pair(ends), pair(dynt_ref[...]))
    final_ref[...] = final
    place = lax.broadcasted_iota(jnp.int32, (ROWS, N), 0) % LEAVES
    run = sums[0]
    for first in (0, 3):
        total = run
        for k in range(first, first + 3):
            moved = pltpu.roll(mul_pair(pair(run), reach_ref[k]), ROWS - REACH[k], 0)
            total = total + pick(place < LEAVES - REACH[k], moved, 0.0)
        run = total
    for i in range(SUB):
        local_ref[i] = sums[i]
    suffix_ref[...] = run
    offsets = stacked(*(run[b * LEAVES : b * LEAVES + 1, :] for b in range(SEQ)))
    offsets = stacked(offsets, jnp.zeros((8 - SEQ, N), F32))
    through = mul_pair(pair(final), cross_ref[1])
    offsets = offsets + pick(last, through, 0.0)
    packed = stacked(offsets[:SEQ], square, seen, jnp.zeros((8 - SEQ - 2, N), F32))
    send_ref[...] = jnp.broadcast_to(packed[None], (BLOCKS, 8, N))


def k_smooth(
    got_ref, local_ref, suffix_ref, final_ref, rows_ref, far_ref, near_ref, cross_ref,
    out_ref, prec_ref, lik_ref,
):
    me = (lax.axis_index("tm_0") * 4 + lax.axis_index("tm_1")) * 2 + lax.axis_index("tm_2")
    on, lp = rows_ref[0:1, :], rows_ref[2:3, :]
    acc = jnp.zeros((4 * 8, N), F32)
    for h in range(8):
        parts = []
        for g in range(4):
            at = me + 1 + 8 * g + h
            parts.append(pick(at < BLOCKS, got_ref[jnp.minimum(at, BLOCKS - 1)], 0.0))
        acc = acc + mul_pair(pair(stacked(*parts)), cross_ref[h])
    leaving = acc[0:8]
    for g in range(1, 4):
        leaving = leaving + mul_pair(pair(acc[8 * g : 8 * g + 8]), cross_ref[7 + g])
    leaving = pick(me == BLOCKS - 1, final_ref[...], leaving)
    rows = []
    for b in range(SEQ):
        column = jnp.transpose(jnp.broadcast_to(leaving[b : b + 1, :], (N, N)))
        for j in range(LEAVES - 1):
            k = b * LEAVES + j
            rows.append(
                jnp.sum(column * far_ref[LEAVES - 1 - j], axis=0, keepdims=True)
                + suffix_ref[k + 1 : k + 2, :]
            )
        rows.append(leaving[b : b + 1, :])
    x = pair(stacked(*rows))
    for i in range(SUB):
        got = mul_pair(x, near_ref[SUB - 1 - i]) + local_ref[i]
        for b in range(SEQ):
            out_ref[b, pl.ds(i, LEAVES, stride=SUB), :] = got[b * LEAVES : (b + 1) * LEAVES]
    both = jnp.sum(got_ref[...], axis=0)
    square, seen = both[SEQ : SEQ + 1], both[SEQ + 1 : SEQ + 2]
    total = float(SEQ * STEPS * BLOCKS)
    prec_ref[...] = lp + (0.5 / total) * on * (seen - square)
    lik = jnp.sum(on * (seen * lp - square), axis=1, keepdims=True) * (0.5 / (total * N))
    lik_ref[...] = jnp.broadcast_to(lik, (1, N))


VM = pl.BlockSpec(memory_space=pltpu.VMEM)
SM = pl.BlockSpec(memory_space=pltpu.SMEM)


def call(kernel, name, specs, shapes, scratch=(), flops=0, moved=0):
    return pl.pallas_call(
        kernel,
        out_shape=shapes,
        in_specs=specs,
        out_specs=jax.tree.map(lambda _: VM, shapes),
        scratch_shapes=list(scratch),
        compiler_params=pltpu.CompilerParams(vmem_limit_bytes=VMEM_LIMIT),
        cost_estimate=pl.CostEstimate(flops=flops, bytes_accessed=moved, transcendentals=0),
        name=name,
    )


def out(shape, dtype=F32):
    return jax.ShapeDtypeStruct(shape, dtype)


def shifted(a, axis, by):
    count = lax.axis_size(axis)
    return lax.ppermute(a, axis, [(i, (i + by) % count) for i in range(count)])


def exchanged(mine, axis, work):
    got = [shifted(mine, axis, d) for d in (1, 2, 3)]
    done = work(mine)
    swaps = [shifted(lax.optimization_barrier((a, done[-1]))[0], "tm_2", 1) for a in got]
    return got, swaps, done


def local(obs, present, sensors, log_prec, dynamics, prior_var, obs_map, init_state):
    lp, pv = log_prec.reshape(1, N), prior_var.reshape(1, N)
    part = out((PART, N))
    square = out((N, N))
    square = out((N, N))
    eye = call(k_first, "k_first", [], square, (), 4 * 10**9, 10**7)()
    root, dyn_t, table, nodes, offs, step, u, mask, obs_s, rows = call(
        k_block,
        "k_block",
        [SM] * 2 + [VM] * 7,
        (
            out((SEQ, N + 8, N)),
            square,
            out((16, N, 2 * N), BF16),
            out((42, N, 2 * N), BF16),
            out((96, N)),
            out((N, 6 * N), BF16),
            out((SUB, ROWS, N)),
            out((SUB, ROWS, N)),
            out((SUB, ROWS, N)),
            out((8, N)),
        ),
        [pltpu.VMEM((SEQ, STEPS, N), F32), pltpu.VMEM((SEQ, STEPS, N), F32)],
        10**9,
        10**6,
    )(present, sensors, eye, obs, present, lp, dynamics, pv, obs_map)
    mate = shifted(root, "tm_2", 1)
    chip, low, high = call(k_core, "k_core", [VM] * 2, (part, part, part), (), 10**7, 10**6)(
        root, mate
    )
    prefix = call(
        k_prefix,
        "k_prefix",
        [VM, SM] + [VM] * 3,
        (out((ROWS, N, N)), out((ROWS, N))),
        (),
        3 * 10**9,
        10**7,
    )
    got, mates, (pre, preoff) = exchanged(
        chip, "tm_1", lambda a: prefix(a, present, table, nodes, offs)
    )
    group, full = call(
        k_total,
        "k_total",
        [VM] * 8,
        (part, out((3, SEQ, N + 8, N))),
        [pltpu.VMEM((4, SEQ, N, N), F32), pltpu.VMEM((4, SEQ, 8, N), F32)],
        10**8,
        10**6,
    )(low, high, *got, *mates)
    powers = call(
        k_powers,
        "k_powers",
        [VM] * 4,
        (
            out((SUB, N, 2 * N), BF16),
            out((LEAVES, N, N)),
            out((len(REACH), N, 2 * N), BF16),
            out((11, N, 2 * N), BF16),
            out((SUB, N, 2 * N), BF16),
        ),
        (),
        3 * 10**9,
        10**7,
    )
    entries = call(
        k_entry, "k_entry", [VM] * 3, (out((SEQ, N, N)), out((8, N))), (), 10**9, 10**7
    )

    def work(a):
        tables = powers(a, eye, dynamics, dyn_t)
        return (*tables, *entries(tables[-1], full, mate))

    got, mates, (near, far, reach, cross, resid, entry, entryoff) = exchanged(group, "tm_0", work)
    send, near_sums, suffix, final = call(
        k_filter,
        "k_filter",
        [VM] * 20,
        (out((BLOCKS, 8, N)), out((SUB, ROWS, N)), out((ROWS, N)), out((8, N))),
        (),
        10**7,
        10**6,
    )(
        *got, *mates, entry, entryoff, init_state, obs_s, rows, dyn_t, pre, preoff, step, u,
        mask, reach, resid, cross,
    )
    got = lax.all_to_all(send, TM, 0, 0, tiled=True)
    smoothed, prec, lik = call(
        k_smooth,
        "k_smooth",
        [VM] * 8,
        (out((SEQ, STEPS, N)), out((1, N)), out((1, N))),
        (),
        10**7,
        10**6,
    )(got, near_sums, suffix, final, rows, far, near, cross)
    return smoothed, prec.reshape(N), lik[0, :1]


def solution(mesh):
    split = Mesh(
        mesh.devices.reshape(mesh.shape["cluster"], 4, 4, 2), ("cluster", "tm_0", "tm_1", "tm_2")
    )
    return jax.shard_map(
        local,
        mesh=split,
        in_specs=(
            P("cluster", TM, None),
            P("cluster", TM),
            P("cluster"),
            P("cluster"),
            P("cluster", None),
            P("cluster"),
            P("cluster", None),
            P("cluster", None),
        ),
        out_specs=(P("cluster", TM, None), P("cluster"), P("cluster")),
        check_vma=False,
    )
```

```python
import jax
import jax.numpy as jnp
from jax import lax
from jax.experimental import pallas as pl
from jax.experimental.pallas import tpu as pltpu
from jax.sharding import Mesh
from jax.sharding import PartitionSpec as P

F32, BF16 = jnp.float32, jnp.bfloat16
TM = ("tm_0", "tm_1", "tm_2")
N = 128
SEQ, STEPS, SUB = 3, 64, 4
LEAVES = STEPS // SUB
ROWS = SEQ * LEAVES
HALF = N // 2
BLOCKS = 32
VMEM_LIMIT = 40 * 1024 * 1024


def dot(a, b):
    return lax.dot(a, b, preferred_element_type=F32)


def lanes(*parts):
    return jnp.concatenate(parts, axis=1)


def stacked(*parts):
    return jnp.concatenate(parts, axis=0)


def split2(a):
    hi = a.astype(BF16)
    return hi, (a - hi.astype(F32)).astype(BF16)


def split3(a):
    hi = a.astype(BF16)
    rest = a - hi.astype(F32)
    mid = rest.astype(BF16)
    return hi, mid, (rest - mid.astype(F32)).astype(BF16)


def pair(a):
    return lanes(*split2(a))


def whole(x):
    n = x.shape[1] // 2
    return x[:, :n].astype(F32) + x[:, n:].astype(F32)


def mul_pair(x, y):
    d = dot(x, stacked(y, y))
    n = y.shape[1] // 2
    return d[:, :n] + d[:, n:]


def mul_exact(a, b):
    a0, a1, a2 = split3(a)
    b0, b1, b2 = split3(b)
    n = b.shape[1]
    y = lanes(b0, b1)
    d = dot(lanes(a0, a1), stacked(y, y))
    return d[:, :n] + (d[:, n:] + dot(lanes(a0, a2), stacked(b2, b0)))


def apply_row(row, matrix):
    column = jnp.transpose(jnp.broadcast_to(row, (N, N)))
    return jnp.sum(column * matrix, axis=0, keepdims=True)


def step_major(ref, i):
    return stacked(*(ref[b, pl.ds(i, LEAVES, stride=SUB), :] for b in range(SEQ)))


def pick(flag, a, b):
    return jnp.where(flag, a, b)


def on_row(sensors_ref):
    return (lax.broadcasted_iota(jnp.int32, (1, N), 1) < sensors_ref[0]).astype(F32)


def identity(rows=N):
    shape = (rows, N)
    return (
        lax.broadcasted_iota(jnp.int32, shape, 0) == lax.broadcasted_iota(jnp.int32, shape, 1)
    ).astype(F32)


def leaf_number(flags, b, j):
    at = 0
    for i in range(SUB):
        at = at * 2 + flags[b, SUB * j + i]
    return at


def joined(left, left_off, right, right_off):
    off = pair(jnp.broadcast_to(left_off, (16, N)))
    got = mul_pair(stacked(left, off), right)
    return got[:N], got[N : N + 1] + right_off


REACH = (1, 2, 3, 4, 8, 12)
LEVELS = ((0, 24), (24, 12), (36, 6))
OFFS = (0, 48, 72, 84)
PART = SEQ * HALF + 8
FULL = SEQ * N + 8


def k_first(eye_ref):
    eye_ref[...] = identity()


def k_block(
    flags, sensors_ref, eye_ref, obs_raw, pres_ref, lp_ref, dyn_ref, pv_ref, map_ref,
    root_ref, dynt_ref, table, nodes, offs, step_ref, u_ref, mask_ref, obs_ref, rows_ref, mask_scr, u_scr,
):
    on = on_row(sensors_ref)
    weight = jnp.exp(lp_ref[...]) * on
    pv, obs_map = pv_ref[...], map_ref[...]
    dyn_t = jnp.transpose(dyn_ref[...])
    dynt_ref[...] = dyn_t
    y = pair(obs_map)
    out_t = mul_pair(pair(dyn_t), pair(jnp.transpose(obs_map)))
    filt_t = dyn_t - mul_pair(pair(out_t * weight), y) * pv
    rows_ref[...] = stacked(on, weight, lp_ref[...], jnp.zeros((5, N), F32))
    step_ref[...] = pair(lanes(dyn_t, filt_t, out_t))
    seen = pres_ref[...].astype(F32)
    seen = jnp.transpose(stacked(seen, jnp.zeros((8 - SEQ, STEPS), F32)))
    for b in range(SEQ):
        mask = jnp.broadcast_to(seen[:, b : b + 1], (STEPS, N))
        mask_scr[b] = mask
        u_scr[b] = mul_pair(pair(obs_raw[b] * weight), y) * pv * mask
    for i in range(SUB):
        u_ref[i] = step_major(u_scr, i)
        mask_ref[i] = step_major(mask_scr, i)
        obs_ref[i] = step_major(obs_raw, i)
    two = mul_exact(stacked(dyn_t, filt_t), lanes(dyn_t, filt_t))
    twos = [two[i * N : (i + 1) * N, j * N : (j + 1) * N] for i in (0, 1) for j in (0, 1)]
    wide = lanes(*twos)
    for i in range(4):
        four = mul_exact(twos[i], wide)
        for j in range(4):
            table[4 * i + j] = pair(four[:, j * N : (j + 1) * N])
    y = pair(lanes(dyn_t, filt_t))
    z = u_ref[0]
    for i in range(1, SUB):
        d = mul_pair(pair(z), y)
        z = pick(mask_ref[i] > 0.5, d[:, N:], d[:, :N]) + u_ref[i]
    offs[0:ROWS, :] = z

    def leaf(k):
        return table[leaf_number(flags, k // LEAVES, k % LEAVES)]

    get = leaf
    for level in range(4):
        count = ROWS >> (level + 1)
        for k in range(count):
            at = OFFS[level] + 2 * k
            matrix, off = joined(
                get(2 * k), offs[at : at + 1, :], get(2 * k + 1), offs[at + 1 : at + 2, :]
            )
            if level == 3:
                root_ref[k, 0:N, :] = matrix
                root_ref[k, N : N + 8, :] = jnp.broadcast_to(off, (8, N))
            else:
                nodes[LEVELS[level][0] + k] = pair(matrix)
                to = OFFS[level + 1] + k
                offs[to : to + 1, :] = off
        if level < 3:
            get = lambda k, level=level: nodes[LEVELS[level][0] + k]


def put(ref, b, matrix):
    rows = matrix.shape[0]
    ref[b * rows : (b + 1) * rows, :] = matrix


def put_offsets(ref, offs):
    rows = ref.shape[0]
    ref[rows - 8 : rows, :] = stacked(*offs, jnp.zeros((8 - SEQ, N), F32))


def offset_of(ref, b):
    at = ref.shape[0] - 8 + b
    return ref[at : at + 1, :]


def half_of(ref, b):
    return ref[b * HALF : (b + 1) * HALF, :]


def full_of(ref, b):
    return ref[b * N : (b + 1) * N, :]


def in_order(mine_ref, mate_ref, b):
    first = lax.axis_index("tm_2") == 0
    mine, mate = half_of(mine_ref, b), half_of(mate_ref, b)
    matrix = stacked(pick(first, mine, mate), pick(first, mate, mine))
    return matrix, offset_of(mine_ref, b)


def chosen(flag, p_ref, q_ref, b):
    return (
        pick(flag, full_of(p_ref, b), full_of(q_ref, b)),
        pick(flag, offset_of(p_ref, b), offset_of(q_ref, b)),
    )


def around(refs, b):
    near, near_mate, two, two_mate = refs
    first = lax.axis_index("tm_2") == 0
    return (
        chosen(first, near, near_mate, b),
        in_order(two, two_mate, b),
        chosen(first, near_mate, near, b),
    )


def then(p, q):
    return joined(pair(p[0]), p[1], pair(q[0]), q[1])


def put_both(full_ref, mine_ref, maps):
    first = lax.axis_index("tm_2") == 0
    for b, (matrix, off) in enumerate(maps):
        put(full_ref, b, matrix)
        put(mine_ref, b, pick(first, matrix[:HALF], matrix[HALF:]))
    for ref in (full_ref, mine_ref):
        put_offsets(ref, [off for _, off in maps])


def k_core(own_ref, mate_ref, out_ref, mine_ref):
    first = lax.axis_index("tm_2") == 0
    maps = []
    for b in range(SEQ):
        own, mate = own_ref[b], mate_ref[b]
        p, q = pick(first, own, mate), pick(first, mate, own)
        maps.append(then((p[:N], p[N : N + 1]), (q[:N], q[N : N + 1])))
    put_both(out_ref, mine_ref, maps)


def k_total(own_ref, near, near_mate, two, two_mate, out_ref, mine_ref, ahead_ref, maps, offs):
    me = lax.axis_index("tm_1")
    for b in range(SEQ):
        for d, (matrix, off) in enumerate(around((near, near_mate, two, two_mate), b)):
            slot = lax.rem(me + 3 - d, 4)
            off = jnp.broadcast_to(off, (8, N))
            maps[slot, b] = matrix
            offs[slot, b] = off
            ahead_ref[d, b, 0:N, :] = matrix
            ahead_ref[d, b, N : N + 8, :] = off
        maps[me, b] = full_of(own_ref, b)
        offs[me, b] = jnp.broadcast_to(offset_of(own_ref, b), (8, N))
    ends = []
    for b in range(SEQ):
        p = [(maps[k, b], offs[k, b, 0:1, :]) for k in range(4)]
        ends.append(then(then(p[0], p[1]), then(p[2], p[3])))
    put_both(out_ref, mine_ref, ends)


def k_prefix(chip_ref, flags, table, nodes, offs, pre_ref, preoff_ref):
    preoff_ref[...] = jnp.zeros_like(preoff_ref)
    for b in range(SEQ):
        pre_ref[b * LEAVES] = jnp.zeros((N, N), F32)
        for level in (3, 2, 1, 0):
            parents = 8 >> level
            span = LEAVES // parents
            for k in range(parents):
                at = b * LEAVES + k * span
                left = b * 2 * parents + 2 * k
                off = offs[OFFS[level] + left : OFFS[level] + left + 1, :]
                if level == 0:
                    got = table[leaf_number(flags, left // LEAVES, left % LEAVES)]
                else:
                    got = nodes[LEVELS[level - 1][0] + left]
                if k == 0:
                    matrix = whole(got)
                else:
                    matrix, off = joined(
                        pair(pre_ref[at]), preoff_ref[at : at + 1, :], got, off
                    )
                to = at + span // 2
                pre_ref[to] = matrix
                preoff_ref[to : to + 1, :] = off


def k_powers(
    eye_ref, dyn_ref, dynt_ref, near_ref, far_ref, reach_ref, cross_ref, resid_ref
):
    eye, dyn = eye_ref[...], dyn_ref[...]
    d2 = mul_exact(dyn, dyn)
    d34 = mul_exact(d2, lanes(dyn, d2))
    d3, d4 = d34[:, :N], d34[:, N:]
    for i, a in enumerate((dyn, d2, d3, d4)):
        near_ref[i] = pair(a)
    resid = eye - mul_exact(dynt_ref[...], dyn)
    resid_ref[0] = pair(resid)
    more = mul_exact(resid, lanes(dyn, d2, d3))
    for i in range(3):
        resid_ref[i + 1] = pair(more[:, i * N : (i + 1) * N])
    far_ref[0] = eye
    far_ref[1] = d4
    for have in (1, 2, 4, 8):
        last = far_ref[have]
        for k in range(1, have + 1):
            got = mul_exact(last, far_ref[k])
            if have + k < LEAVES:
                far_ref[have + k] = got
    for i, k in enumerate(REACH):
        reach_ref[i] = pair(far_ref[k])
    cross_ref[0] = pair(eye)
    powers = [None, got]
    for k in range(2, 9):
        powers.append(mul_exact(powers[k // 2], powers[k - k // 2]))
    for k in range(1, 8):
        cross_ref[k] = pair(powers[k])
    w16 = mul_exact(powers[8], powers[8])
    cross_ref[8] = pair(powers[8])
    cross_ref[9] = pair(w16)
    cross_ref[10] = pair(mul_exact(w16, powers[8]))


def k_entry(ahead_ref, mate_ref, entry_ref, entryoff_ref):
    me, second = lax.axis_index("tm_1"), lax.axis_index("tm_2") == 1
    entryoff_ref[...] = jnp.zeros_like(entryoff_ref)
    for b in range(SEQ):
        so_far = (identity(), jnp.zeros((1, N), F32))
        for source, flag in (
            (ahead_ref.at[2], me >= 3), (ahead_ref.at[1], me >= 2), (ahead_ref.at[0], me >= 1),
            (mate_ref, second),
        ):
            got = then(so_far, (source[b, 0:N, :], source[b, N : N + 1, :]))
            so_far = (pick(flag, got[0], so_far[0]), pick(flag, got[1], so_far[1]))
        entry_ref[b] = so_far[0]
        entryoff_ref[b : b + 1, :] = so_far[1]


def k_tables(
    after_ref, eye_ref, dyn_ref, dynt_ref, ahead_ref, mate_ref,
    near_ref, far_ref, reach_ref, cross_ref, resid_ref, entry_ref, entryoff_ref,
):
    k_entry(ahead_ref, mate_ref, entry_ref, entryoff_ref)
    k_powers(eye_ref, dyn_ref, dynt_ref, near_ref, far_ref, reach_ref, cross_ref, resid_ref)


def k_filter(
    near, near_mate, two, two_mate, entry_ref, entryoff_ref, init_ref, obs_ref,
    rows_ref, dynt_ref, pre_ref, preoff_ref, step_ref, u_ref, mask_ref, reach_ref,
    resid_ref, cross_ref, send_ref, local_ref, suffix_ref, final_ref,
):
    group = lax.axis_index("tm_0")
    last = (group == 3) & (lax.axis_index("tm_1") == 3) & (lax.axis_index("tm_2") == 1)
    starts = []
    for b in range(SEQ):
        row = init_ref[b : b + 1, :]
        ahead = around((near, near_mate, two, two_mate), b)
        for d in (3, 2, 1):
            matrix, off = ahead[d - 1]
            row = pick(group >= d, apply_row(row, matrix) + off, row)
        starts.append(apply_row(row, entry_ref[b]) + entryoff_ref[b : b + 1, :])
    rows = []
    for b in range(SEQ):
        column = jnp.transpose(jnp.broadcast_to(starts[b], (N, N)))
        rows.append(starts[b])
        for j in range(1, LEAVES):
            k = b * LEAVES + j
            rows.append(
                jnp.sum(column * pre_ref[k], axis=0, keepdims=True) + preoff_ref[k : k + 1, :]
            )
    state = stacked(*rows)
    weight = rows_ref[1:2, :]
    step = step_ref[...]
    square = jnp.zeros((ROWS, N), F32)
    seen = jnp.zeros((ROWS, N), F32)
    sums = [None] * SUB
    for i in range(SUB):
        d = mul_pair(pair(state), step)
        mask = mask_ref[i]
        error = obs_ref[i] - d[:, 2 * N :]
        square = square + mask * (error * error)
        seen = seen + mask
        state = pick(mask > 0.5, d[:, N : 2 * N], d[:, :N]) + u_ref[i]
        x = pair(state)
        for k in range(i + 1):
            add = mul_pair(x, resid_ref[i - k])
            sums[k] = add if k == i else sums[k] + add
    square = jnp.sum(square, axis=0, keepdims=True) * weight
    seen = jnp.sum(seen, axis=0, keepdims=True)
    ends = stacked(*(state[(b + 1) * LEAVES - 1 : (b + 1) * LEAVES, :] for b in range(SEQ)))
    ends = stacked(ends, jnp.zeros((8 - SEQ, N), F32))
    final = mul_pair(pair(ends), pair(dynt_ref[...]))
    final_ref[...] = final
    place = lax.broadcasted_iota(jnp.int32, (ROWS, N), 0) % LEAVES
    run = sums[0]
    for first in (0, 3):
        total = run
        for k in range(first, first + 3):
            moved = pltpu.roll(mul_pair(pair(run), reach_ref[k]), ROWS - REACH[k], 0)
            total = total + pick(place < LEAVES - REACH[k], moved, 0.0)
        run = total
    for i in range(SUB):
        local_ref[i] = sums[i]
    suffix_ref[...] = run
    offsets = stacked(*(run[b * LEAVES : b * LEAVES + 1, :] for b in range(SEQ)))
    offsets = stacked(offsets, jnp.zeros((8 - SEQ, N), F32))
    through = mul_pair(pair(final), cross_ref[1])
    offsets = offsets + pick(last, through, 0.0)
    packed = stacked(offsets[:SEQ], square, seen, jnp.zeros((8 - SEQ - 2, N), F32))
    send_ref[...] = jnp.broadcast_to(packed[None], (BLOCKS, 8, N))


def k_smooth(
    got_ref, local_ref, suffix_ref, final_ref, rows_ref, far_ref, near_ref, cross_ref,
    out_ref, prec_ref, lik_ref,
):
    me = (lax.axis_index("tm_0") * 4 + lax.axis_index("tm_1")) * 2 + lax.axis_index("tm_2")
    on, lp = rows_ref[0:1, :], rows_ref[2:3, :]
    acc = jnp.zeros((4 * 8, N), F32)
    for h in range(8):
        parts = []
        for g in range(4):
            at = me + 1 + 8 * g + h
            parts.append(pick(at < BLOCKS, got_ref[jnp.minimum(at, BLOCKS - 1)], 0.0))
        acc = acc + mul_pair(pair(stacked(*parts)), cross_ref[h])
    leaving = acc[0:8]
    for g in range(1, 4):
        leaving = leaving + mul_pair(pair(acc[8 * g : 8 * g + 8]), cross_ref[7 + g])
    leaving = pick(me == BLOCKS - 1, final_ref[...], leaving)
    rows = []
    for b in range(SEQ):
        column = jnp.transpose(jnp.broadcast_to(leaving[b : b + 1, :], (N, N)))
        for j in range(LEAVES - 1):
            k = b * LEAVES + j
            rows.append(
                jnp.sum(column * far_ref[LEAVES - 1 - j], axis=0, keepdims=True)
                + suffix_ref[k + 1 : k + 2, :]
            )
        rows.append(leaving[b : b + 1, :])
    x = pair(stacked(*rows))
    for i in range(SUB):
        got = mul_pair(x, near_ref[SUB - 1 - i]) + local_ref[i]
        for b in range(SEQ):
            out_ref[b, pl.ds(i, LEAVES, stride=SUB), :] = got[b * LEAVES : (b + 1) * LEAVES]
    both = jnp.sum(got_ref[...], axis=0)
    square, seen = both[SEQ : SEQ + 1], both[SEQ + 1 : SEQ + 2]
    total = float(SEQ * STEPS * BLOCKS)
    prec_ref[...] = lp + (0.5 / total) * on * (seen - square)
    lik = jnp.sum(on * (seen * lp - square), axis=1, keepdims=True) * (0.5 / (total * N))
    lik_ref[...] = jnp.broadcast_to(lik, (1, N))


VM = pl.BlockSpec(memory_space=pltpu.VMEM)
SM = pl.BlockSpec(memory_space=pltpu.SMEM)


def call(kernel, name, specs, shapes, scratch=(), flops=0, moved=0):
    return pl.pallas_call(
        kernel,
        out_shape=shapes,
        in_specs=specs,
        out_specs=jax.tree.map(lambda _: VM, shapes),
        scratch_shapes=list(scratch),
        compiler_params=pltpu.CompilerParams(vmem_limit_bytes=VMEM_LIMIT),
        cost_estimate=pl.CostEstimate(flops=flops, bytes_accessed=moved, transcendentals=0),
        name=name,
    )


def out(shape, dtype=F32):
    return jax.ShapeDtypeStruct(shape, dtype)


def shifted(a, axis, by):
    count = lax.axis_size(axis)
    return lax.ppermute(a, axis, [(i, (i + by) % count) for i in range(count)])


def exchanged(full, mine, axis, work):
    ring = [(2 * i, (2 * i + 2) % 8) for i in range(4)] + [
        (2 * i + 1, (2 * i + 7) % 8) for i in range(4)
    ]
    got = [lax.ppermute(full, (axis, "tm_2"), ring), shifted(mine, axis, 2)]
    done = work(full)
    swaps = [shifted(lax.optimization_barrier((a, done[-1]))[0], "tm_2", 1) for a in got]
    return (got[0], swaps[0], got[1], swaps[1]), done


def local(obs, present, sensors, log_prec, dynamics, prior_var, obs_map, init_state):
    lp, pv = log_prec.reshape(1, N), prior_var.reshape(1, N)
    both = (out((FULL, N)), out((PART, N)))
    square = out((N, N))
    square = out((N, N))
    eye = call(k_first, "k_first", [], square, (), 4 * 10**9, 10**7)()
    root, dyn_t, table, nodes, offs, step, u, mask, obs_s, rows = call(
        k_block,
        "k_block",
        [SM] * 2 + [VM] * 7,
        (
            out((SEQ, N + 8, N)),
            square,
            out((16, N, 2 * N), BF16),
            out((42, N, 2 * N), BF16),
            out((96, N)),
            out((N, 6 * N), BF16),
            out((SUB, ROWS, N)),
            out((SUB, ROWS, N)),
            out((SUB, ROWS, N)),
            out((8, N)),
        ),
        [pltpu.VMEM((SEQ, STEPS, N), F32), pltpu.VMEM((SEQ, STEPS, N), F32)],
        10**9,
        10**6,
    )(present, sensors, eye, obs, present, lp, dynamics, pv, obs_map)
    mate = shifted(root, "tm_2", 1)
    chip, mine = call(k_core, "k_core", [VM] * 2, both, (), 10**7, 10**6)(root, mate)
    prefix = call(
        k_prefix,
        "k_prefix",
        [VM, SM] + [VM] * 3,
        (out((ROWS, N, N)), out((ROWS, N))),
        (),
        3 * 10**9,
        10**7,
    )
    got, (pre, preoff) = exchanged(
        chip, mine, "tm_1", lambda a: prefix(a, present, table, nodes, offs)
    )
    group, mine, ahead = call(
        k_total,
        "k_total",
        [VM] * 5,
        (*both, out((3, SEQ, N + 8, N))),
        [pltpu.VMEM((4, SEQ, N, N), F32), pltpu.VMEM((4, SEQ, 8, N), F32)],
        10**8,
        10**6,
    )(chip, *got)
    tables = call(
        k_tables,
        "k_tables",
        [VM] * 6,
        (
            out((SUB, N, 2 * N), BF16),
            out((LEAVES, N, N)),
            out((len(REACH), N, 2 * N), BF16),
            out((11, N, 2 * N), BF16),
            out((SUB, N, 2 * N), BF16),
            out((SEQ, N, N)),
            out((8, N)),
        ),
        (),
        4 * 10**9,
        10**7,
    )
    got, (near, far, reach, cross, resid, entry, entryoff) = exchanged(
        group, mine, "tm_0", lambda a: tables(a, eye, dynamics, dyn_t, ahead, mate)
    )
    send, near_sums, suffix, final = call(
        k_filter,
        "k_filter",
        [VM] * 18,
        (out((BLOCKS, 8, N)), out((SUB, ROWS, N)), out((ROWS, N)), out((8, N))),
        (),
        10**7,
        10**6,
    )(
        *got, entry, entryoff, init_state, obs_s, rows, dyn_t, pre, preoff, step, u,
        mask, reach, resid, cross,
    )
    got = lax.all_to_all(send, TM, 0, 0, tiled=True)
    smoothed, prec, lik = call(
        k_smooth,
        "k_smooth",
        [VM] * 8,
        (out((SEQ, STEPS, N)), out((1, N)), out((1, N))),
        (),
        10**7,
        10**6,
    )(got, near_sums, suffix, final, rows, far, near, cross)
    return smoothed, prec.reshape(N), lik[0, :1]


def solution(mesh):
    split = Mesh(
        mesh.devices.reshape(mesh.shape["cluster"], 4, 4, 2), ("cluster", "tm_0", "tm_1", "tm_2")
    )
    return jax.shard_map(
        local,
        mesh=split,
        in_specs=(
            P("cluster", TM, None),
            P("cluster", TM),
            P("cluster"),
            P("cluster"),
            P("cluster", None),
            P("cluster"),
            P("cluster", None),
            P("cluster", None),
        ),
        out_specs=(P("cluster", TM, None), P("cluster"), P("cluster")),
        check_vma=False,
    )
```

```python
import jax
import jax.numpy as jnp
from jax import lax
from jax.experimental import pallas as pl
from jax.experimental.pallas import tpu as pltpu
from jax.sharding import Mesh
from jax.sharding import PartitionSpec as P

F32, BF16 = jnp.float32, jnp.bfloat16
TM = ("tm_0", "tm_1", "tm_2")
N = 128
SEQ, STEPS, SUB = 3, 64, 4
LEAVES = STEPS // SUB
ROWS = SEQ * LEAVES
HALF = N // 2
BLOCKS = 32
VMEM_LIMIT = 40 * 1024 * 1024


def dot(a, b):
    return lax.dot(a, b, preferred_element_type=F32)


def lanes(*parts):
    return jnp.concatenate(parts, axis=1)


def stacked(*parts):
    return jnp.concatenate(parts, axis=0)


def split2(a):
    hi = a.astype(BF16)
    return hi, (a - hi.astype(F32)).astype(BF16)


def split3(a):
    hi = a.astype(BF16)
    rest = a - hi.astype(F32)
    mid = rest.astype(BF16)
    return hi, mid, (rest - mid.astype(F32)).astype(BF16)


def pair(a):
    return lanes(*split2(a))


def whole(x):
    n = x.shape[1] // 2
    return x[:, :n].astype(F32) + x[:, n:].astype(F32)


def mul_pair(x, y):
    d = dot(x, stacked(y, y))
    n = y.shape[1] // 2
    return d[:, :n] + d[:, n:]


def mul_exact(a, b):
    a0, a1, a2 = split3(a)
    b0, b1, b2 = split3(b)
    n = b.shape[1]
    y = lanes(b0, b1)
    d = dot(lanes(a0, a1), stacked(y, y))
    return d[:, :n] + (d[:, n:] + dot(lanes(a0, a2), stacked(b2, b0)))


def apply_row(row, matrix):
    column = jnp.transpose(jnp.broadcast_to(row, (N, N)))
    return jnp.sum(column * matrix, axis=0, keepdims=True)


def step_major(ref, i):
    return stacked(*(ref[b, pl.ds(i, LEAVES, stride=SUB), :] for b in range(SEQ)))


def pick(flag, a, b):
    return jnp.where(flag, a, b)


def on_row(sensors_ref):
    return (lax.broadcasted_iota(jnp.int32, (1, N), 1) < sensors_ref[0]).astype(F32)


def identity(rows=N):
    shape = (rows, N)
    return (
        lax.broadcasted_iota(jnp.int32, shape, 0) == lax.broadcasted_iota(jnp.int32, shape, 1)
    ).astype(F32)


def leaf_number(flags, b, j):
    at = 0
    for i in range(SUB):
        at = at * 2 + flags[b, SUB * j + i]
    return at


def joined(left, left_off, right, right_off):
    off = pair(jnp.broadcast_to(left_off, (16, N)))
    got = mul_pair(stacked(left, off), right)
    return got[:N], got[N : N + 1] + right_off


REACH = (1, 2, 3, 4, 8, 12)
LEVELS = ((0, 24), (24, 12), (36, 6))
OFFS = (0, 48, 72, 84)
PART = SEQ * HALF + 8
FULL = SEQ * N + 8


def k_first(eye_ref):
    eye_ref[...] = identity()


def k_block(
    flags, sensors_ref, eye_ref, obs_raw, pres_ref, lp_ref, dyn_ref, pv_ref, map_ref,
    root_ref, dynt_ref, table, nodes, offs, step_ref, twos_ref, u_ref, mask_ref, obs_ref, rows_ref, mask_scr, u_scr,
):
    on = on_row(sensors_ref)
    weight = jnp.exp(lp_ref[...]) * on
    pv, obs_map = pv_ref[...], map_ref[...]
    dyn_t = jnp.transpose(dyn_ref[...])
    dynt_ref[...] = dyn_t
    y = pair(obs_map)
    out_t = mul_pair(pair(dyn_t), pair(jnp.transpose(obs_map)))
    filt_t = dyn_t - mul_pair(pair(out_t * weight), y) * pv
    rows_ref[...] = stacked(on, weight, lp_ref[...], jnp.zeros((5, N), F32))
    step_ref[...] = pair(lanes(dyn_t, filt_t, out_t))
    seen = pres_ref[...].astype(F32)
    seen = jnp.transpose(stacked(seen, jnp.zeros((8 - SEQ, STEPS), F32)))
    for b in range(SEQ):
        mask = jnp.broadcast_to(seen[:, b : b + 1], (STEPS, N))
        mask_scr[b] = mask
        u_scr[b] = mul_pair(pair(obs_raw[b] * weight), y) * pv * mask
    for i in range(SUB):
        u_ref[i] = step_major(u_scr, i)
        mask_ref[i] = step_major(mask_scr, i)
        obs_ref[i] = step_major(obs_raw, i)
    two = mul_exact(stacked(dyn_t, filt_t), lanes(dyn_t, filt_t))
    twos = [two[i * N : (i + 1) * N, j * N : (j + 1) * N] for i in (0, 1) for j in (0, 1)]
    wide = lanes(*twos)
    twos_ref[...] = pair(wide)
    for i in range(4):
        four = mul_exact(twos[i], wide)
        for j in range(4):
            table[4 * i + j] = pair(four[:, j * N : (j + 1) * N])
    y = pair(lanes(dyn_t, filt_t))
    z = u_ref[0]
    for i in range(1, SUB):
        d = mul_pair(pair(z), y)
        z = pick(mask_ref[i] > 0.5, d[:, N:], d[:, :N]) + u_ref[i]
    offs[0:ROWS, :] = z

    def leaf(k):
        return table[leaf_number(flags, k // LEAVES, k % LEAVES)]

    get = leaf
    for level in range(4):
        count = ROWS >> (level + 1)
        for k in range(count):
            at = OFFS[level] + 2 * k
            matrix, off = joined(
                get(2 * k), offs[at : at + 1, :], get(2 * k + 1), offs[at + 1 : at + 2, :]
            )
            if level == 3:
                root_ref[k, 0:N, :] = matrix
                root_ref[k, N : N + 8, :] = jnp.broadcast_to(off, (8, N))
            else:
                nodes[LEVELS[level][0] + k] = pair(matrix)
                to = OFFS[level + 1] + k
                offs[to : to + 1, :] = off
        if level < 3:
            get = lambda k, level=level: nodes[LEVELS[level][0] + k]


def put(ref, b, matrix):
    rows = matrix.shape[0]
    ref[b * rows : (b + 1) * rows, :] = matrix


def put_offsets(ref, offs):
    rows = ref.shape[0]
    ref[rows - 8 : rows, :] = stacked(*offs, jnp.zeros((8 - SEQ, N), F32))


def offset_of(ref, b):
    at = ref.shape[0] - 8 + b
    return ref[at : at + 1, :]


def half_of(ref, b):
    return ref[b * HALF : (b + 1) * HALF, :]


def full_of(ref, b):
    return ref[b * N : (b + 1) * N, :]


def in_order(mine_ref, mate_ref, b):
    first = lax.axis_index("tm_2") == 0
    mine, mate = half_of(mine_ref, b), half_of(mate_ref, b)
    matrix = stacked(pick(first, mine, mate), pick(first, mate, mine))
    return matrix, offset_of(mine_ref, b)


def chosen(flag, p_ref, q_ref, b):
    return (
        pick(flag, full_of(p_ref, b), full_of(q_ref, b)),
        pick(flag, offset_of(p_ref, b), offset_of(q_ref, b)),
    )


def then(p, q):
    return joined(pair(p[0]), p[1], pair(q[0]), q[1])


def put_all(ref, maps):
    for b, (matrix, _) in enumerate(maps):
        put(ref, b, matrix)
    put_offsets(ref, [off for _, off in maps])


def put_halves(ref, maps):
    first = lax.axis_index("tm_2") == 0
    put_all(ref, [(pick(first, m[:HALF], m[HALF:]), off) for m, off in maps])


def k_core(own_ref, mate_ref, out_ref, mine_ref):
    first = lax.axis_index("tm_2") == 0
    maps = []
    for b in range(SEQ):
        own, mate = own_ref[b], mate_ref[b]
        p, q = pick(first, own, mate), pick(first, mate, own)
        maps.append(then((p[:N], p[N : N + 1]), (q[:N], q[N : N + 1])))
    put_all(out_ref, maps)
    put_halves(mine_ref, maps)


def k_total(
    own_ref, near, near_mate, two, two_mate, init_ref, mine_ref, state_ref, ahead_ref, maps, offs
):
    me, first = lax.axis_index("tm_1"), lax.axis_index("tm_2") == 0
    state_ref[...] = jnp.zeros_like(state_ref)
    for b in range(SEQ):
        ring = (
            chosen(first, near, near_mate, b),
            in_order(two, two_mate, b),
            chosen(first, near_mate, near, b),
        )
        for d, (matrix, off) in enumerate(ring):
            slot = lax.rem(me + 3 - d, 4)
            off = jnp.broadcast_to(off, (8, N))
            maps[slot, b] = matrix
            offs[slot, b] = off
            ahead_ref[d, b, 0:N, :] = matrix
            ahead_ref[d, b, N : N + 8, :] = off
        maps[me, b] = full_of(own_ref, b)
        offs[me, b] = jnp.broadcast_to(offset_of(own_ref, b), (8, N))
    ends = []
    for b in range(SEQ):
        p = [(maps[k, b], offs[k, b, 0:1, :]) for k in range(4)]
        ends.append(then(then(p[0], p[1]), then(p[2], p[3])))
        state_ref[b : b + 1, :] = apply_row(init_ref[b : b + 1, :], ends[b][0]) + ends[b][1]
    put_halves(mine_ref, ends)


def k_prefix(flags, table, nodes, offs, step_ref, u_ref, mask_ref, pre_ref, preoff_ref, u2_ref):
    y = lanes(step_ref[:, 0 : 2 * N], step_ref[:, 3 * N : 5 * N])
    for i in range(SUB // 2):
        d = mul_pair(pair(u_ref[2 * i]), y)
        u2_ref[i] = pick(mask_ref[2 * i + 1] > 0.5, d[:, N:], d[:, :N]) + u_ref[2 * i + 1]
    preoff_ref[...] = jnp.zeros_like(preoff_ref)
    for b in range(SEQ):
        pre_ref[b * LEAVES] = jnp.zeros((N, N), F32)
        for level in (3, 2, 1, 0):
            parents = 8 >> level
            span = LEAVES // parents
            for k in range(parents):
                at = b * LEAVES + k * span
                left = b * 2 * parents + 2 * k
                off = offs[OFFS[level] + left : OFFS[level] + left + 1, :]
                if level == 0:
                    got = table[leaf_number(flags, left // LEAVES, left % LEAVES)]
                else:
                    got = nodes[LEVELS[level - 1][0] + left]
                if k == 0:
                    matrix = whole(got)
                else:
                    matrix, off = joined(
                        pair(pre_ref[at]), preoff_ref[at : at + 1, :], got, off
                    )
                to = at + span // 2
                pre_ref[to] = matrix
                preoff_ref[to : to + 1, :] = off


def k_powers(
    eye_ref, dyn_ref, dynt_ref, near_ref, far_ref, reach_ref, cross_ref, resid_ref
):
    eye, dyn = eye_ref[...], dyn_ref[...]
    d2 = mul_exact(dyn, dyn)
    d34 = mul_exact(d2, lanes(dyn, d2))
    d3, d4 = d34[:, :N], d34[:, N:]
    for i, a in enumerate((dyn, d2, d3, d4)):
        near_ref[i] = pair(a)
    resid = eye - mul_exact(dynt_ref[...], dyn)
    resid_ref[0] = pair(resid)
    more = mul_exact(resid, lanes(dyn, d2, d3))
    for i in range(3):
        resid_ref[i + 1] = pair(more[:, i * N : (i + 1) * N])
    far_ref[0] = eye
    far_ref[1] = d4
    for have in (1, 2, 4, 8):
        last = far_ref[have]
        for k in range(1, have + 1):
            got = mul_exact(last, far_ref[k])
            if have + k < LEAVES:
                far_ref[have + k] = got
    for i, k in enumerate(REACH):
        reach_ref[i] = pair(far_ref[k])
    cross_ref[0] = pair(eye)
    powers = [None, got]
    for k in range(2, 9):
        powers.append(mul_exact(powers[k // 2], powers[k - k // 2]))
    for k in range(1, 8):
        cross_ref[k] = pair(powers[k])
    w16 = mul_exact(powers[8], powers[8])
    cross_ref[8] = pair(powers[8])
    cross_ref[9] = pair(w16)
    cross_ref[10] = pair(mul_exact(w16, powers[8]))


def k_entry(after_ref, ahead_ref, mate_ref, entry_ref, entryoff_ref):
    me, second = lax.axis_index("tm_1"), lax.axis_index("tm_2") == 1
    entryoff_ref[...] = jnp.zeros_like(entryoff_ref)
    for b in range(SEQ):
        so_far = (identity(), jnp.zeros((1, N), F32))
        for source, flag in (
            (ahead_ref.at[2], me >= 3), (ahead_ref.at[1], me >= 2), (ahead_ref.at[0], me >= 1),
            (mate_ref, second),
        ):
            got = then(so_far, (source[b, 0:N, :], source[b, N : N + 1, :]))
            so_far = (pick(flag, got[0], so_far[0]), pick(flag, got[1], so_far[1]))
        entry_ref[b] = so_far[0]
        entryoff_ref[b : b + 1, :] = so_far[1]


def k_tables(
    after_ref, flags, table, nodes, offs, step_ref, u_ref, mask_ref, eye_ref, dyn_ref, dynt_ref,
    pre_ref, preoff_ref, u2_ref, near_ref, far_ref, reach_ref, cross_ref, resid_ref,
):
    k_prefix(flags, table, nodes, offs, step_ref, u_ref, mask_ref, pre_ref, preoff_ref, u2_ref)
    k_powers(eye_ref, dyn_ref, dynt_ref, near_ref, far_ref, reach_ref, cross_ref, resid_ref)


def k_filter(
    one, one_mate, two, two_mate, sent, sent_mate, entry_ref, entryoff_ref, init_ref, obs_ref,
    rows_ref, dynt_ref, pre_ref, preoff_ref, step_ref, twos_ref, u_ref, u2_ref, mask_ref, reach_ref,
    resid_ref, cross_ref, send_ref, local_ref, suffix_ref, final_ref,
):
    group, core = lax.axis_index("tm_0"), lax.axis_index("tm_2")
    direct = ((group == 2) & (core == 0)) | ((group == 3) & (core == 1))
    last = (group == 3) & (lax.axis_index("tm_1") == 3) & (lax.axis_index("tm_2") == 1)
    starts = []
    for b in range(SEQ):
        row = pick(direct, sent[b : b + 1, :], sent_mate[b : b + 1, :])
        row = pick(group >= 2, row, init_ref[b : b + 1, :])
        for flag, mine, mate in ((group == 3, two, two_mate), (group >= 1, one, one_mate)):
            matrix, off = in_order(mine, mate, b)
            row = pick(flag, apply_row(row, matrix) + off, row)
        starts.append(apply_row(row, entry_ref[b]) + entryoff_ref[b : b + 1, :])
    rows = []
    for b in range(SEQ):
        column = jnp.transpose(jnp.broadcast_to(starts[b], (N, N)))
        rows.append(starts[b])
        for j in range(1, LEAVES):
            k = b * LEAVES + j
            rows.append(
                jnp.sum(column * pre_ref[k], axis=0, keepdims=True) + preoff_ref[k : k + 1, :]
            )
    state = stacked(*rows)
    weight = rows_ref[1:2, :]
    step = step_ref[...]
    square = jnp.zeros((ROWS, N), F32)
    seen = jnp.zeros((ROWS, N), F32)
    sums = [None] * SUB
    out_pair = lanes(step[:, 2 * N : 3 * N], step[:, 5 * N : 6 * N])
    for i in range(0, SUB, 2):
        x = pair(state)
        d = mul_pair(x, step)
        q = mul_pair(x, twos_ref[...])
        m1, m2 = mask_ref[i], mask_ref[i + 1]
        on1, on2 = m1 > 0.5, m2 > 0.5
        middle = pick(on1, d[:, N : 2 * N], d[:, :N]) + u_ref[i]
        state = u2_ref[i // 2] + pick(
            on1,
            pick(on2, q[:, 3 * N :], q[:, 2 * N : 3 * N]),
            pick(on2, q[:, N : 2 * N], q[:, :N]),
        )
        x1 = pair(middle)
        e1 = obs_ref[i] - d[:, 2 * N :]
        e2 = obs_ref[i + 1] - mul_pair(x1, out_pair)
        square = square + m1 * (e1 * e1) + m2 * (e2 * e2)
        seen = seen + m1 + m2
        for j, x in ((i, x1), (i + 1, pair(state))):
            for k in range(j + 1):
                add = mul_pair(x, resid_ref[j - k])
                sums[k] = add if k == j else sums[k] + add
    square = jnp.sum(square, axis=0, keepdims=True) * weight
    seen = jnp.sum(seen, axis=0, keepdims=True)
    ends = stacked(*(state[(b + 1) * LEAVES - 1 : (b + 1) * LEAVES, :] for b in range(SEQ)))
    ends = stacked(ends, jnp.zeros((8 - SEQ, N), F32))
    final = mul_pair(pair(ends), pair(dynt_ref[...]))
    final_ref[...] = final
    place = lax.broadcasted_iota(jnp.int32, (ROWS, N), 0) % LEAVES
    run = sums[0]
    for first in (0, 3):
        total = run
        for k in range(first, first + 3):
            moved = pltpu.roll(mul_pair(pair(run), reach_ref[k]), ROWS - REACH[k], 0)
            total = total + pick(place < LEAVES - REACH[k], moved, 0.0)
        run = total
    for i in range(SUB):
        local_ref[i] = sums[i]
    suffix_ref[...] = run
    offsets = stacked(*(run[b * LEAVES : b * LEAVES + 1, :] for b in range(SEQ)))
    offsets = stacked(offsets, jnp.zeros((8 - SEQ, N), F32))
    through = mul_pair(pair(final), cross_ref[1])
    offsets = offsets + pick(last, through, 0.0)
    packed = stacked(offsets[:SEQ], square, seen, jnp.zeros((8 - SEQ - 2, N), F32))
    send_ref[...] = jnp.broadcast_to(packed[None], (BLOCKS, 8, N))


def k_smooth(
    got_ref, local_ref, suffix_ref, final_ref, rows_ref, far_ref, near_ref, cross_ref,
    out_ref, prec_ref, lik_ref,
):
    me = (lax.axis_index("tm_0") * 4 + lax.axis_index("tm_1")) * 2 + lax.axis_index("tm_2")
    on, lp = rows_ref[0:1, :], rows_ref[2:3, :]
    acc = jnp.zeros((4 * 8, N), F32)
    for h in range(8):
        parts = []
        for g in range(4):
            at = me + 1 + 8 * g + h
            parts.append(pick(at < BLOCKS, got_ref[jnp.minimum(at, BLOCKS - 1)], 0.0))
        acc = acc + mul_pair(pair(stacked(*parts)), cross_ref[h])
    leaving = acc[0:8]
    for g in range(1, 4):
        leaving = leaving + mul_pair(pair(acc[8 * g : 8 * g + 8]), cross_ref[7 + g])
    leaving = pick(me == BLOCKS - 1, final_ref[...], leaving)
    rows = []
    for b in range(SEQ):
        column = jnp.transpose(jnp.broadcast_to(leaving[b : b + 1, :], (N, N)))
        for j in range(LEAVES - 1):
            k = b * LEAVES + j
            rows.append(
                jnp.sum(column * far_ref[LEAVES - 1 - j], axis=0, keepdims=True)
                + suffix_ref[k + 1 : k + 2, :]
            )
        rows.append(leaving[b : b + 1, :])
    x = pair(stacked(*rows))
    for i in range(SUB):
        got = mul_pair(x, near_ref[SUB - 1 - i]) + local_ref[i]
        for b in range(SEQ):
            out_ref[b, pl.ds(i, LEAVES, stride=SUB), :] = got[b * LEAVES : (b + 1) * LEAVES]
    both = jnp.sum(got_ref[...], axis=0)
    square, seen = both[SEQ : SEQ + 1], both[SEQ + 1 : SEQ + 2]
    total = float(SEQ * STEPS * BLOCKS)
    prec_ref[...] = lp + (0.5 / total) * on * (seen - square)
    lik = jnp.sum(on * (seen * lp - square), axis=1, keepdims=True) * (0.5 / (total * N))
    lik_ref[...] = jnp.broadcast_to(lik, (1, N))


VM = pl.BlockSpec(memory_space=pltpu.VMEM)
SM = pl.BlockSpec(memory_space=pltpu.SMEM)


def call(kernel, name, specs, shapes, scratch=(), flops=0, moved=0):
    return pl.pallas_call(
        kernel,
        out_shape=shapes,
        in_specs=specs,
        out_specs=jax.tree.map(lambda _: VM, shapes),
        scratch_shapes=list(scratch),
        compiler_params=pltpu.CompilerParams(vmem_limit_bytes=VMEM_LIMIT),
        cost_estimate=pl.CostEstimate(flops=flops, bytes_accessed=moved, transcendentals=0),
        name=name,
    )


def out(shape, dtype=F32):
    return jax.ShapeDtypeStruct(shape, dtype)


def shifted(a, axis, by):
    count = lax.axis_size(axis)
    return lax.ppermute(a, axis, [(i, (i + by) % count) for i in range(count)])


def swapped(a, *done):
    return shifted(lax.optimization_barrier((a, done))[0], "tm_2", 1)


RING = [(2 * i, (2 * i + 2) % 8) for i in range(4)] + [(2 * i + 1, (2 * i + 7) % 8) for i in range(4)]
SKIP = [(2, 6), (3, 7), (6, 2), (7, 3), (0, 1), (1, 0), (4, 5), (5, 4)]
FIRST = [(0, 4), (1, 7), (4, 0), (7, 1), (2, 3), (3, 2), (5, 6), (6, 5)]


def local(obs, present, sensors, log_prec, dynamics, prior_var, obs_map, init_state):
    lp, pv = log_prec.reshape(1, N), prior_var.reshape(1, N)
    both = (out((FULL, N)), out((PART, N)))
    square = out((N, N))
    square = out((N, N))
    eye = call(k_first, "k_first", [], square, (), 4 * 10**9, 10**7)()
    root, dyn_t, table, nodes, offs, step, twos, u, mask, obs_s, rows = call(
        k_block,
        "k_block",
        [SM] * 2 + [VM] * 7,
        (
            out((SEQ, N + 8, N)),
            square,
            out((16, N, 2 * N), BF16),
            out((42, N, 2 * N), BF16),
            out((96, N)),
            out((N, 6 * N), BF16),
            out((N, 8 * N), BF16),
            out((SUB, ROWS, N)),
            out((SUB, ROWS, N)),
            out((SUB, ROWS, N)),
            out((8, N)),
        ),
        [pltpu.VMEM((SEQ, STEPS, N), F32), pltpu.VMEM((SEQ, STEPS, N), F32)],
        10**9,
        10**6,
    )(present, sensors, eye, obs, present, lp, dynamics, pv, obs_map)
    mate = shifted(root, "tm_2", 1)
    chip, mine = call(k_core, "k_core", [VM] * 2, both, (), 10**7, 10**6)(root, mate)
    near = lax.ppermute(chip, ("tm_1", "tm_2"), RING)
    two = shifted(mine, "tm_1", 2)
    pre, preoff, u2, step_near, far, reach, cross, resid = call(
        k_tables,
        "k_tables",
        [VM, SM] + [VM] * 9,
        (
            out((ROWS, N, N)),
            out((ROWS, N)),
            out((SUB // 2, ROWS, N)),
            out((SUB, N, 2 * N), BF16),
            out((LEAVES, N, N)),
            out((len(REACH), N, 2 * N), BF16),
            out((11, N, 2 * N), BF16),
            out((SUB, N, 2 * N), BF16),
        ),
        (),
        4 * 10**9,
        10**7,
    )(chip, present, table, nodes, offs, step, u, mask, eye, dynamics, dyn_t)
    got = near, swapped(near, resid), two, swapped(two, resid)
    mine, state, ahead = call(
        k_total,
        "k_total",
        [VM] * 6,
        (out((PART, N)), out((8, N)), out((3, SEQ, N + 8, N))),
        [pltpu.VMEM((4, SEQ, N, N), F32), pltpu.VMEM((4, SEQ, 8, N), F32)],
        10**8,
        10**6,
    )(chip, *got, init_state)
    one = shifted(mine, "tm_0", 1)
    two = lax.ppermute(mine, ("tm_0", "tm_2"), SKIP)
    sent = lax.ppermute(state, ("tm_0", "tm_2"), FIRST)
    entry, entryoff = call(
        k_entry, "k_entry", [VM] * 3, (out((SEQ, N, N)), out((8, N))), (), 4 * 10**9, 10**7
    )(mine, ahead, mate)
    got = (
        one, swapped(one, entryoff, sent), two, swapped(two, entryoff, sent),
        sent, swapped(sent, entryoff),
    )
    send, near_sums, suffix, final = call(
        k_filter,
        "k_filter",
        [VM] * 22,
        (out((BLOCKS, 8, N)), out((SUB, ROWS, N)), out((ROWS, N)), out((8, N))),
        (),
        10**7,
        10**6,
    )(
        *got, entry, entryoff, init_state, obs_s, rows, dyn_t, pre, preoff, step, twos, u, u2,
        mask, reach, resid, cross,
    )
    got = lax.all_to_all(send, TM, 0, 0, tiled=True)
    smoothed, prec, lik = call(
        k_smooth,
        "k_smooth",
        [VM] * 8,
        (out((SEQ, STEPS, N)), out((1, N)), out((1, N))),
        (),
        10**7,
        10**6,
    )(got, near_sums, suffix, final, rows, far, step_near, cross)
    return smoothed, prec.reshape(N), lik[0, :1]


def solution(mesh):
    split = Mesh(
        mesh.devices.reshape(mesh.shape["cluster"], 4, 4, 2), ("cluster", "tm_0", "tm_1", "tm_2")
    )
    return jax.shard_map(
        local,
        mesh=split,
        in_specs=(
            P("cluster", TM, None),
            P("cluster", TM),
            P("cluster"),
            P("cluster"),
            P("cluster", None),
            P("cluster"),
            P("cluster", None),
            P("cluster", None),
        ),
        out_specs=(P("cluster", TM, None), P("cluster"), P("cluster")),
        check_vma=False,
    )
```

```python
import jax
import jax.numpy as jnp
from jax import lax
from jax.experimental import pallas as pl
from jax.experimental.pallas import tpu as pltpu
from jax.sharding import Mesh
from jax.sharding import PartitionSpec as P

F32, BF16 = jnp.float32, jnp.bfloat16
TM = ("tm_0", "tm_1", "tm_2")
N = 128
SEQ, STEPS, SUB = 3, 64, 4
LEAVES = STEPS // SUB
ROWS = SEQ * LEAVES
HALF = N // 2
BLOCKS = 32
VMEM_LIMIT = 40 * 1024 * 1024


def dot(a, b):
    return lax.dot(a, b, preferred_element_type=F32)


def lanes(*parts):
    return jnp.concatenate(parts, axis=1)


def stacked(*parts):
    return jnp.concatenate(parts, axis=0)


def split2(a):
    hi = a.astype(BF16)
    return hi, (a - hi.astype(F32)).astype(BF16)


def split3(a):
    hi = a.astype(BF16)
    rest = a - hi.astype(F32)
    mid = rest.astype(BF16)
    return hi, mid, (rest - mid.astype(F32)).astype(BF16)


def pair(a):
    return lanes(*split2(a))


def whole(x):
    n = x.shape[1] // 2
    return x[:, :n].astype(F32) + x[:, n:].astype(F32)


def mul_pair(x, y):
    d = dot(x, stacked(y, y))
    n = y.shape[1] // 2
    return d[:, :n] + d[:, n:]


def mul_exact(a, b):
    a0, a1, a2 = split3(a)
    b0, b1, b2 = split3(b)
    n = b.shape[1]
    y = lanes(b0, b1)
    d = dot(lanes(a0, a1), stacked(y, y))
    return d[:, :n] + (d[:, n:] + dot(lanes(a0, a2), stacked(b2, b0)))


def apply_row(row, matrix):
    column = jnp.transpose(jnp.broadcast_to(row, (N, N)))
    return jnp.sum(column * matrix, axis=0, keepdims=True)


def step_major(ref, i):
    return stacked(*(ref[b, pl.ds(i, LEAVES, stride=SUB), :] for b in range(SEQ)))


def pick(flag, a, b):
    return jnp.where(flag, a, b)


def on_row(sensors_ref):
    return (lax.broadcasted_iota(jnp.int32, (1, N), 1) < sensors_ref[0]).astype(F32)


def identity(rows=N):
    shape = (rows, N)
    return (
        lax.broadcasted_iota(jnp.int32, shape, 0) == lax.broadcasted_iota(jnp.int32, shape, 1)
    ).astype(F32)


def leaf_number(flags, b, j):
    at = 0
    for i in range(SUB):
        at = at * 2 + flags[b, SUB * j + i]
    return at


def joined(left, left_off, right, right_off):
    off = pair(jnp.broadcast_to(left_off, (16, N)))
    got = mul_pair(stacked(left, off), right)
    return got[:N], got[N : N + 1] + right_off


REACH = (1, 2, 3, 4, 8, 12)
LEVELS = ((0, 24), (24, 12), (36, 6))
OFFS = (0, 48, 72, 84)
PART = SEQ * HALF + 8
FULL = SEQ * N + 8


def k_first(eye_ref):
    eye_ref[...] = identity()


def k_block(
    flags, sensors_ref, eye_ref, obs_raw, pres_ref, lp_ref, dyn_ref, pv_ref, map_ref,
    root_ref, dynt_ref, table, nodes, offs, step_ref, twos_ref, u_ref, mask_ref, obs_ref, rows_ref, mask_scr, u_scr,
):
    on = on_row(sensors_ref)
    weight = jnp.exp(lp_ref[...]) * on
    pv, obs_map = pv_ref[...], map_ref[...]
    dyn_t = jnp.transpose(dyn_ref[...])
    dynt_ref[...] = dyn_t
    y = pair(obs_map)
    out_t = mul_pair(pair(dyn_t), pair(jnp.transpose(obs_map)))
    filt_t = dyn_t - mul_pair(pair(out_t * weight), y) * pv
    rows_ref[...] = stacked(on, weight, lp_ref[...], jnp.zeros((5, N), F32))
    step_ref[...] = pair(lanes(dyn_t, filt_t, out_t))
    seen = pres_ref[...].astype(F32)
    seen = jnp.transpose(stacked(seen, jnp.zeros((8 - SEQ, STEPS), F32)))
    for b in range(SEQ):
        mask = jnp.broadcast_to(seen[:, b : b + 1], (STEPS, N))
        mask_scr[b] = mask
        u_scr[b] = mul_pair(pair(obs_raw[b] * weight), y) * pv * mask
    for i in range(SUB):
        u_ref[i] = step_major(u_scr, i)
        mask_ref[i] = step_major(mask_scr, i)
        obs_ref[i] = step_major(obs_raw, i)
    two = mul_exact(stacked(dyn_t, filt_t), lanes(dyn_t, filt_t))
    twos = [two[i * N : (i + 1) * N, j * N : (j + 1) * N] for i in (0, 1) for j in (0, 1)]
    wide = lanes(*twos)
    twos_ref[...] = pair(wide)
    for i in range(4):
        four = mul_exact(twos[i], wide)
        for j in range(4):
            table[4 * i + j] = pair(four[:, j * N : (j + 1) * N])
    y = pair(lanes(dyn_t, filt_t))
    z = u_ref[0]
    for i in range(1, SUB):
        d = mul_pair(pair(z), y)
        z = pick(mask_ref[i] > 0.5, d[:, N:], d[:, :N]) + u_ref[i]
    offs[0:ROWS, :] = z

    def leaf(k):
        return table[leaf_number(flags, k // LEAVES, k % LEAVES)]

    get = leaf
    for level in range(4):
        count = ROWS >> (level + 1)
        for k in range(count):
            at = OFFS[level] + 2 * k
            matrix, off = joined(
                get(2 * k), offs[at : at + 1, :], get(2 * k + 1), offs[at + 1 : at + 2, :]
            )
            if level == 3:
                root_ref[k, 0:N, :] = matrix
                root_ref[k, N : N + 8, :] = jnp.broadcast_to(off, (8, N))
            else:
                nodes[LEVELS[level][0] + k] = pair(matrix)
                to = OFFS[level + 1] + k
                offs[to : to + 1, :] = off
        if level < 3:
            get = lambda k, level=level: nodes[LEVELS[level][0] + k]


def put(ref, b, matrix):
    rows = matrix.shape[0]
    ref[b * rows : (b + 1) * rows, :] = matrix


def put_offsets(ref, offs):
    rows = ref.shape[0]
    ref[rows - 8 : rows, :] = stacked(*offs, jnp.zeros((8 - SEQ, N), F32))


def offset_of(ref, b):
    at = ref.shape[0] - 8 + b
    return ref[at : at + 1, :]


def half_of(ref, b):
    return ref[b * HALF : (b + 1) * HALF, :]


def full_of(ref, b):
    return ref[b * N : (b + 1) * N, :]


def in_order(mine_ref, mate_ref, b):
    first = lax.axis_index("tm_2") == 0
    mine, mate = half_of(mine_ref, b), half_of(mate_ref, b)
    matrix = stacked(pick(first, mine, mate), pick(first, mate, mine))
    return matrix, offset_of(mine_ref, b)


def chosen(flag, p_ref, q_ref, b):
    return (
        pick(flag, full_of(p_ref, b), full_of(q_ref, b)),
        pick(flag, offset_of(p_ref, b), offset_of(q_ref, b)),
    )


def then(p, q):
    return joined(pair(p[0]), p[1], pair(q[0]), q[1])


def put_all(ref, maps):
    for b, (matrix, _) in enumerate(maps):
        put(ref, b, matrix)
    put_offsets(ref, [off for _, off in maps])


def put_halves(ref, maps):
    first = lax.axis_index("tm_2") == 0
    put_all(ref, [(pick(first, m[:HALF], m[HALF:]), off) for m, off in maps])


def k_core(own_ref, mate_ref, out_ref, mine_ref):
    first = lax.axis_index("tm_2") == 0
    maps = []
    for b in range(SEQ):
        own, mate = own_ref[b], mate_ref[b]
        p, q = pick(first, own, mate), pick(first, mate, own)
        maps.append(then((p[:N], p[N : N + 1]), (q[:N], q[N : N + 1])))
    put_all(out_ref, maps)
    put_halves(mine_ref, maps)


def k_total(
    own_ref, near, near_mate, two, two_mate, init_ref, mine_ref, state_ref, ahead_ref, maps, offs
):
    me, first = lax.axis_index("tm_1"), lax.axis_index("tm_2") == 0
    state_ref[...] = jnp.zeros_like(state_ref)
    for b in range(SEQ):
        ring = (
            chosen(first, near, near_mate, b),
            in_order(two, two_mate, b),
            chosen(first, near_mate, near, b),
        )
        for d, (matrix, off) in enumerate(ring):
            slot = lax.rem(me + 3 - d, 4)
            off = jnp.broadcast_to(off, (8, N))
            maps[slot, b] = matrix
            offs[slot, b] = off
            ahead_ref[d, b, 0:N, :] = matrix
            ahead_ref[d, b, N : N + 8, :] = off
        maps[me, b] = full_of(own_ref, b)
        offs[me, b] = jnp.broadcast_to(offset_of(own_ref, b), (8, N))
    ends = []
    for b in range(SEQ):
        p = [(maps[k, b], offs[k, b, 0:1, :]) for k in range(4)]
        ends.append(then(then(p[0], p[1]), then(p[2], p[3])))
        state_ref[b : b + 1, :] = apply_row(init_ref[b : b + 1, :], ends[b][0]) + ends[b][1]
    put_halves(mine_ref, ends)


def k_prefix(flags, table, nodes, offs, step_ref, u_ref, mask_ref, pre_ref, preoff_ref, u2_ref):
    y = lanes(step_ref[:, 0 : 2 * N], step_ref[:, 3 * N : 5 * N])
    for i in range(SUB // 2):
        d = mul_pair(pair(u_ref[2 * i]), y)
        u2_ref[i] = pick(mask_ref[2 * i + 1] > 0.5, d[:, N:], d[:, :N]) + u_ref[2 * i + 1]
    preoff_ref[...] = jnp.zeros_like(preoff_ref)
    for b in range(SEQ):
        pre_ref[b * LEAVES] = jnp.zeros((N, N), F32)
        for level in (3, 2, 1, 0):
            parents = 8 >> level
            span = LEAVES // parents
            for k in range(parents):
                at = b * LEAVES + k * span
                left = b * 2 * parents + 2 * k
                off = offs[OFFS[level] + left : OFFS[level] + left + 1, :]
                if level == 0:
                    got = table[leaf_number(flags, left // LEAVES, left % LEAVES)]
                else:
                    got = nodes[LEVELS[level - 1][0] + left]
                if k == 0:
                    matrix = whole(got)
                else:
                    matrix, off = joined(
                        pair(pre_ref[at]), preoff_ref[at : at + 1, :], got, off
                    )
                to = at + span // 2
                pre_ref[to] = matrix
                preoff_ref[to : to + 1, :] = off


def k_powers(
    eye_ref, dyn_ref, dynt_ref, near_ref, far_ref, reach_ref, cross_ref, resid_ref
):
    eye, dyn = eye_ref[...], dyn_ref[...]
    d2 = mul_exact(dyn, dyn)
    d34 = mul_exact(d2, lanes(dyn, d2))
    d3, d4 = d34[:, :N], d34[:, N:]
    for i, a in enumerate((dyn, d2, d3, d4)):
        near_ref[i] = pair(a)
    resid = eye - mul_exact(dynt_ref[...], dyn)
    resid_ref[0] = pair(resid)
    more = mul_exact(resid, lanes(dyn, d2, d3))
    for i in range(3):
        resid_ref[i + 1] = pair(more[:, i * N : (i + 1) * N])
    far_ref[0] = eye
    far_ref[1] = d4
    for have in (1, 2, 4, 8):
        last = far_ref[have]
        for k in range(1, have + 1):
            got = mul_exact(last, far_ref[k])
            if have + k < LEAVES:
                far_ref[have + k] = got
    for i, k in enumerate(REACH):
        reach_ref[i] = pair(far_ref[k])
    cross_ref[0] = pair(eye)
    powers = [None, got]
    for k in range(2, 9):
        powers.append(mul_exact(powers[k // 2], powers[k - k // 2]))
    for k in range(1, 8):
        cross_ref[k] = pair(powers[k])
    w16 = mul_exact(powers[8], powers[8])
    cross_ref[8] = pair(powers[8])
    cross_ref[9] = pair(w16)
    cross_ref[10] = pair(mul_exact(w16, powers[8]))


def k_entry(after_ref, ahead_ref, mate_ref, entry_ref, entryoff_ref):
    me, second = lax.axis_index("tm_1"), lax.axis_index("tm_2") == 1
    entryoff_ref[...] = jnp.zeros_like(entryoff_ref)
    for b in range(SEQ):
        so_far = (identity(), jnp.zeros((1, N), F32))
        for source, flag in (
            (ahead_ref.at[2], me >= 3), (ahead_ref.at[1], me >= 2), (ahead_ref.at[0], me >= 1),
            (mate_ref, second),
        ):
            got = then(so_far, (source[b, 0:N, :], source[b, N : N + 1, :]))
            so_far = (pick(flag, got[0], so_far[0]), pick(flag, got[1], so_far[1]))
        entry_ref[b] = so_far[0]
        entryoff_ref[b : b + 1, :] = so_far[1]


def k_tables(
    after_ref, flags, table, nodes, offs, step_ref, u_ref, mask_ref, eye_ref, dyn_ref, dynt_ref,
    pre_ref, preoff_ref, u2_ref, near_ref, far_ref, reach_ref, cross_ref, resid_ref,
):
    k_prefix(flags, table, nodes, offs, step_ref, u_ref, mask_ref, pre_ref, preoff_ref, u2_ref)
    k_powers(eye_ref, dyn_ref, dynt_ref, near_ref, far_ref, reach_ref, cross_ref, resid_ref)


def k_filter(
    one, one_mate, two, two_mate, sent, sent_mate, entry_ref, entryoff_ref, init_ref, obs_ref,
    rows_ref, dynt_ref, pre_ref, preoff_ref, step_ref, twos_ref, u_ref, u2_ref, mask_ref, reach_ref,
    resid_ref, cross_ref, send_ref, local_ref, suffix_ref, final_ref,
):
    group, core = lax.axis_index("tm_0"), lax.axis_index("tm_2")
    direct = ((group == 2) & (core == 0)) | ((group == 3) & (core == 1))
    last = (group == 3) & (lax.axis_index("tm_1") == 3) & (lax.axis_index("tm_2") == 1)
    starts = []
    for b in range(SEQ):
        row = pick(direct, sent[b : b + 1, :], sent_mate[b : b + 1, :])
        row = pick(group >= 2, row, init_ref[b : b + 1, :])
        for flag, mine, mate in ((group == 3, two, two_mate), (group >= 1, one, one_mate)):
            matrix, off = in_order(mine, mate, b)
            row = pick(flag, apply_row(row, matrix) + off, row)
        starts.append(apply_row(row, entry_ref[b]) + entryoff_ref[b : b + 1, :])
    rows = []
    for b in range(SEQ):
        column = jnp.transpose(jnp.broadcast_to(starts[b], (N, N)))
        rows.append(starts[b])
        for j in range(1, LEAVES):
            k = b * LEAVES + j
            rows.append(
                jnp.sum(column * pre_ref[k], axis=0, keepdims=True) + preoff_ref[k : k + 1, :]
            )
    state = stacked(*rows)
    weight = rows_ref[1:2, :]
    step = step_ref[...]
    square = jnp.zeros((ROWS, N), F32)
    seen = jnp.zeros((ROWS, N), F32)
    sums = [None] * SUB
    out_pair = lanes(step[:, 2 * N : 3 * N], step[:, 5 * N : 6 * N])
    for i in range(0, SUB, 2):
        x = pair(state)
        d = mul_pair(x, step)
        q = mul_pair(x, twos_ref[...])
        m1, m2 = mask_ref[i], mask_ref[i + 1]
        on1, on2 = m1 > 0.5, m2 > 0.5
        middle = pick(on1, d[:, N : 2 * N], d[:, :N]) + u_ref[i]
        state = u2_ref[i // 2] + pick(
            on1,
            pick(on2, q[:, 3 * N :], q[:, 2 * N : 3 * N]),
            pick(on2, q[:, N : 2 * N], q[:, :N]),
        )
        x1 = pair(middle)
        e1 = obs_ref[i] - d[:, 2 * N :]
        e2 = obs_ref[i + 1] - mul_pair(x1, out_pair)
        square = square + m1 * (e1 * e1) + m2 * (e2 * e2)
        seen = seen + m1 + m2
        for j, x in ((i, x1), (i + 1, pair(state))):
            for k in range(j + 1):
                add = mul_pair(x, resid_ref[j - k])
                sums[k] = add if k == j else sums[k] + add
    square = jnp.sum(square, axis=0, keepdims=True) * weight
    seen = jnp.sum(seen, axis=0, keepdims=True)
    ends = stacked(*(state[(b + 1) * LEAVES - 1 : (b + 1) * LEAVES, :] for b in range(SEQ)))
    ends = stacked(ends, jnp.zeros((8 - SEQ, N), F32))
    final = mul_pair(pair(ends), pair(dynt_ref[...]))
    final_ref[...] = final
    place = lax.broadcasted_iota(jnp.int32, (ROWS, N), 0) % LEAVES
    run = sums[0]
    for first in (0, 3):
        total = run
        for k in range(first, first + 3):
            moved = pltpu.roll(mul_pair(pair(run), reach_ref[k]), ROWS - REACH[k], 0)
            total = total + pick(place < LEAVES - REACH[k], moved, 0.0)
        run = total
    for i in range(SUB):
        local_ref[i] = sums[i]
    suffix_ref[...] = run
    offsets = stacked(*(run[b * LEAVES : b * LEAVES + 1, :] for b in range(SEQ)))
    offsets = stacked(offsets, jnp.zeros((8 - SEQ, N), F32))
    through = mul_pair(pair(final), cross_ref[1])
    offsets = offsets + pick(last, through, 0.0)
    packed = stacked(offsets[:SEQ], square, seen, jnp.zeros((8 - SEQ - 2, N), F32))
    send_ref[...] = jnp.broadcast_to(packed[None], (BLOCKS, 8, N))


def k_smooth(
    got_ref, local_ref, suffix_ref, final_ref, rows_ref, far_ref, near_ref, cross_ref,
    out_ref, prec_ref, lik_ref,
):
    me = (lax.axis_index("tm_0") * 4 + lax.axis_index("tm_1")) * 2 + lax.axis_index("tm_2")
    on, lp = rows_ref[0:1, :], rows_ref[2:3, :]
    acc = jnp.zeros((4 * 8, N), F32)
    for h in range(8):
        parts = []
        for g in range(4):
            at = me + 1 + 8 * g + h
            parts.append(pick(at < BLOCKS, got_ref[jnp.minimum(at, BLOCKS - 1)], 0.0))
        acc = acc + mul_pair(pair(stacked(*parts)), cross_ref[h])
    leaving = acc[0:8]
    for g in range(1, 4):
        leaving = leaving + mul_pair(pair(acc[8 * g : 8 * g + 8]), cross_ref[7 + g])
    leaving = pick(me == BLOCKS - 1, final_ref[...], leaving)
    rows = []
    for b in range(SEQ):
        column = jnp.transpose(jnp.broadcast_to(leaving[b : b + 1, :], (N, N)))
        for j in range(LEAVES - 1):
            k = b * LEAVES + j
            rows.append(
                jnp.sum(column * far_ref[LEAVES - 1 - j], axis=0, keepdims=True)
                + suffix_ref[k + 1 : k + 2, :]
            )
        rows.append(leaving[b : b + 1, :])
    x = pair(stacked(*rows))
    for i in range(SUB):
        got = mul_pair(x, near_ref[SUB - 1 - i]) + local_ref[i]
        for b in range(SEQ):
            out_ref[b, pl.ds(i, LEAVES, stride=SUB), :] = got[b * LEAVES : (b + 1) * LEAVES]
    both = jnp.sum(got_ref[...], axis=0)
    square, seen = both[SEQ : SEQ + 1], both[SEQ + 1 : SEQ + 2]
    total = float(SEQ * STEPS * BLOCKS)
    prec_ref[...] = lp + (0.5 / total) * on * (seen - square)
    lik = jnp.sum(on * (seen * lp - square), axis=1, keepdims=True) * (0.5 / (total * N))
    lik_ref[...] = jnp.broadcast_to(lik, (1, N))


VM = pl.BlockSpec(memory_space=pltpu.VMEM)
SM = pl.BlockSpec(memory_space=pltpu.SMEM)


def call(kernel, name, specs, shapes, scratch=(), flops=0, moved=0):
    return pl.pallas_call(
        kernel,
        out_shape=shapes,
        in_specs=specs,
        out_specs=jax.tree.map(lambda _: VM, shapes),
        scratch_shapes=list(scratch),
        compiler_params=pltpu.CompilerParams(vmem_limit_bytes=VMEM_LIMIT),
        cost_estimate=pl.CostEstimate(flops=flops, bytes_accessed=moved, transcendentals=0),
        name=name,
    )


def out(shape, dtype=F32):
    return jax.ShapeDtypeStruct(shape, dtype)


def shifted(a, axis, by):
    count = lax.axis_size(axis)
    return lax.ppermute(a, axis, [(i, (i + by) % count) for i in range(count)])


def swapped(a, *done):
    return shifted(lax.optimization_barrier((a, done))[0], "tm_2", 1)


RING = [(2 * i, (2 * i + 2) % 8) for i in range(4)] + [(2 * i + 1, (2 * i + 7) % 8) for i in range(4)]
SKIP = [(2, 6), (3, 7), (6, 2), (7, 3), (0, 1), (1, 0), (4, 5), (5, 4)]
FIRST = [(0, 4), (1, 7), (4, 0), (7, 1), (2, 3), (3, 2), (5, 6), (6, 5)]


def local(obs, present, sensors, log_prec, dynamics, prior_var, obs_map, init_state):
    lp, pv = log_prec.reshape(1, N), prior_var.reshape(1, N)
    both = (out((FULL, N)), out((PART, N)))
    square = out((N, N))
    square = out((N, N))
    eye = call(k_first, "k_first", [], square, (), 4 * 10**9, 10**7)()
    root, dyn_t, table, nodes, offs, step, twos, u, mask, obs_s, rows = call(
        k_block,
        "k_block",
        [SM] * 2 + [VM] * 7,
        (
            out((SEQ, N + 8, N)),
            square,
            out((16, N, 2 * N), BF16),
            out((42, N, 2 * N), BF16),
            out((96, N)),
            out((N, 6 * N), BF16),
            out((N, 8 * N), BF16),
            out((SUB, ROWS, N)),
            out((SUB, ROWS, N)),
            out((SUB, ROWS, N)),
            out((8, N)),
        ),
        [pltpu.VMEM((SEQ, STEPS, N), F32), pltpu.VMEM((SEQ, STEPS, N), F32)],
        10**9,
        10**6,
    )(present, sensors, eye, obs, present, lp, dynamics, pv, obs_map)
    mate = shifted(root, "tm_2", 1)
    chip, mine = call(k_core, "k_core", [VM] * 2, both, (), 10**7, 10**6)(root, mate)
    near = lax.ppermute(chip, ("tm_1", "tm_2"), RING)
    two = shifted(mine, "tm_1", 2)
    pre, preoff, u2, step_near, far, reach, cross, resid = call(
        k_tables,
        "k_tables",
        [VM, SM] + [VM] * 9,
        (
            out((ROWS, N, N)),
            out((ROWS, N)),
            out((SUB // 2, ROWS, N)),
            out((SUB, N, 2 * N), BF16),
            out((LEAVES, N, N)),
            out((len(REACH), N, 2 * N), BF16),
            out((11, N, 2 * N), BF16),
            out((SUB, N, 2 * N), BF16),
        ),
        (),
        4 * 10**9,
        10**7,
    )(chip, present, table, nodes, offs, step, u, mask, eye, dynamics, dyn_t)
    got = near, swapped(near, resid), two, swapped(two, resid)
    mine, state, ahead = call(
        k_total,
        "k_total",
        [VM] * 6,
        (out((PART, N)), out((8, N)), out((3, SEQ, N + 8, N))),
        [pltpu.VMEM((4, SEQ, N, N), F32), pltpu.VMEM((4, SEQ, 8, N), F32)],
        10**8,
        10**6,
    )(chip, *got, init_state)
    one = shifted(mine, "tm_0", 1)
    two = lax.ppermute(mine, ("tm_0", "tm_2"), SKIP)
    sent = lax.ppermute(state, ("tm_0", "tm_2"), FIRST)
    entry, entryoff = call(
        k_entry, "k_entry", [VM] * 3, (out((SEQ, N, N)), out((8, N))), (), 4 * 10**9, 10**7
    )(mine, ahead, mate)
    got = (
        one, swapped(one, entryoff, sent), two, swapped(two, entryoff),
        sent, swapped(sent, entryoff),
    )
    send, near_sums, suffix, final = call(
        k_filter,
        "k_filter",
        [VM] * 22,
        (out((BLOCKS, 8, N)), out((SUB, ROWS, N)), out((ROWS, N)), out((8, N))),
        (),
        10**7,
        10**6,
    )(
        *got, entry, entryoff, init_state, obs_s, rows, dyn_t, pre, preoff, step, twos, u, u2,
        mask, reach, resid, cross,
    )
    got = lax.all_to_all(send, TM, 0, 0, tiled=True)
    smoothed, prec, lik = call(
        k_smooth,
        "k_smooth",
        [VM] * 8,
        (out((SEQ, STEPS, N)), out((1, N)), out((1, N))),
        (),
        10**7,
        10**6,
    )(got, near_sums, suffix, final, rows, far, step_near, cross)
    return smoothed, prec.reshape(N), lik[0, :1]


def solution(mesh):
    split = Mesh(
        mesh.devices.reshape(mesh.shape["cluster"], 4, 4, 2), ("cluster", "tm_0", "tm_1", "tm_2")
    )
    return jax.shard_map(
        local,
        mesh=split,
        in_specs=(
            P("cluster", TM, None),
            P("cluster", TM),
            P("cluster"),
            P("cluster"),
            P("cluster", None),
            P("cluster"),
            P("cluster", None),
            P("cluster", None),
        ),
        out_specs=(P("cluster", TM, None), P("cluster"), P("cluster")),
        check_vma=False,
    )
```

```python
import jax
import jax.numpy as jnp
from jax import lax
from jax.experimental import pallas as pl
from jax.experimental.pallas import tpu as pltpu
from jax.sharding import Mesh
from jax.sharding import PartitionSpec as P

F32, BF16 = jnp.float32, jnp.bfloat16
TM = ("tm_0", "tm_1", "tm_2")
N = 128
SEQ, STEPS, SUB = 3, 64, 4
LEAVES = STEPS // SUB
ROWS = SEQ * LEAVES
HALF = N // 2
BLOCKS = 32
VMEM_LIMIT = 40 * 1024 * 1024


def dot(a, b):
    return lax.dot(a, b, preferred_element_type=F32)


def lanes(*parts):
    return jnp.concatenate(parts, axis=1)


def stacked(*parts):
    return jnp.concatenate(parts, axis=0)


def split2(a):
    hi = a.astype(BF16)
    return hi, (a - hi.astype(F32)).astype(BF16)


def split3(a):
    hi = a.astype(BF16)
    rest = a - hi.astype(F32)
    mid = rest.astype(BF16)
    return hi, mid, (rest - mid.astype(F32)).astype(BF16)


def pair(a):
    return lanes(*split2(a))


def whole(x):
    n = x.shape[1] // 2
    return x[:, :n].astype(F32) + x[:, n:].astype(F32)


def mul_pair(x, y):
    d = dot(x, stacked(y, y))
    n = y.shape[1] // 2
    return d[:, :n] + d[:, n:]


def mul_exact(a, b):
    a0, a1, a2 = split3(a)
    b0, b1, b2 = split3(b)
    n = b.shape[1]
    y = lanes(b0, b1)
    d = dot(lanes(a0, a1), stacked(y, y))
    return d[:, :n] + (d[:, n:] + dot(lanes(a0, a2), stacked(b2, b0)))


def apply_row(row, matrix):
    column = jnp.transpose(jnp.broadcast_to(row, (N, N)))
    return jnp.sum(column * matrix, axis=0, keepdims=True)


def step_major(ref, i):
    return stacked(*(ref[b, pl.ds(i, LEAVES, stride=SUB), :] for b in range(SEQ)))


def pick(flag, a, b):
    return jnp.where(flag, a, b)


def on_row(sensors_ref):
    return (lax.broadcasted_iota(jnp.int32, (1, N), 1) < sensors_ref[0]).astype(F32)


def identity(rows=N):
    shape = (rows, N)
    return (
        lax.broadcasted_iota(jnp.int32, shape, 0) == lax.broadcasted_iota(jnp.int32, shape, 1)
    ).astype(F32)


def leaf_number(flags, b, j):
    at = 0
    for i in range(SUB):
        at = at * 2 + flags[b, SUB * j + i]
    return at


def joined(left, left_off, right, right_off):
    off = pair(jnp.broadcast_to(left_off, (16, N)))
    got = mul_pair(stacked(left, off), right)
    return got[:N], got[N : N + 1] + right_off


REACH = (1, 2, 3, 4, 8, 12)
LEVELS = ((0, 24), (24, 12), (36, 6))
OFFS = (0, 48, 72, 84)
PART = SEQ * HALF + 8
FULL = SEQ * N + 8


def k_first(eye_ref):
    eye_ref[...] = identity()


def k_block(
    flags, sensors_ref, eye_ref, obs_raw, pres_ref, lp_ref, dyn_ref, pv_ref, map_ref,
    root_ref, dynt_ref, table, nodes, offs, step_ref, twos_ref, u_ref, mask_ref, obs_ref, rows_ref, mask_scr, u_scr,
):
    on = on_row(sensors_ref)
    weight = jnp.exp(lp_ref[...]) * on
    pv, obs_map = pv_ref[...], map_ref[...]
    dyn_t = jnp.transpose(dyn_ref[...])
    dynt_ref[...] = dyn_t
    y = pair(obs_map)
    out_t = mul_pair(pair(dyn_t), pair(jnp.transpose(obs_map)))
    filt_t = dyn_t - mul_pair(pair(out_t * weight), y) * pv
    rows_ref[...] = stacked(on, weight, lp_ref[...], jnp.zeros((5, N), F32))
    step_ref[...] = pair(lanes(dyn_t, filt_t, out_t))
    seen = pres_ref[...].astype(F32)
    seen = jnp.transpose(stacked(seen, jnp.zeros((8 - SEQ, STEPS), F32)))
    for b in range(SEQ):
        mask = jnp.broadcast_to(seen[:, b : b + 1], (STEPS, N))
        mask_scr[b] = mask
        u_scr[b] = mul_pair(pair(obs_raw[b] * weight), y) * pv * mask
    for i in range(SUB):
        u_ref[i] = step_major(u_scr, i)
        mask_ref[i] = step_major(mask_scr, i)
        obs_ref[i] = step_major(obs_raw, i)
    two = mul_exact(stacked(dyn_t, filt_t), lanes(dyn_t, filt_t))
    twos = [two[i * N : (i + 1) * N, j * N : (j + 1) * N] for i in (0, 1) for j in (0, 1)]
    wide = lanes(*twos)
    twos_ref[...] = pair(wide)
    for i in range(4):
        four = mul_exact(twos[i], wide)
        for j in range(4):
            table[4 * i + j] = pair(four[:, j * N : (j + 1) * N])
    y = pair(lanes(dyn_t, filt_t))
    z = u_ref[0]
    for i in range(1, SUB):
        d = mul_pair(pair(z), y)
        z = pick(mask_ref[i] > 0.5, d[:, N:], d[:, :N]) + u_ref[i]
    offs[0:ROWS, :] = z

    def leaf(k):
        return table[leaf_number(flags, k // LEAVES, k % LEAVES)]

    get = leaf
    for level in range(4):
        count = ROWS >> (level + 1)
        for k in range(count):
            at = OFFS[level] + 2 * k
            matrix, off = joined(
                get(2 * k), offs[at : at + 1, :], get(2 * k + 1), offs[at + 1 : at + 2, :]
            )
            if level == 3:
                root_ref[k, 0:N, :] = matrix
                root_ref[k, N : N + 8, :] = jnp.broadcast_to(off, (8, N))
            else:
                nodes[LEVELS[level][0] + k] = pair(matrix)
                to = OFFS[level + 1] + k
                offs[to : to + 1, :] = off
        if level < 3:
            get = lambda k, level=level: nodes[LEVELS[level][0] + k]


def put(ref, b, matrix):
    rows = matrix.shape[0]
    ref[b * rows : (b + 1) * rows, :] = matrix


def put_offsets(ref, offs):
    rows = ref.shape[0]
    ref[rows - 8 : rows, :] = stacked(*offs, jnp.zeros((8 - SEQ, N), F32))


def offset_of(ref, b):
    at = ref.shape[0] - 8 + b
    return ref[at : at + 1, :]


def half_of(ref, b):
    return ref[b * HALF : (b + 1) * HALF, :]


def full_of(ref, b):
    return ref[b * N : (b + 1) * N, :]


def in_order(mine_ref, mate_ref, b):
    first = lax.axis_index("tm_2") == 0
    mine, mate = half_of(mine_ref, b), half_of(mate_ref, b)
    matrix = stacked(pick(first, mine, mate), pick(first, mate, mine))
    return matrix, offset_of(mine_ref, b)


def chosen(flag, p_ref, q_ref, b):
    return (
        pick(flag, full_of(p_ref, b), full_of(q_ref, b)),
        pick(flag, offset_of(p_ref, b), offset_of(q_ref, b)),
    )


def around(refs, b):
    near, near_mate, two, two_mate = refs
    first = lax.axis_index("tm_2") == 0
    return (
        chosen(first, near, near_mate, b),
        in_order(two, two_mate, b),
        chosen(first, near_mate, near, b),
    )


def then(p, q):
    return joined(pair(p[0]), p[1], pair(q[0]), q[1])


def put_all(ref, maps):
    for b, (matrix, _) in enumerate(maps):
        put(ref, b, matrix)
    put_offsets(ref, [off for _, off in maps])


def put_halves(ref, maps):
    first = lax.axis_index("tm_2") == 0
    put_all(ref, [(pick(first, m[:HALF], m[HALF:]), off) for m, off in maps])


def k_core(own_ref, mate_ref, out_ref, mine_ref):
    first = lax.axis_index("tm_2") == 0
    maps = []
    for b in range(SEQ):
        own, mate = own_ref[b], mate_ref[b]
        p, q = pick(first, own, mate), pick(first, mate, own)
        maps.append(then((p[:N], p[N : N + 1]), (q[:N], q[N : N + 1])))
    put_all(out_ref, maps)
    put_halves(mine_ref, maps)


def k_total(
    own_ref, near, near_mate, two, two_mate, init_ref, mine_ref, state_ref, maps, offs
):
    me = lax.axis_index("tm_1")
    state_ref[...] = jnp.zeros_like(state_ref)
    for b in range(SEQ):
        for d, (matrix, off) in enumerate(around((near, near_mate, two, two_mate), b)):
            slot = lax.rem(me + 3 - d, 4)
            off = jnp.broadcast_to(off, (8, N))
            maps[slot, b] = matrix
            offs[slot, b] = off
        maps[me, b] = full_of(own_ref, b)
        offs[me, b] = jnp.broadcast_to(offset_of(own_ref, b), (8, N))
    ends = []
    for b in range(SEQ):
        p = [(maps[k, b], offs[k, b, 0:1, :]) for k in range(4)]
        ends.append(then(then(p[0], p[1]), then(p[2], p[3])))
        state_ref[b : b + 1, :] = apply_row(init_ref[b : b + 1, :], ends[b][0]) + ends[b][1]
    put_halves(mine_ref, ends)


def k_prefix(flags, table, nodes, offs, step_ref, u_ref, mask_ref, pre_ref, preoff_ref, u2_ref):
    y = lanes(step_ref[:, 0 : 2 * N], step_ref[:, 3 * N : 5 * N])
    for i in range(SUB // 2):
        d = mul_pair(pair(u_ref[2 * i]), y)
        u2_ref[i] = pick(mask_ref[2 * i + 1] > 0.5, d[:, N:], d[:, :N]) + u_ref[2 * i + 1]
    preoff_ref[...] = jnp.zeros_like(preoff_ref)
    for b in range(SEQ):
        pre_ref[b * LEAVES] = jnp.zeros((N, N), F32)
        for level in (3, 2, 1, 0):
            parents = 8 >> level
            span = LEAVES // parents
            for k in range(parents):
                at = b * LEAVES + k * span
                left = b * 2 * parents + 2 * k
                off = offs[OFFS[level] + left : OFFS[level] + left + 1, :]
                if level == 0:
                    got = table[leaf_number(flags, left // LEAVES, left % LEAVES)]
                else:
                    got = nodes[LEVELS[level - 1][0] + left]
                if k == 0:
                    matrix = whole(got)
                else:
                    matrix, off = joined(
                        pair(pre_ref[at]), preoff_ref[at : at + 1, :], got, off
                    )
                to = at + span // 2
                pre_ref[to] = matrix
                preoff_ref[to : to + 1, :] = off


def k_powers(
    eye_ref, dyn_ref, dynt_ref, near_ref, far_ref, reach_ref, cross_ref, resid_ref
):
    eye, dyn = eye_ref[...], dyn_ref[...]
    d2 = mul_exact(dyn, dyn)
    d34 = mul_exact(d2, lanes(dyn, d2))
    d3, d4 = d34[:, :N], d34[:, N:]
    for i, a in enumerate((dyn, d2, d3, d4)):
        near_ref[i] = pair(a)
    resid = eye - mul_exact(dynt_ref[...], dyn)
    resid_ref[0] = pair(resid)
    more = mul_exact(resid, lanes(dyn, d2, d3))
    for i in range(3):
        resid_ref[i + 1] = pair(more[:, i * N : (i + 1) * N])
    far_ref[0] = eye
    far_ref[1] = d4
    for have in (1, 2, 4, 8):
        last = far_ref[have]
        for k in range(1, have + 1):
            got = mul_exact(last, far_ref[k])
            if have + k < LEAVES:
                far_ref[have + k] = got
    for i, k in enumerate(REACH):
        reach_ref[i] = pair(far_ref[k])
    cross_ref[0] = pair(eye)
    powers = [None, got]
    for k in range(2, 9):
        powers.append(mul_exact(powers[k // 2], powers[k - k // 2]))
    for k in range(1, 8):
        cross_ref[k] = pair(powers[k])
    w16 = mul_exact(powers[8], powers[8])
    cross_ref[8] = pair(powers[8])
    cross_ref[9] = pair(w16)
    cross_ref[10] = pair(mul_exact(w16, powers[8]))


def k_entry(after_ref, near, near_mate, two, two_mate, mate_ref, entry_ref, entryoff_ref):
    me, second = lax.axis_index("tm_1"), lax.axis_index("tm_2") == 1
    entryoff_ref[...] = jnp.zeros_like(entryoff_ref)
    for b in range(SEQ):
        so_far = (identity(), jnp.zeros((1, N), F32))
        ring = around((near, near_mate, two, two_mate), b)
        mate = mate_ref[b, 0:N, :], mate_ref[b, N : N + 1, :]
        for source, flag in (
            (ring[2], me >= 3), (ring[1], me >= 2), (ring[0], me >= 1), (mate, second),
        ):
            got = then(so_far, source)
            so_far = (pick(flag, got[0], so_far[0]), pick(flag, got[1], so_far[1]))
        entry_ref[b] = so_far[0]
        entryoff_ref[b : b + 1, :] = so_far[1]


def k_tables(
    after_ref, flags, table, nodes, offs, step_ref, u_ref, mask_ref, eye_ref, dyn_ref, dynt_ref,
    pre_ref, preoff_ref, u2_ref, near_ref, far_ref, reach_ref, cross_ref, resid_ref,
):
    k_prefix(flags, table, nodes, offs, step_ref, u_ref, mask_ref, pre_ref, preoff_ref, u2_ref)
    k_powers(eye_ref, dyn_ref, dynt_ref, near_ref, far_ref, reach_ref, cross_ref, resid_ref)


def k_filter(
    one, one_mate, two, two_mate, sent, sent_mate, entry_ref, entryoff_ref, init_ref, obs_ref,
    rows_ref, dynt_ref, pre_ref, preoff_ref, step_ref, twos_ref, u_ref, u2_ref, mask_ref, reach_ref,
    resid_ref, cross_ref, send_ref, local_ref, suffix_ref, final_ref,
):
    group, core = lax.axis_index("tm_0"), lax.axis_index("tm_2")
    direct = ((group == 2) & (core == 0)) | ((group == 3) & (core == 1))
    last = (group == 3) & (lax.axis_index("tm_1") == 3) & (lax.axis_index("tm_2") == 1)
    starts = []
    for b in range(SEQ):
        row = pick(direct, sent[b : b + 1, :], sent_mate[b : b + 1, :])
        row = pick(group >= 2, row, init_ref[b : b + 1, :])
        for flag, mine, mate in ((group == 3, two, two_mate), (group >= 1, one, one_mate)):
            matrix, off = in_order(mine, mate, b)
            row = pick(flag, apply_row(row, matrix) + off, row)
        starts.append(apply_row(row, entry_ref[b]) + entryoff_ref[b : b + 1, :])
    rows = []
    for b in range(SEQ):
        column = jnp.transpose(jnp.broadcast_to(starts[b], (N, N)))
        rows.append(starts[b])
        for j in range(1, LEAVES):
            k = b * LEAVES + j
            rows.append(
                jnp.sum(column * pre_ref[k], axis=0, keepdims=True) + preoff_ref[k : k + 1, :]
            )
    state = stacked(*rows)
    weight = rows_ref[1:2, :]
    step = step_ref[...]
    square = jnp.zeros((ROWS, N), F32)
    seen = jnp.zeros((ROWS, N), F32)
    sums = [None] * SUB
    out_pair = lanes(step[:, 2 * N : 3 * N], step[:, 5 * N : 6 * N])
    for i in range(0, SUB, 2):
        x = pair(state)
        d = mul_pair(x, step)
        q = mul_pair(x, twos_ref[...])
        m1, m2 = mask_ref[i], mask_ref[i + 1]
        on1, on2 = m1 > 0.5, m2 > 0.5
        middle = pick(on1, d[:, N : 2 * N], d[:, :N]) + u_ref[i]
        state = u2_ref[i // 2] + pick(
            on1,
            pick(on2, q[:, 3 * N :], q[:, 2 * N : 3 * N]),
            pick(on2, q[:, N : 2 * N], q[:, :N]),
        )
        x1 = pair(middle)
        e1 = obs_ref[i] - d[:, 2 * N :]
        e2 = obs_ref[i + 1] - mul_pair(x1, out_pair)
        square = square + m1 * (e1 * e1) + m2 * (e2 * e2)
        seen = seen + m1 + m2
        for j, x in ((i, x1), (i + 1, pair(state))):
            for k in range(j + 1):
                add = mul_pair(x, resid_ref[j - k])
                sums[k] = add if k == j else sums[k] + add
    square = jnp.sum(square, axis=0, keepdims=True) * weight
    seen = jnp.sum(seen, axis=0, keepdims=True)
    ends = stacked(*(state[(b + 1) * LEAVES - 1 : (b + 1) * LEAVES, :] for b in range(SEQ)))
    ends = stacked(ends, jnp.zeros((8 - SEQ, N), F32))
    final = mul_pair(pair(ends), pair(dynt_ref[...]))
    final_ref[...] = final
    place = lax.broadcasted_iota(jnp.int32, (ROWS, N), 0) % LEAVES
    run = sums[0]
    for first in (0, 3):
        total = run
        for k in range(first, first + 3):
            moved = pltpu.roll(mul_pair(pair(run), reach_ref[k]), ROWS - REACH[k], 0)
            total = total + pick(place < LEAVES - REACH[k], moved, 0.0)
        run = total
    for i in range(SUB):
        local_ref[i] = sums[i]
    suffix_ref[...] = run
    offsets = stacked(*(run[b * LEAVES : b * LEAVES + 1, :] for b in range(SEQ)))
    offsets = stacked(offsets, jnp.zeros((8 - SEQ, N), F32))
    through = mul_pair(pair(final), cross_ref[1])
    offsets = offsets + pick(last, through, 0.0)
    packed = stacked(offsets[:SEQ], square, seen, jnp.zeros((8 - SEQ - 2, N), F32))
    send_ref[...] = jnp.broadcast_to(packed[None], (BLOCKS, 8, N))


def k_smooth(
    got_ref, local_ref, suffix_ref, final_ref, rows_ref, far_ref, near_ref, cross_ref,
    out_ref, prec_ref, lik_ref,
):
    me = (lax.axis_index("tm_0") * 4 + lax.axis_index("tm_1")) * 2 + lax.axis_index("tm_2")
    on, lp = rows_ref[0:1, :], rows_ref[2:3, :]
    acc = jnp.zeros((4 * 8, N), F32)
    for h in range(8):
        parts = []
        for g in range(4):
            at = me + 1 + 8 * g + h
            parts.append(pick(at < BLOCKS, got_ref[jnp.minimum(at, BLOCKS - 1)], 0.0))
        acc = acc + mul_pair(pair(stacked(*parts)), cross_ref[h])
    leaving = acc[0:8]
    for g in range(1, 4):
        leaving = leaving + mul_pair(pair(acc[8 * g : 8 * g + 8]), cross_ref[7 + g])
    leaving = pick(me == BLOCKS - 1, final_ref[...], leaving)
    rows = []
    for b in range(SEQ):
        column = jnp.transpose(jnp.broadcast_to(leaving[b : b + 1, :], (N, N)))
        for j in range(LEAVES - 1):
            k = b * LEAVES + j
            rows.append(
                jnp.sum(column * far_ref[LEAVES - 1 - j], axis=0, keepdims=True)
                + suffix_ref[k + 1 : k + 2, :]
            )
        rows.append(leaving[b : b + 1, :])
    x = pair(stacked(*rows))
    for i in range(SUB):
        got = mul_pair(x, near_ref[SUB - 1 - i]) + local_ref[i]
        for b in range(SEQ):
            out_ref[b, pl.ds(i, LEAVES, stride=SUB), :] = got[b * LEAVES : (b + 1) * LEAVES]
    both = jnp.sum(got_ref[...], axis=0)
    square, seen = both[SEQ : SEQ + 1], both[SEQ + 1 : SEQ + 2]
    total = float(SEQ * STEPS * BLOCKS)
    prec_ref[...] = lp + (0.5 / total) * on * (seen - square)
    lik = jnp.sum(on * (seen * lp - square), axis=1, keepdims=True) * (0.5 / (total * N))
    lik_ref[...] = jnp.broadcast_to(lik, (1, N))


VM = pl.BlockSpec(memory_space=pltpu.VMEM)
SM = pl.BlockSpec(memory_space=pltpu.SMEM)


def call(kernel, name, specs, shapes, scratch=(), flops=0, moved=0):
    return pl.pallas_call(
        kernel,
        out_shape=shapes,
        in_specs=specs,
        out_specs=jax.tree.map(lambda _: VM, shapes),
        scratch_shapes=list(scratch),
        compiler_params=pltpu.CompilerParams(vmem_limit_bytes=VMEM_LIMIT),
        cost_estimate=pl.CostEstimate(flops=flops, bytes_accessed=moved, transcendentals=0),
        name=name,
    )


def out(shape, dtype=F32):
    return jax.ShapeDtypeStruct(shape, dtype)


def shifted(a, axis, by):
    count = lax.axis_size(axis)
    return lax.ppermute(a, axis, [(i, (i + by) % count) for i in range(count)])


def swapped(a, *done):
    return shifted(lax.optimization_barrier((a, done))[0], "tm_2", 1)


RING = [(2 * i, (2 * i + 2) % 8) for i in range(4)] + [(2 * i + 1, (2 * i + 7) % 8) for i in range(4)]
SKIP = [(2, 6), (3, 7), (6, 2), (7, 3), (0, 1), (1, 0), (4, 5), (5, 4)]
FIRST = [(0, 4), (1, 7), (4, 0), (7, 1), (2, 3), (3, 2), (5, 6), (6, 5)]


def local(obs, present, sensors, log_prec, dynamics, prior_var, obs_map, init_state):
    lp, pv = log_prec.reshape(1, N), prior_var.reshape(1, N)
    both = (out((FULL, N)), out((PART, N)))
    square = out((N, N))
    square = out((N, N))
    eye = call(k_first, "k_first", [], square, (), 4 * 10**9, 10**7)()
    root, dyn_t, table, nodes, offs, step, twos, u, mask, obs_s, rows = call(
        k_block,
        "k_block",
        [SM] * 2 + [VM] * 7,
        (
            out((SEQ, N + 8, N)),
            square,
            out((16, N, 2 * N), BF16),
            out((42, N, 2 * N), BF16),
            out((96, N)),
            out((N, 6 * N), BF16),
            out((N, 8 * N), BF16),
            out((SUB, ROWS, N)),
            out((SUB, ROWS, N)),
            out((SUB, ROWS, N)),
            out((8, N)),
        ),
        [pltpu.VMEM((SEQ, STEPS, N), F32), pltpu.VMEM((SEQ, STEPS, N), F32)],
        10**9,
        10**6,
    )(present, sensors, eye, obs, present, lp, dynamics, pv, obs_map)
    mate = shifted(root, "tm_2", 1)
    chip, mine = call(k_core, "k_core", [VM] * 2, both, (), 10**7, 10**6)(root, mate)
    near = lax.ppermute(chip, ("tm_1", "tm_2"), RING)
    two = shifted(mine, "tm_1", 2)
    pre, preoff, u2, step_near, far, reach, cross, resid = call(
        k_tables,
        "k_tables",
        [VM, SM] + [VM] * 9,
        (
            out((ROWS, N, N)),
            out((ROWS, N)),
            out((SUB // 2, ROWS, N)),
            out((SUB, N, 2 * N), BF16),
            out((LEAVES, N, N)),
            out((len(REACH), N, 2 * N), BF16),
            out((11, N, 2 * N), BF16),
            out((SUB, N, 2 * N), BF16),
        ),
        (),
        4 * 10**9,
        10**7,
    )(chip, present, table, nodes, offs, step, u, mask, eye, dynamics, dyn_t)
    got = near, swapped(near, resid), two, swapped(two, resid)
    mine, state = call(
        k_total,
        "k_total",
        [VM] * 6,
        (out((PART, N)), out((8, N))),
        [pltpu.VMEM((4, SEQ, N, N), F32), pltpu.VMEM((4, SEQ, 8, N), F32)],
        10**8,
        10**6,
    )(chip, *got, init_state)
    one = shifted(mine, "tm_0", 1)
    two = lax.ppermute(mine, ("tm_0", "tm_2"), SKIP)
    sent = lax.ppermute(state, ("tm_0", "tm_2"), FIRST)
    entry, entryoff = call(
        k_entry, "k_entry", [VM] * 6, (out((SEQ, N, N)), out((8, N))), (), 4 * 10**9, 10**7
    )(mine, *got, mate)
    got = (
        one, swapped(one, entryoff, sent), two, swapped(two, entryoff, sent),
        sent, swapped(sent, entryoff),
    )
    send, near_sums, suffix, final = call(
        k_filter,
        "k_filter",
        [VM] * 22,
        (out((BLOCKS, 8, N)), out((SUB, ROWS, N)), out((ROWS, N)), out((8, N))),
        (),
        10**7,
        10**6,
    )(
        *got, entry, entryoff, init_state, obs_s, rows, dyn_t, pre, preoff, step, twos, u, u2,
        mask, reach, resid, cross,
    )
    got = lax.all_to_all(send, TM, 0, 0, tiled=True)
    smoothed, prec, lik = call(
        k_smooth,
        "k_smooth",
        [VM] * 8,
        (out((SEQ, STEPS, N)), out((1, N)), out((1, N))),
        (),
        10**7,
        10**6,
    )(got, near_sums, suffix, final, rows, far, step_near, cross)
    return smoothed, prec.reshape(N), lik[0, :1]


def solution(mesh):
    split = Mesh(
        mesh.devices.reshape(mesh.shape["cluster"], 4, 4, 2), ("cluster", "tm_0", "tm_1", "tm_2")
    )
    return jax.shard_map(
        local,
        mesh=split,
        in_specs=(
            P("cluster", TM, None),
            P("cluster", TM),
            P("cluster"),
            P("cluster"),
            P("cluster", None),
            P("cluster"),
            P("cluster", None),
            P("cluster", None),
        ),
        out_specs=(P("cluster", TM, None), P("cluster"), P("cluster")),
        check_vma=False,
    )
```

```python
import jax
import jax.numpy as jnp
from jax import lax
from jax.experimental import pallas as pl
from jax.experimental.pallas import tpu as pltpu
from jax.sharding import Mesh
from jax.sharding import PartitionSpec as P

F32, BF16 = jnp.float32, jnp.bfloat16
TM = ("tm_0", "tm_1", "tm_2")
N = 128
SEQ, STEPS, SUB = 3, 64, 4
LEAVES = STEPS // SUB
ROWS = SEQ * LEAVES
HALF = N // 2
BLOCKS = 32
VMEM_LIMIT = 40 * 1024 * 1024


def dot(a, b):
    return lax.dot(a, b, preferred_element_type=F32)


def lanes(*parts):
    return jnp.concatenate(parts, axis=1)


def stacked(*parts):
    return jnp.concatenate(parts, axis=0)


def split2(a):
    hi = a.astype(BF16)
    return hi, (a - hi.astype(F32)).astype(BF16)


def split3(a):
    hi = a.astype(BF16)
    rest = a - hi.astype(F32)
    mid = rest.astype(BF16)
    return hi, mid, (rest - mid.astype(F32)).astype(BF16)


def pair(a):
    return lanes(*split2(a))


def whole(x):
    n = x.shape[1] // 2
    return x[:, :n].astype(F32) + x[:, n:].astype(F32)


def mul_pair(x, y):
    d = dot(x, stacked(y, y))
    n = y.shape[1] // 2
    return d[:, :n] + d[:, n:]


def mul_exact(a, b):
    a0, a1, a2 = split3(a)
    b0, b1, b2 = split3(b)
    n = b.shape[1]
    y = lanes(b0, b1)
    d = dot(lanes(a0, a1), stacked(y, y))
    return d[:, :n] + (d[:, n:] + dot(lanes(a0, a2), stacked(b2, b0)))


def apply_row(row, matrix):
    column = jnp.transpose(jnp.broadcast_to(row, (N, N)))
    return jnp.sum(column * matrix, axis=0, keepdims=True)


def step_major(ref, i):
    return stacked(*(ref[b, pl.ds(i, LEAVES, stride=SUB), :] for b in range(SEQ)))


def pick(flag, a, b):
    return jnp.where(flag, a, b)


def on_row(sensors_ref):
    return (lax.broadcasted_iota(jnp.int32, (1, N), 1) < sensors_ref[0]).astype(F32)


def identity(rows=N):
    shape = (rows, N)
    return (
        lax.broadcasted_iota(jnp.int32, shape, 0) == lax.broadcasted_iota(jnp.int32, shape, 1)
    ).astype(F32)


def leaf_number(flags, b, j):
    at = 0
    for i in range(SUB):
        at = at * 2 + flags[b, SUB * j + i]
    return at


def joined(left, left_off, right, right_off):
    off = pair(jnp.broadcast_to(left_off, (16, N)))
    got = mul_pair(stacked(left, off), right)
    return got[:N], got[N : N + 1] + right_off


REACH = (1, 2, 3, 4, 8, 12)
LEVELS = ((0, 24), (24, 12), (36, 6))
OFFS = (0, 48, 72, 84)
PART = SEQ * HALF + 8
FULL = SEQ * N + 8


def k_first(eye_ref):
    eye_ref[...] = identity()


def k_block(
    flags, sensors_ref, eye_ref, obs_raw, pres_ref, lp_ref, dyn_ref, pv_ref, map_ref,
    root_ref, dynt_ref, table, nodes, offs, step_ref, wide_ref, u_ref, mask_ref, rows_ref, mask_scr, u_scr,
):
    on = on_row(sensors_ref)
    weight = jnp.exp(lp_ref[...]) * on
    pv, obs_map = pv_ref[...], map_ref[...]
    dyn_t = jnp.transpose(dyn_ref[...])
    dynt_ref[...] = dyn_t
    y = pair(obs_map)
    out_t = mul_pair(pair(dyn_t), pair(jnp.transpose(obs_map)))
    filt_t = dyn_t - mul_pair(pair(out_t * weight), y) * pv
    rows_ref[...] = stacked(on, weight, lp_ref[...], jnp.zeros((5, N), F32))
    step_ref[...] = pair(lanes(dyn_t, filt_t, out_t))
    seen = pres_ref[...].astype(F32)
    seen = jnp.transpose(stacked(seen, jnp.zeros((8 - SEQ, STEPS), F32)))
    for b in range(SEQ):
        mask = jnp.broadcast_to(seen[:, b : b + 1], (STEPS, N))
        mask_scr[b] = mask
        u_scr[b] = mul_pair(pair(obs_raw[b] * weight), y) * pv * mask
    for i in range(SUB):
        u_ref[i] = step_major(u_scr, i)
        mask_ref[i] = step_major(mask_scr, i)
    two = mul_exact(stacked(dyn_t, filt_t), lanes(dyn_t, filt_t))
    twos = [two[i * N : (i + 1) * N, j * N : (j + 1) * N] for i in (0, 1) for j in (0, 1)]
    wide = lanes(*twos)
    wide_ref[...] = wide
    for i in range(4):
        four = mul_exact(twos[i], wide)
        for j in range(4):
            table[4 * i + j] = pair(four[:, j * N : (j + 1) * N])
    y = pair(lanes(dyn_t, filt_t))
    z = u_ref[0]
    for i in range(1, SUB):
        d = mul_pair(pair(z), y)
        z = pick(mask_ref[i] > 0.5, d[:, N:], d[:, :N]) + u_ref[i]
    offs[0:ROWS, :] = z

    def leaf(k):
        return table[leaf_number(flags, k // LEAVES, k % LEAVES)]

    get = leaf
    for level in range(4):
        count = ROWS >> (level + 1)
        for k in range(count):
            at = OFFS[level] + 2 * k
            matrix, off = joined(
                get(2 * k), offs[at : at + 1, :], get(2 * k + 1), offs[at + 1 : at + 2, :]
            )
            if level == 3:
                root_ref[k, 0:N, :] = matrix
                root_ref[k, N : N + 8, :] = jnp.broadcast_to(off, (8, N))
            else:
                nodes[LEVELS[level][0] + k] = pair(matrix)
                to = OFFS[level + 1] + k
                offs[to : to + 1, :] = off
        if level < 3:
            get = lambda k, level=level: nodes[LEVELS[level][0] + k]


def put(ref, b, matrix):
    rows = matrix.shape[0]
    ref[b * rows : (b + 1) * rows, :] = matrix


def put_offsets(ref, offs):
    rows = ref.shape[0]
    ref[rows - 8 : rows, :] = stacked(*offs, jnp.zeros((8 - SEQ, N), F32))


def offset_of(ref, b):
    at = ref.shape[0] - 8 + b
    return ref[at : at + 1, :]


def half_of(ref, b):
    return ref[b * HALF : (b + 1) * HALF, :]


def full_of(ref, b):
    return ref[b * N : (b + 1) * N, :]


def in_order(mine_ref, mate_ref, b):
    first = lax.axis_index("tm_2") == 0
    mine, mate = half_of(mine_ref, b), half_of(mate_ref, b)
    matrix = stacked(pick(first, mine, mate), pick(first, mate, mine))
    return matrix, offset_of(mine_ref, b)


def chosen(flag, p_ref, q_ref, b):
    return (
        pick(flag, full_of(p_ref, b), full_of(q_ref, b)),
        pick(flag, offset_of(p_ref, b), offset_of(q_ref, b)),
    )


def then(p, q):
    return joined(pair(p[0]), p[1], pair(q[0]), q[1])


def put_all(ref, maps):
    for b, (matrix, _) in enumerate(maps):
        put(ref, b, matrix)
    put_offsets(ref, [off for _, off in maps])


def put_halves(ref, maps):
    first = lax.axis_index("tm_2") == 0
    put_all(ref, [(pick(first, m[:HALF], m[HALF:]), off) for m, off in maps])


def k_core(own_ref, mate_ref, out_ref, mine_ref):
    first = lax.axis_index("tm_2") == 0
    maps = []
    for b in range(SEQ):
        own, mate = own_ref[b], mate_ref[b]
        p, q = pick(first, own, mate), pick(first, mate, own)
        maps.append(then((p[:N], p[N : N + 1]), (q[:N], q[N : N + 1])))
    put_all(out_ref, maps)
    put_halves(mine_ref, maps)


def k_total(
    own_ref, near, near_mate, two, two_mate, init_ref, mine_ref, state_ref, ahead_ref, maps, offs
):
    me, first = lax.axis_index("tm_1"), lax.axis_index("tm_2") == 0
    state_ref[...] = jnp.zeros_like(state_ref)
    for b in range(SEQ):
        ring = (
            chosen(first, near, near_mate, b),
            in_order(two, two_mate, b),
            chosen(first, near_mate, near, b),
        )
        for d, (matrix, off) in enumerate(ring):
            slot = lax.rem(me + 3 - d, 4)
            off = jnp.broadcast_to(off, (8, N))
            maps[slot, b] = matrix
            offs[slot, b] = off
            ahead_ref[d, b, 0:N, :] = matrix
            ahead_ref[d, b, N : N + 8, :] = off
        maps[me, b] = full_of(own_ref, b)
        offs[me, b] = jnp.broadcast_to(offset_of(own_ref, b), (8, N))
    ends = []
    for b in range(SEQ):
        p = [(maps[k, b], offs[k, b, 0:1, :]) for k in range(4)]
        ends.append(then(then(p[0], p[1]), then(p[2], p[3])))
        state_ref[b : b + 1, :] = apply_row(init_ref[b : b + 1, :], ends[b][0]) + ends[b][1]
    put_halves(mine_ref, ends)


def k_prefix(flags, table, nodes, offs, step_ref, u_ref, mask_ref, pre_ref, preoff_ref, u2_ref):
    y = lanes(step_ref[:, 0 : 2 * N], step_ref[:, 3 * N : 5 * N])
    for i in range(SUB // 2):
        d = mul_pair(pair(u_ref[2 * i]), y)
        u2_ref[i] = pick(mask_ref[2 * i + 1] > 0.5, d[:, N:], d[:, :N]) + u_ref[2 * i + 1]
    preoff_ref[...] = jnp.zeros_like(preoff_ref)
    for b in range(SEQ):
        pre_ref[b * LEAVES] = jnp.zeros((N, N), F32)
        for level in (3, 2, 1, 0):
            parents = 8 >> level
            span = LEAVES // parents
            for k in range(parents):
                at = b * LEAVES + k * span
                left = b * 2 * parents + 2 * k
                off = offs[OFFS[level] + left : OFFS[level] + left + 1, :]
                if level == 0:
                    got = table[leaf_number(flags, left // LEAVES, left % LEAVES)]
                else:
                    got = nodes[LEVELS[level - 1][0] + left]
                if k == 0:
                    matrix = whole(got)
                else:
                    matrix, off = joined(
                        pair(pre_ref[at]), preoff_ref[at : at + 1, :], got, off
                    )
                to = at + span // 2
                pre_ref[to] = matrix
                preoff_ref[to : to + 1, :] = off


def k_powers(
    eye_ref, dyn_ref, dynt_ref, near_ref, far_ref, reach_ref, cross_ref, resid_ref
):
    eye, dyn = eye_ref[...], dyn_ref[...]
    d2 = mul_exact(dyn, dyn)
    d34 = mul_exact(d2, lanes(dyn, d2))
    d3, d4 = d34[:, :N], d34[:, N:]
    for i, a in enumerate((dyn, d2, d3, d4)):
        near_ref[i] = pair(a)
    resid = eye - mul_exact(dynt_ref[...], dyn)
    resid_ref[0] = pair(resid)
    more = mul_exact(resid, lanes(dyn, d2, d3))
    for i in range(3):
        resid_ref[i + 1] = pair(more[:, i * N : (i + 1) * N])
    far_ref[0] = eye
    far_ref[1] = d4
    for have in (1, 2, 4, 8):
        last = far_ref[have]
        for k in range(1, have + 1):
            got = mul_exact(last, far_ref[k])
            if have + k < LEAVES:
                far_ref[have + k] = got
    for i, k in enumerate(REACH):
        reach_ref[i] = pair(far_ref[k])
    cross_ref[0] = pair(eye)
    powers = [None, got]
    for k in range(2, 9):
        powers.append(mul_exact(powers[k // 2], powers[k - k // 2]))
    for k in range(1, 8):
        cross_ref[k] = pair(powers[k])
    w16 = mul_exact(powers[8], powers[8])
    cross_ref[8] = pair(powers[8])
    cross_ref[9] = pair(w16)
    cross_ref[10] = pair(mul_exact(w16, powers[8]))


def k_entry(after_ref, ahead_ref, mate_ref, entry_ref, entryoff_ref):
    me, second = lax.axis_index("tm_1"), lax.axis_index("tm_2") == 1
    entryoff_ref[...] = jnp.zeros_like(entryoff_ref)
    for b in range(SEQ):
        so_far = (identity(), jnp.zeros((1, N), F32))
        for source, flag in (
            (ahead_ref.at[2], me >= 3), (ahead_ref.at[1], me >= 2), (ahead_ref.at[0], me >= 1),
            (mate_ref, second),
        ):
            got = then(so_far, (source[b, 0:N, :], source[b, N : N + 1, :]))
            so_far = (pick(flag, got[0], so_far[0]), pick(flag, got[1], so_far[1]))
        entry_ref[b] = so_far[0]
        entryoff_ref[b : b + 1, :] = so_far[1]


def k_tables(
    after_ref, flags, table, nodes, offs, step_ref, u_ref, mask_ref, eye_ref, dyn_ref, dynt_ref,
    obs_raw, wide_ref, obs_ref, twos_ref, pre_ref, preoff_ref, u2_ref, near_ref, far_ref, reach_ref, cross_ref, resid_ref,
):
    twos_ref[...] = pair(wide_ref[...])
    for i in range(SUB):
        obs_ref[i] = step_major(obs_raw, i)
    k_prefix(flags, table, nodes, offs, step_ref, u_ref, mask_ref, pre_ref, preoff_ref, u2_ref)
    k_powers(eye_ref, dyn_ref, dynt_ref, near_ref, far_ref, reach_ref, cross_ref, resid_ref)


def k_filter(
    one, one_mate, two, two_mate, sent, sent_mate, entry_ref, entryoff_ref, init_ref, obs_ref,
    rows_ref, dynt_ref, pre_ref, preoff_ref, step_ref, twos_ref, u_ref, u2_ref, mask_ref, reach_ref,
    resid_ref, cross_ref, send_ref, local_ref, suffix_ref, final_ref,
):
    group, core = lax.axis_index("tm_0"), lax.axis_index("tm_2")
    direct = ((group == 2) & (core == 0)) | ((group == 3) & (core == 1))
    last = (group == 3) & (lax.axis_index("tm_1") == 3) & (lax.axis_index("tm_2") == 1)
    starts = []
    for b in range(SEQ):
        row = pick(direct, sent[b : b + 1, :], sent_mate[b : b + 1, :])
        row = pick(group >= 2, row, init_ref[b : b + 1, :])
        for flag, mine, mate in ((group == 3, two, two_mate), (group >= 1, one, one_mate)):
            matrix, off = in_order(mine, mate, b)
            row = pick(flag, apply_row(row, matrix) + off, row)
        starts.append(apply_row(row, entry_ref[b]) + entryoff_ref[b : b + 1, :])
    rows = []
    for b in range(SEQ):
        column = jnp.transpose(jnp.broadcast_to(starts[b], (N, N)))
        rows.append(starts[b])
        for j in range(1, LEAVES):
            k = b * LEAVES + j
            rows.append(
                jnp.sum(column * pre_ref[k], axis=0, keepdims=True) + preoff_ref[k : k + 1, :]
            )
    state = stacked(*rows)
    weight = rows_ref[1:2, :]
    step = step_ref[...]
    square = jnp.zeros((ROWS, N), F32)
    seen = jnp.zeros((ROWS, N), F32)
    sums = [None] * SUB
    out_pair = lanes(step[:, 2 * N : 3 * N], step[:, 5 * N : 6 * N])
    for i in range(0, SUB, 2):
        x = pair(state)
        d = mul_pair(x, step)
        q = mul_pair(x, twos_ref[...])
        m1, m2 = mask_ref[i], mask_ref[i + 1]
        on1, on2 = m1 > 0.5, m2 > 0.5
        middle = pick(on1, d[:, N : 2 * N], d[:, :N]) + u_ref[i]
        state = u2_ref[i // 2] + pick(
            on1,
            pick(on2, q[:, 3 * N :], q[:, 2 * N : 3 * N]),
            pick(on2, q[:, N : 2 * N], q[:, :N]),
        )
        x1 = pair(middle)
        e1 = obs_ref[i] - d[:, 2 * N :]
        e2 = obs_ref[i + 1] - mul_pair(x1, out_pair)
        square = square + m1 * (e1 * e1) + m2 * (e2 * e2)
        seen = seen + m1 + m2
        for j, x in ((i, x1), (i + 1, pair(state))):
            for k in range(j + 1):
                add = mul_pair(x, resid_ref[j - k])
                sums[k] = add if k == j else sums[k] + add
    square = jnp.sum(square, axis=0, keepdims=True) * weight
    seen = jnp.sum(seen, axis=0, keepdims=True)
    ends = stacked(*(state[(b + 1) * LEAVES - 1 : (b + 1) * LEAVES, :] for b in range(SEQ)))
    ends = stacked(ends, jnp.zeros((8 - SEQ, N), F32))
    final = mul_pair(pair(ends), pair(dynt_ref[...]))
    final_ref[...] = final
    place = lax.broadcasted_iota(jnp.int32, (ROWS, N), 0) % LEAVES
    run = sums[0]
    for first in (0, 3):
        total = run
        for k in range(first, first + 3):
            moved = pltpu.roll(mul_pair(pair(run), reach_ref[k]), ROWS - REACH[k], 0)
            total = total + pick(place < LEAVES - REACH[k], moved, 0.0)
        run = total
    for i in range(SUB):
        local_ref[i] = sums[i]
    suffix_ref[...] = run
    offsets = stacked(*(run[b * LEAVES : b * LEAVES + 1, :] for b in range(SEQ)))
    offsets = stacked(offsets, jnp.zeros((8 - SEQ, N), F32))
    through = mul_pair(pair(final), cross_ref[1])
    offsets = offsets + pick(last, through, 0.0)
    packed = stacked(offsets[:SEQ], square, seen, jnp.zeros((8 - SEQ - 2, N), F32))
    send_ref[...] = jnp.broadcast_to(packed[None], (BLOCKS, 8, N))


def k_smooth(
    got_ref, local_ref, suffix_ref, final_ref, rows_ref, far_ref, near_ref, cross_ref,
    out_ref, prec_ref, lik_ref,
):
    me = (lax.axis_index("tm_0") * 4 + lax.axis_index("tm_1")) * 2 + lax.axis_index("tm_2")
    on, lp = rows_ref[0:1, :], rows_ref[2:3, :]
    acc = jnp.zeros((4 * 8, N), F32)
    for h in range(8):
        parts = []
        for g in range(4):
            at = me + 1 + 8 * g + h
            parts.append(pick(at < BLOCKS, got_ref[jnp.minimum(at, BLOCKS - 1)], 0.0))
        acc = acc + mul_pair(pair(stacked(*parts)), cross_ref[h])
    leaving = acc[0:8]
    for g in range(1, 4):
        leaving = leaving + mul_pair(pair(acc[8 * g : 8 * g + 8]), cross_ref[7 + g])
    leaving = pick(me == BLOCKS - 1, final_ref[...], leaving)
    rows = []
    for b in range(SEQ):
        column = jnp.transpose(jnp.broadcast_to(leaving[b : b + 1, :], (N, N)))
        for j in range(LEAVES - 1):
            k = b * LEAVES + j
            rows.append(
                jnp.sum(column * far_ref[LEAVES - 1 - j], axis=0, keepdims=True)
                + suffix_ref[k + 1 : k + 2, :]
            )
        rows.append(leaving[b : b + 1, :])
    x = pair(stacked(*rows))
    for i in range(SUB):
        got = mul_pair(x, near_ref[SUB - 1 - i]) + local_ref[i]
        for b in range(SEQ):
            out_ref[b, pl.ds(i, LEAVES, stride=SUB), :] = got[b * LEAVES : (b + 1) * LEAVES]
    both = jnp.sum(got_ref[...], axis=0)
    square, seen = both[SEQ : SEQ + 1], both[SEQ + 1 : SEQ + 2]
    total = float(SEQ * STEPS * BLOCKS)
    prec_ref[...] = lp + (0.5 / total) * on * (seen - square)
    lik = jnp.sum(on * (seen * lp - square), axis=1, keepdims=True) * (0.5 / (total * N))
    lik_ref[...] = jnp.broadcast_to(lik, (1, N))


VM = pl.BlockSpec(memory_space=pltpu.VMEM)
SM = pl.BlockSpec(memory_space=pltpu.SMEM)


def call(kernel, name, specs, shapes, scratch=(), flops=0, moved=0):
    return pl.pallas_call(
        kernel,
        out_shape=shapes,
        in_specs=specs,
        out_specs=jax.tree.map(lambda _: VM, shapes),
        scratch_shapes=list(scratch),
        compiler_params=pltpu.CompilerParams(vmem_limit_bytes=VMEM_LIMIT),
        cost_estimate=pl.CostEstimate(flops=flops, bytes_accessed=moved, transcendentals=0),
        name=name,
    )


def out(shape, dtype=F32):
    return jax.ShapeDtypeStruct(shape, dtype)


def shifted(a, axis, by):
    count = lax.axis_size(axis)
    return lax.ppermute(a, axis, [(i, (i + by) % count) for i in range(count)])


def swapped(a, *done):
    return shifted(lax.optimization_barrier((a, done))[0], "tm_2", 1)


RING = [(2 * i, (2 * i + 2) % 8) for i in range(4)] + [(2 * i + 1, (2 * i + 7) % 8) for i in range(4)]
SKIP = [(2, 6), (3, 7), (6, 2), (7, 3), (0, 1), (1, 0), (4, 5), (5, 4)]
FIRST = [(0, 4), (1, 7), (4, 0), (7, 1), (2, 3), (3, 2), (5, 6), (6, 5)]


def local(obs, present, sensors, log_prec, dynamics, prior_var, obs_map, init_state):
    lp, pv = log_prec.reshape(1, N), prior_var.reshape(1, N)
    both = (out((FULL, N)), out((PART, N)))
    square = out((N, N))
    square = out((N, N))
    eye = call(k_first, "k_first", [], square, (), 4 * 10**9, 10**7)()
    root, dyn_t, table, nodes, offs, step, wide, u, mask, rows = call(
        k_block,
        "k_block",
        [SM] * 2 + [VM] * 7,
        (
            out((SEQ, N + 8, N)),
            square,
            out((16, N, 2 * N), BF16),
            out((42, N, 2 * N), BF16),
            out((96, N)),
            out((N, 6 * N), BF16),
            out((N, 4 * N)),
            out((SUB, ROWS, N)),
            out((SUB, ROWS, N)),
            out((8, N)),
        ),
        [pltpu.VMEM((SEQ, STEPS, N), F32), pltpu.VMEM((SEQ, STEPS, N), F32)],
        10**9,
        10**6,
    )(present, sensors, eye, obs, present, lp, dynamics, pv, obs_map)
    mate = shifted(root, "tm_2", 1)
    chip, mine = call(k_core, "k_core", [VM] * 2, both, (), 10**7, 10**6)(root, mate)
    near = lax.ppermute(chip, ("tm_1", "tm_2"), RING)
    two = shifted(mine, "tm_1", 2)
    obs_s, twos, pre, preoff, u2, step_near, far, reach, cross, resid = call(
        k_tables,
        "k_tables",
        [VM, SM] + [VM] * 11,
        (
            out((SUB, ROWS, N)),
            out((N, 8 * N), BF16),
            out((ROWS, N, N)),
            out((ROWS, N)),
            out((SUB // 2, ROWS, N)),
            out((SUB, N, 2 * N), BF16),
            out((LEAVES, N, N)),
            out((len(REACH), N, 2 * N), BF16),
            out((11, N, 2 * N), BF16),
            out((SUB, N, 2 * N), BF16),
        ),
        (),
        4 * 10**9,
        10**7,
    )(chip, present, table, nodes, offs, step, u, mask, eye, dynamics, dyn_t, obs, wide)
    got = near, swapped(near, resid), two, swapped(two, resid)
    mine, state, ahead = call(
        k_total,
        "k_total",
        [VM] * 6,
        (out((PART, N)), out((8, N)), out((3, SEQ, N + 8, N))),
        [pltpu.VMEM((4, SEQ, N, N), F32), pltpu.VMEM((4, SEQ, 8, N), F32)],
        10**8,
        10**6,
    )(chip, *got, init_state)
    one = shifted(mine, "tm_0", 1)
    two = lax.ppermute(mine, ("tm_0", "tm_2"), SKIP)
    sent = lax.ppermute(state, ("tm_0", "tm_2"), FIRST)
    entry, entryoff = call(
        k_entry, "k_entry", [VM] * 3, (out((SEQ, N, N)), out((8, N))), (), 4 * 10**9, 10**7
    )(mine, ahead, mate)
    got = (
        one, swapped(one, entryoff, sent), two, swapped(two, entryoff, sent),
        sent, swapped(sent, entryoff),
    )
    send, near_sums, suffix, final = call(
        k_filter,
        "k_filter",
        [VM] * 22,
        (out((BLOCKS, 8, N)), out((SUB, ROWS, N)), out((ROWS, N)), out((8, N))),
        (),
        10**7,
        10**6,
    )(
        *got, entry, entryoff, init_state, obs_s, rows, dyn_t, pre, preoff, step, twos, u, u2,
        mask, reach, resid, cross,
    )
    got = lax.all_to_all(send, TM, 0, 0, tiled=True)
    smoothed, prec, lik = call(
        k_smooth,
        "k_smooth",
        [VM] * 8,
        (out((SEQ, STEPS, N)), out((1, N)), out((1, N))),
        (),
        10**7,
        10**6,
    )(got, near_sums, suffix, final, rows, far, step_near, cross)
    return smoothed, prec.reshape(N), lik[0, :1]


def solution(mesh):
    split = Mesh(
        mesh.devices.reshape(mesh.shape["cluster"], 4, 4, 2), ("cluster", "tm_0", "tm_1", "tm_2")
    )
    return jax.shard_map(
        local,
        mesh=split,
        in_specs=(
            P("cluster", TM, None),
            P("cluster", TM),
            P("cluster"),
            P("cluster"),
            P("cluster", None),
            P("cluster"),
            P("cluster", None),
            P("cluster", None),
        ),
        out_specs=(P("cluster", TM, None), P("cluster"), P("cluster")),
        check_vma=False,
    )
```
